128 devices in a mesh: lon: 8 (over z_lo, x), lat: 16 (over z_hi, y, core).
Axes of the slice: x: 4, y: 4, z: 4 (z_hi: 2, z_lo: 2; z = z_hi * 2 + z_lo), core: 2. Of those that a mesh axis runs over, the one named last changes fastest.
Arguments:
- source_field: float32 [4, 768, 4096], P(None, 'lat', 'lon'), may hold values from -6 to 6
- helm_diag: float32 [4, 768, 4096], P(None, 'lat', 'lon'), may hold values from 0.05 to 1
- vertical: float32 [4], replicated, may hold values from 0.25 to 2
- cubic_band: float32 [8, 4], replicated, may hold values from 0.1 to 0.5
- lat_offset: int32 [768], P('lat'), may hold values from -8 to 8, as said below
- zonal_shift: int32 [768], P('lat'), may hold values from -16 to 15
- row_class: int32 [768], P('lat'), may hold values from 0 to 7
Outputs:
- departure: float32 [4, 768, 4096], P(None, 'lat', 'lon')
- solution: float32 [4, 768, 4096], P(None, 'lat', 'lon')
The draws below stay inside these ranges and needn't reach their ends.
Inputs may be any that keep to these rules, and one draw needn't show every extreme that they name: j + lat_offset[j] lies within 0 to 767 for every row j.
All inputs are finite; a program needn't handle non-finite values.
Results may differ from the reference program's by a relative error of at most 0.0001.
Values sent between devices are 32-bit elements; how exact they have to be, the bound alone decides.
A program may use at most 192 MiB of HBM per device.

```python
import math
import jax
import jax.numpy as jnp
from jax import lax

LEVELS = 4
LAT_DEV = 48
DRIFT = 8
CLASSES = 8
ITERS = 8
NLAT = 768
NLON = 4096
NBLOCKS = 32


def draw_lat_offset(key, part):
    key = jax.random.fold_in(key, 11)
    latitudes = jnp.arange(NLAT, dtype=jnp.int32)
    distance = jnp.abs(2 * latitudes - (NLAT - 1))
    reach = 1 + (DRIFT - 1) * distance * distance // ((NLAT - 1) * (NLAT - 1))
    offset = jax.random.randint(key, (NLAT,), -reach, reach + 1, dtype=jnp.int32)
    position = latitudes % LAT_DEV
    offset = jnp.where(position == 0, -DRIFT, offset)
    offset = jnp.where(position == LAT_DEV - 1, DRIFT, offset)
    offset = jnp.clip(latitudes + offset, 0, NLAT - 1) - latitudes
    offset = offset.at[NLAT // 4].set(DRIFT)
    offset = offset.at[3 * NLAT // 4].set(-DRIFT)
    return offset.astype(jnp.int32)


def draw_zonal_shift(key, part):
    key = jax.random.fold_in(key, 23)
    latitudes = jnp.arange(NLAT, dtype=jnp.int32)
    distance = jnp.abs(2 * latitudes - (NLAT - 1))
    halfway = NLON // 256
    reach = 1 + (halfway - 1) * distance * distance // ((NLAT - 1) * (NLAT - 1))
    shifts = jax.random.randint(key, (NLAT,), -reach, reach + 1, dtype=jnp.int32)
    shifts = jnp.clip(shifts, -halfway, halfway - 1)
    shifts = shifts.at[0].set(-halfway)
    shifts = shifts.at[NLAT - 1].set(halfway - 1)
    return shifts.astype(jnp.int32)


def touch_ends(result, own_key, low, top_value):
    longest = result.shape.index(max(result.shape))
    spots = []
    for shift in (0, 1):
        where = [jax.random.randint(jax.random.fold_in(own_key, axis), (), 0, length) for axis, length in enumerate(result.shape)]
        where[longest] = (where[longest] + shift) % result.shape[longest]
        spots.append(tuple(where))
    return result.at[spots[0]].set(low).at[spots[1]].set(top_value)


def block_scale(key, extent, shards, least, largest):
    gain = 1.0
    for dim, blocks in shards:
        draws = jax.random.uniform(jax.random.fold_in(jax.random.fold_in(key, 6), dim), (blocks,), jnp.float32, least / len(shards), largest / len(shards))
        gain = gain * jnp.repeat(jnp.exp(draws), extent[dim] // blocks).reshape((-1,) + (1,) * (len(extent) - 1 - dim))
    return gain


def scatter_about(rng, shape, width, bound, cuts=(), kind=jnp.bfloat16):
    gain = block_scale(rng, shape, cuts, -0.22, 0.18) if cuts else 1.0
    entries = jax.random.normal(rng, shape, jnp.float32) * width * gain
    return jnp.minimum(jnp.maximum(entries, -bound), bound).astype(kind)


def setup_inputs(seed: int = 0) -> dict:
    streams_of = jax.random.split(jax.random.key(seed), 8)
    return {
        "source_field": scatter_about(streams_of[0], (LEVELS, NLAT, NLON), 1.0, 6.0, ((1, 16), (2, 8)), jnp.float32),
        "helm_diag": jnp.clip(0.05 + 0.95 * jax.random.uniform(streams_of[1], (LEVELS, NLAT, NLON), jnp.float32) ** block_scale(streams_of[1], (LEVELS, NLAT, NLON), ((1, 16), (2, 8)), -0.2, 0.2), 0.05, 1.0),
        "vertical": jnp.clip(jnp.exp(jax.random.uniform(streams_of[2], (LEVELS,), jnp.float32, math.log(0.25), math.log(2.0))), 0.25, 2.0),
        "cubic_band": jnp.clip(jax.random.uniform(streams_of[3], (CLASSES, 4), jnp.float32, 0.1, 0.5), 0.1, 0.5),
        "lat_offset": draw_lat_offset(jax.random.fold_in(streams_of[7], 71), 0),
        "zonal_shift": draw_zonal_shift(jax.random.fold_in(streams_of[7], 71), 0),
        "row_class": touch_ends(jax.random.randint(streams_of[6], (NLAT,), 0, CLASSES), jax.random.fold_in(streams_of[6], 1), 0, CLASSES - 1).astype(jnp.int32),
    }


def band_row(row_cells, begin_at, weights, length):
    window = lax.dynamic_slice_in_dim(row_cells, begin_at, length + 3, 1)
    summed = weights[0] * window[:, 0:length]
    summed = summed + weights[1] * window[:, 1:length + 1]
    summed = summed + weights[2] * window[:, 2:length + 2]
    summed = summed + weights[3] * window[:, 3:length + 3]
    return summed


def operate(values, helm_diag, vertical):
    east_west = jnp.roll(values, -1, 2) + jnp.roll(values, 1, 2)
    padded = jnp.pad(values, ((0, 0), (1, 1), (0, 0)))
    north_south = padded[:, 2:, :] + padded[:, :-2, :]
    stacked = jnp.pad(values, ((1, 1), (0, 0), (0, 0)))
    up_down = stacked[2:] + stacked[:-2]
    coupling = vertical[:, None, None]
    return (4.0 + 2.0 * coupling + helm_diag) * values - (east_west + north_south) - coupling * up_down


def reference(source_field, helm_diag, vertical, cubic_band, lat_offset, zonal_shift, row_class):
    latitudes = jnp.arange(NLAT, dtype=jnp.int32)
    source_rows = (latitudes + lat_offset).astype(jnp.int32)
    blocks = jnp.mod(zonal_shift, NBLOCKS).astype(jnp.int32)
    begins = jnp.mod(NLON - (128 * blocks + 1), NLON).astype(jnp.int32)
    weights = cubic_band[row_class]

    def one_row(packed):
        source_row, begin_at, row_weights = packed
        row_data = lax.dynamic_index_in_dim(source_field, source_row, 1, keepdims=False)
        wrapped = jnp.concatenate([row_data, row_data, row_data[:, :128]], 1)
        return band_row(wrapped, begin_at, row_weights, NLON)

    shifted = lax.map(one_row, (source_rows, begins, weights))
    departure = jnp.transpose(shifted, (1, 0, 2))
    solution = jnp.zeros_like(departure)
    residual = departure
    direction = departure
    norm_now = jnp.sum(residual * residual)
    for iteration in range(ITERS):
        applied = operate(direction, helm_diag, vertical)
        step_size = norm_now / jnp.sum(direction * applied)
        solution = solution + step_size * direction
        if iteration + 1 < ITERS:
            residual = residual - step_size * applied
            norm_next = jnp.sum(residual * residual)
            direction = residual + (norm_next / norm_now) * direction
            norm_now = norm_next
    return departure, solution
```

```python
from functools import partial

import jax
import jax.numpy as jnp
from jax import lax
from jax.experimental import pallas as pl
from jax.experimental.pallas import tpu as pltpu
from jax.sharding import PartitionSpec as P

DRIFT = 8
ITERS = 8


def with_halo(cells, sides, width, closed):
    for axis, dim in sides:
        count = lax.axis_size(axis)
        ends = count if closed else count - 1
        head = lax.slice_in_dim(cells, 0, width, axis=dim)
        tail = lax.slice_in_dim(cells, cells.shape[dim] - width, cells.shape[dim], axis=dim)
        cells = jnp.concatenate(
            [
                lax.ppermute(tail, axis, [(i, (i + 1) % count) for i in range(ends)]),
                cells,
                lax.ppermute(head, axis, [((i + 1) % count, i) for i in range(ends)]),
            ],
            axis=dim,
        )
    return cells


def shifted(x, axis, by):
    peers = lax.axis_size(axis)
    return lax.ppermute(x, axis, [(i, (i + by) % peers) for i in range(peers)])


def band_row(row_cells, begin_at, weights, length):
    window = lax.dynamic_slice_in_dim(row_cells, begin_at, length + 3, 1)
    summed = weights[0] * window[:, 0:length]
    summed = summed + weights[1] * window[:, 1 : length + 1]
    summed = summed + weights[2] * window[:, 2 : length + 2]
    summed = summed + weights[3] * window[:, 3 : length + 3]
    return summed


def finish(framed, remain, row_table, lon_cells):
    begins = lon_cells - 128 * remain - 1
    banded = jax.vmap(partial(band_row, length=lon_cells), in_axes=(1, 0, 0), out_axes=1)
    return banded(framed, begins, row_table)


def local_terms(values, helm_diag, vertical, east_west, north_south):
    stacked = jnp.pad(values, ((1, 1), (0, 0), (0, 0)))
    up_down = stacked[2:] + stacked[:-2]
    coupling = vertical[:, None, None]
    return (
        (4.0 + 2.0 * coupling + helm_diag) * values - (east_west + north_south) - coupling * up_down
    )


def operate(values, helm_diag, vertical):
    zonal = with_halo(values, (("lon", 2),), 1, True)
    meridional = with_halo(values, (("lat", 1),), 1, False)
    east_west = zonal[:, :, 2:] + zonal[:, :, :-2]
    north_south = meridional[:, 2:, :] + meridional[:, :-2, :]
    return local_terms(values, helm_diag, vertical, east_west, north_south)


def squares(residual):
    return lax.psum(jnp.sum(residual * residual), ("lon", "lat"))


MESH = pl.DeviceIdType.MESH
F32 = jnp.float32
STEPS = 4
LOW, REST = 0.05, 9.0
LIMIT = 1.5e4
ROWS, COLS = 48, 512
XR, XC = 56, 640


def iota(shape, dim):
    return lax.broadcasted_iota(jnp.int32, shape, dim)


class Remote:
    def __init__(self, send_sems, recv_sems):
        self.send_sems, self.recv_sems, self.used, self.all = send_sems, recv_sems, 0, []

    def start(self, src, dst, lon, lat):
        copy = pltpu.make_async_remote_copy(
            src_ref=src,
            dst_ref=dst,
            send_sem=self.send_sems.at[self.used],
            recv_sem=self.recv_sems.at[self.used],
            device_id=(lon, lat),
            device_id_type=MESH,
        )
        self.used += 1
        copy.start()
        self.all.append(copy)
        return copy

    def drain(self):
        for copy in self.all:
            copy.wait_send()


def coefficients(gram, steps, middle, half, final):
    shared = gram.shared
    base = 0 if shared else steps + 1

    def apply(vec):
        out = {}

        def add(i, x):
            out[i] = out[i] + x if i in out else x

        for i, x in vec.items():
            start = 0 if i <= steps else steps + 1
            add(i, x * middle)
            if i == start:
                add(i + 1, x * half)
            else:
                add(i + 1, x * (0.5 * half))
                add(i - 1, x * (0.5 * half))
        return out

    def form(a, b):
        total = size = None
        for i, x in a.items():
            inner = bulk = None
            for j, y in b.items():
                term = gram(i, j) * y
                inner = term if inner is None else inner + term
                bulk = jnp.abs(term) if bulk is None else bulk + jnp.abs(term)
            total = x * inner if total is None else total + x * inner
            size = jnp.abs(x) * bulk if size is None else size + jnp.abs(x) * bulk
        return total, size / jnp.abs(total)

    def plus(a, scale, b):
        return {i: a[i] + scale * b[i] if i in a and i in b else (a[i] if i in a else scale * b[i]) for i in {**a, **b}}

    one = jnp.ones((8, 128), F32)
    direction, residual, answer = {0: one}, {base: one}, {}
    norm, worst = gram(base, base), one
    for count in range(steps):
        applied = apply(direction)
        slope, size = form(direction, applied)
        worst = jnp.maximum(worst, size)
        rate = norm / slope
        answer = plus(answer, rate, direction)
        if not (final and count == steps - 1):
            residual = plus(residual, -rate, applied)
            follow, size = form(residual, residual)
            worst = jnp.maximum(worst, size)
            direction = plus(residual, follow / norm, direction)
            norm = follow
    return answer, direction, residual, worst


class Gram:
    def __init__(self, row, pairs, shared):
        self.row, self.place, self.shared, self.cache = row, {p: i for i, p in enumerate(pairs)}, shared, {}

    def __call__(self, i, j):
        pair = (min(i, j), max(i, j))
        if pair not in self.cache:
            at = self.place[pair]
            self.cache[pair] = jnp.broadcast_to(self.row[:, at : at + 1], (8, 128))
        return self.cache[pair]


def solve_kernel(
    nlon, nlat, vertical, dep, helm, out, flag,
    vs, dd, lat_in, lon_in, packs, stage, slot_lon, slot_lat, local_sems, send_sems, recv_sems,
):
    lon, lat = lax.axis_index("lon"), lax.axis_index("lat")

    def east(k):
        return lax.rem(lon + (k + nlon), nlon)

    def north(k):
        return lax.rem(lat + (k + nlat), nlat)

    own = [
        pltpu.make_async_copy(helm, dd.at[:, pl.ds(0, ROWS), pl.ds(0, COLS)], local_sems.at[0]),
        pltpu.make_async_copy(dep, vs.at[0, pl.ds(1, 4), pl.ds(0, ROWS), pl.ds(0, COLS)], local_sems.at[1]),
    ]
    for copy in own:
        copy.start()
    barrier = pltpu.get_barrier_semaphore()
    greeted = 0
    for k in range(1, nlon):
        pl.semaphore_signal(barrier, inc=1, device_id=(east(k), lat), device_id_type=MESH)
        greeted += 1
    for k in range(1, nlat):
        pl.semaphore_signal(barrier, inc=1, device_id=(lon, north(k)), device_id_type=MESH)
        greeted += 1
    for a in (-1, 1):
        for b in (-1, 1):
            pl.semaphore_signal(barrier, inc=1, device_id=(east(a), north(b)), device_id_type=MESH)
            greeted += 1

    remote = Remote(send_sems, recv_sems)
    lane, sub = iota((8, 128), 1), iota((8, 128), 0)
    top_ok, bottom_ok = lat > 0, lat < nlat - 1

    zero = jnp.zeros((XR, XC), F32)
    for j in range(2 * STEPS + 1):
        vs[j, 0] = zero
        vs[j, 5] = zero
    stage[...] = jnp.zeros_like(stage)

    biggest = jnp.maximum(jnp.maximum(vertical[0], vertical[1]), jnp.maximum(vertical[2], vertical[3]))
    top = REST + 4.0 * biggest
    middle, half = 0.5 * (top + LOW), 0.5 * (top - LOW)
    double = (jnp.full((8, 128), 2.0, F32) / jnp.broadcast_to(half, (8, 128)))

    def start_exchange(tile, rows, which):
        right = left = jnp.zeros((8, 128), F32)
        for i in range(24):
            here = lane // 4 == i
            right = jnp.where(here, pltpu.roll(tile(i // 6, i % 6, 3), (4 * i + 4) % 128, 1), right)
            left = jnp.where(here, pltpu.roll(tile(i // 6, i % 6, 0), (4 * i) % 128, 1), left)
        packs[which, 0] = right
        packs[which, 1] = left
        return [
            remote.start(rows(40), lat_in.at[which, 0], lon, north(1)),
            remote.start(rows(0), lat_in.at[which, 1], lon, north(-1)),
            remote.start(packs.at[which, 0], lon_in.at[which, 0], east(1), lat),
            remote.start(packs.at[which, 0], lon_in.at[which, 1], east(1), north(1)),
            remote.start(packs.at[which, 0], lon_in.at[which, 2], east(1), north(-1)),
            remote.start(packs.at[which, 1], lon_in.at[which, 3], east(-1), lat),
            remote.start(packs.at[which, 1], lon_in.at[which, 4], east(-1), north(1)),
            remote.start(packs.at[which, 1], lon_in.at[which, 5], east(-1), north(-1)),
        ]

    def finish_exchange(copies, put, which):
        for copy in copies:
            copy.wait_recv()
        ok = jnp.where(sub < 4, bottom_ok.astype(jnp.int32), top_ok.astype(jnp.int32)) > 0
        packed = [lon_in[which, i] for i in range(6)]
        for level in range(4):
            for t in range(7):
                if t < 6:
                    i = level * 6 + t
                    west, east_ = packed[0], packed[3]
                    westward = pltpu.roll(west, (124 - 4 * i) % 128, 1)
                    eastward = pltpu.roll(east_, (-4 * i) % 128, 1)
                    put(level, t, 4, jnp.where(lane < 64, eastward, westward))
                else:
                    first, last = level * 6, level * 6 + 5
                    westward = jnp.where(
                        sub < 4,
                        pltpu.roll(packed[2], (124 - 4 * first) % 128, 1),
                        pltpu.roll(packed[1], (124 - 4 * last) % 128, 1),
                    )
                    eastward = jnp.where(
                        sub < 4,
                        pltpu.roll(packed[5], (-4 * first) % 128, 1),
                        pltpu.roll(packed[4], (-4 * last) % 128, 1),
                    )
                    put(level, t, 4, jnp.where(ok, jnp.where(lane < 64, eastward, westward), 0.0))
            for b in range(4):
                above = lat_in[which, 0, level, :, 128 * b : 128 * b + 128]
                below = lat_in[which, 1, level, :, 128 * b : 128 * b + 128]
                put(level, 6, b, jnp.where(ok, jnp.where(sub < 4, below, above), 0.0))

    def vector(j):
        def tile(level, t, b):
            return vs[j, level + 1, 8 * t : 8 * t + 8, 128 * b : 128 * b + 128]

        def put(level, t, b, value):
            vs[j, level + 1, 8 * t : 8 * t + 8, 128 * b : 128 * b + 128] = value

        def rows(at):
            return vs.at[j, pl.ds(1, 4), pl.ds(at, 8), pl.ds(0, COLS)]

        return tile, rows, put

    def diag_tile(level, t, b):
        return dd[level, 8 * t : 8 * t + 8, 128 * b : 128 * b + 128]

    def diag_put(level, t, b, value):
        dd[level, 8 * t : 8 * t + 8, 128 * b : 128 * b + 128] = value

    def diag_rows(at):
        return dd.at[:, pl.ds(at, 8), pl.ds(0, COLS)]

    def wide(x, shape):
        return jnp.broadcast_to(x[0:1, 0:1], shape)

    def chebyshev(src, before, dst):
        mask = jnp.where(iota((8, XC), 0) < 4, bottom_ok.astype(F32), top_ok.astype(F32))
        scale = wide(double, (XR, XC))

        def one(level, carry):
            mid = vs[src, level + 1]
            sides = pltpu.roll(mid, 1, 1) + pltpu.roll(mid, XC - 1, 1)
            sides = sides + (pltpu.roll(mid, 1, 0) + pltpu.roll(mid, XR - 1, 0))
            stack = vs[src, level] + vs[src, level + 2]
            value = dd[level] * mid - scale * (sides + vertical[level] * stack)
            value = 0.5 * value if before is None else value - vs[before, level + 1]
            vs[dst, level + 1, 0:ROWS, :] = value[0:ROWS]
            vs[dst, level + 1, ROWS:XR, :] = value[ROWS:XR] * mask
            return carry

        lax.fori_loop(0, 4, one, 0)

    def build(base, count):
        for k in range(1, count):
            chebyshev(base + k - 1, None if k == 1 else base + k - 2, base + k)

    def all_reduce(value, turn):
        slot_lon[turn, lon] = value
        copies = [
            remote.start(slot_lon.at[turn, lon], slot_lon.at[turn, lon], east(k), lat) for k in range(1, nlon)
        ]
        for copy in copies:
            copy.wait_recv()
        value = slot_lon[turn, 0]
        for i in range(1, nlon):
            value = value + slot_lon[turn, i]
        slot_lat[turn, lat] = value
        copies = [
            remote.start(slot_lat.at[turn, lat], slot_lat.at[turn, lat], lon, north(k)) for k in range(1, nlat)
        ]
        for copy in copies:
            copy.wait_recv()
        value = slot_lat[turn, 0]
        for i in range(1, nlat):
            value = value + slot_lat[turn, i]
        return value

    def gram(count, turn, shared):
        pairs = [(i, j) for i in range(count) for j in range(i, count)]

        def one(t, sums):
            level, r = t // 6, pl.multiple_of((t % 6) * 8, 8)
            sums = list(sums)
            for b in range(4):
                tiles = [vs[i, level + 1, pl.ds(r, 8), 128 * b : 128 * b + 128] for i in range(count)]
                for n, (i, j) in enumerate(pairs):
                    sums[n] = sums[n] + tiles[i] * tiles[j]
            return tuple(sums)

        sums = lax.fori_loop(0, 24, one, tuple(jnp.zeros((8, 128), F32) for _ in pairs))
        for n, part in enumerate(sums):
            stage[n : n + 1, :] = jnp.sum(part, axis=0, keepdims=True)
        row = lax.dot_general(
            jnp.ones((8, 128), F32), stage[...], (((1,), (1,)), ((), ())),
            precision=lax.Precision.HIGHEST, preferred_element_type=F32,
        )
        return Gram(all_reduce(row, turn), pairs, shared)

    def combine(count, outputs):
        def one(t, carry):
            level, r = t // 6, pl.multiple_of((t % 6) * 8, 8)
            for b in range(4):
                tiles = [vs[i, level + 1, pl.ds(r, 8), 128 * b : 128 * b + 128] for i in range(count)]
                values = []
                for coef, _ in outputs:
                    value = None
                    for i, x in coef.items():
                        value = x * tiles[i] if value is None else value + x * tiles[i]
                    values.append(value)
                for value, (_, write) in zip(values, outputs):
                    write(level, pl.ds(r, 8), pl.ds(128 * b, 128), value)
            return carry

        lax.fori_loop(0, 24, one, 0)

    def put_out(level, r, b, value):
        out[level, r, b] = value

    def add_out(level, r, b, value):
        out[level, r, b] = out[level, r, b] + value

    def put_vector(j):
        def write(level, r, b, value):
            vs[j, level + 1, r, b] = value

        return write

    for copy in own:
        copy.wait()
    pl.semaphore_wait(barrier, greeted)

    b_tile, b_rows, b_put = vector(0)
    waiting = [start_exchange(diag_tile, diag_rows, 0), start_exchange(b_tile, b_rows, 1)]
    finish_exchange(waiting[0], diag_put, 0)

    def shift_diag(level, carry):
        add = 4.0 + 2.0 * vertical[level] - middle
        dd[level] = wide(double, (XR, XC)) * (dd[level] + add)
        return carry

    remote.drain()
    remote.all.clear()
    lax.fori_loop(0, 4, shift_diag, 0)
    finish_exchange(waiting[1], b_put, 1)
    build(0, STEPS + 1)
    answer, direction, residual, worst = coefficients(gram(STEPS + 1, 0, True), STEPS, middle, half, False)
    combine(
        STEPS + 1,
        [(answer, put_out), (direction, put_vector(0)), (residual, put_vector(STEPS + 1))],
    )
    p_tile, p_rows, p_put = vector(0)
    r_tile, r_rows, r_put = vector(STEPS + 1)
    waiting = [start_exchange(p_tile, p_rows, 2), start_exchange(r_tile, r_rows, 3)]
    finish_exchange(waiting[0], p_put, 2)
    build(0, STEPS + 1)
    finish_exchange(waiting[1], r_put, 3)
    build(STEPS + 1, STEPS)
    answer, _, _, second = coefficients(gram(2 * STEPS + 1, 1, False), STEPS, middle, half, True)
    combine(2 * STEPS + 1, [(answer, add_out)])
    flag[...] = jnp.maximum(worst, second)
    remote.drain()


def solve(departure, helm_diag, vertical, nlon, nlat):
    copies = 4 * 8 + 2 * (nlon - 1 + nlat - 1)
    vmem = pl.BlockSpec(memory_space=pltpu.VMEM)
    anywhere = pl.BlockSpec(memory_space=pl.ANY)
    return pl.pallas_call(
        partial(solve_kernel, nlon, nlat),
        out_shape=(
            jax.ShapeDtypeStruct(departure.shape, F32),
            jax.ShapeDtypeStruct((8, 128), F32),
        ),
        in_specs=[pl.BlockSpec(memory_space=pltpu.SMEM), anywhere, anywhere],
        out_specs=(vmem, vmem),
        scratch_shapes=[
            pltpu.VMEM((2 * STEPS + 1, 6, XR, XC), F32),
            pltpu.VMEM((4, XR, XC), F32),
            pltpu.VMEM((4, 2, 4, 8, COLS), F32),
            pltpu.VMEM((4, 6, 8, 128), F32),
            pltpu.VMEM((4, 2, 8, 128), F32),
            pltpu.VMEM((128, 128), F32),
            pltpu.VMEM((2, nlon, 8, 128), F32),
            pltpu.VMEM((2, nlat, 8, 128), F32),
            pltpu.SemaphoreType.DMA((2,)),
            pltpu.SemaphoreType.DMA((copies,)),
            pltpu.SemaphoreType.DMA((copies,)),
        ],
        compiler_params=pltpu.CompilerParams(
            collective_id=0, has_side_effects=True, vmem_limit_bytes=40 * 1024 * 1024
        ),
        name="solve",
    )(vertical, departure, helm_diag)


def iterate(departure, helm_diag, vertical):
    def one(_, carry):
        answer, residual, direction, norm = carry
        applied = operate(direction, helm_diag, vertical)
        rate = norm / lax.psum(jnp.sum(direction * applied), ("lon", "lat"))
        answer = answer + rate * direction
        residual = residual - rate * applied
        follow = squares(residual)
        return answer, residual, residual + follow / norm * direction, follow

    start = (jnp.zeros_like(departure), departure, departure, squares(departure))
    answer, _, direction, norm = lax.fori_loop(0, ITERS - 1, one, start)
    applied = operate(direction, helm_diag, vertical)
    return answer + norm / lax.psum(jnp.sum(direction * applied), ("lon", "lat")) * direction


def body(source_field, helm_diag, vertical, cubic_band, lat_offset, zonal_shift, row_class):
    levels, lat_rows, lon_cells = source_field.shape
    lon_count = lax.axis_size("lon")
    total_lon = lon_cells * lon_count
    blocks = jnp.mod(zonal_shift, total_lon // 128)
    row_table = jnp.dot(
        jax.nn.one_hot(row_class, cubic_band.shape[0], dtype=jnp.float32),
        cubic_band,
        precision=lax.Precision.HIGHEST,
    )
    padded = with_halo(source_field, (("lat", 1),), DRIFT, False)
    picked = jnp.take(padded, jnp.arange(lat_rows, dtype=jnp.int32) + DRIFT + lat_offset, axis=1)
    per_device = lon_cells // 128
    device_steps = (blocks // per_device)[None, :, None]
    remain = blocks % per_device

    def advance(counter, carry):
        current, result = carry
        current = shifted(current, "lon", 1)
        result = jnp.where(device_steps == counter, current, result)
        return (current, result)

    moved = lax.fori_loop(1, lon_count, advance, (picked, picked))[1]
    framed = with_halo(moved, (("lon", 2),), lon_cells, True)
    departure = finish(framed, remain, row_table, lon_cells)
    quick, worst = solve(departure, helm_diag, vertical, lon_count, lax.axis_size("lat"))
    answer = lax.cond(
        worst[0, 0] < LIMIT, lambda *_: quick, iterate, departure, helm_diag, vertical
    )
    return (departure, answer)


def solution(mesh):
    return jax.shard_map(
        body,
        mesh=mesh,
        in_specs=(
            P(None, "lat", "lon"),
            P(None, "lat", "lon"),
            P(),
            P(),
            P("lat"),
            P("lat"),
            P("lat"),
        ),
        out_specs=(P(None, "lat", "lon"), P(None, "lat", "lon")),
        check_vma=False,
    )
```

```python
from functools import partial

import jax
import jax.numpy as jnp
from jax import lax
from jax.experimental import pallas as pl
from jax.experimental.pallas import tpu as pltpu
from jax.sharding import PartitionSpec as P

DRIFT = 8
ITERS = 8


def with_halo(cells, sides, width, closed):
    for axis, dim in sides:
        count = lax.axis_size(axis)
        ends = count if closed else count - 1
        head = lax.slice_in_dim(cells, 0, width, axis=dim)
        tail = lax.slice_in_dim(cells, cells.shape[dim] - width, cells.shape[dim], axis=dim)
        cells = jnp.concatenate(
            [
                lax.ppermute(tail, axis, [(i, (i + 1) % count) for i in range(ends)]),
                cells,
                lax.ppermute(head, axis, [((i + 1) % count, i) for i in range(ends)]),
            ],
            axis=dim,
        )
    return cells


def local_terms(values, helm_diag, vertical, east_west, north_south):
    stacked = jnp.pad(values, ((1, 1), (0, 0), (0, 0)))
    up_down = stacked[2:] + stacked[:-2]
    coupling = vertical[:, None, None]
    return (
        (4.0 + 2.0 * coupling + helm_diag) * values - (east_west + north_south) - coupling * up_down
    )


def operate(values, helm_diag, vertical):
    zonal = with_halo(values, (("lon", 2),), 1, True)
    meridional = with_halo(values, (("lat", 1),), 1, False)
    east_west = zonal[:, :, 2:] + zonal[:, :, :-2]
    north_south = meridional[:, 2:, :] + meridional[:, :-2, :]
    return local_terms(values, helm_diag, vertical, east_west, north_south)


def squares(residual):
    return lax.psum(jnp.sum(residual * residual), ("lon", "lat"))


MESH = pl.DeviceIdType.MESH
F32 = jnp.float32
STEPS = 4
LOW, REST = 0.05, 9.0
LIMIT = 1.5e4
ROWS, COLS = 48, 512
XR, XC = 56, 640


def iota(shape, dim):
    return lax.broadcasted_iota(jnp.int32, shape, dim)


class Remote:
    def __init__(self, send_sems, recv_sems):
        self.send_sems, self.recv_sems, self.used, self.all = send_sems, recv_sems, 0, []

    def start(self, src, dst, lon, lat):
        copy = pltpu.make_async_remote_copy(
            src_ref=src,
            dst_ref=dst,
            send_sem=self.send_sems.at[self.used],
            recv_sem=self.recv_sems.at[self.used],
            device_id=(lon, lat),
            device_id_type=MESH,
        )
        self.used += 1
        copy.start()
        self.all.append(copy)
        return copy

    def settle(self, copies):
        for copy in copies:
            copy.wait_send()
            self.all = [other for other in self.all if other is not copy]

    def drain(self):
        for copy in self.all:
            copy.wait_send()


def coefficients(gram, steps, middle, half, final):
    shared = gram.shared
    base = 0 if shared else steps + 1

    def apply(vec):
        out = {}

        def add(i, x):
            out[i] = out[i] + x if i in out else x

        for i, x in vec.items():
            start = 0 if i <= steps else steps + 1
            add(i, x * middle)
            if i == start:
                add(i + 1, x * half)
            else:
                add(i + 1, x * (0.5 * half))
                add(i - 1, x * (0.5 * half))
        return out

    def form(a, b):
        total = size = None
        for i, x in a.items():
            inner = bulk = None
            for j, y in b.items():
                term = gram(i, j) * y
                inner = term if inner is None else inner + term
                bulk = jnp.abs(term) if bulk is None else bulk + jnp.abs(term)
            total = x * inner if total is None else total + x * inner
            size = jnp.abs(x) * bulk if size is None else size + jnp.abs(x) * bulk
        return total, size / jnp.abs(total)

    def plus(a, scale, b):
        return {i: a[i] + scale * b[i] if i in a and i in b else (a[i] if i in a else scale * b[i]) for i in {**a, **b}}

    one = jnp.ones((8, 128), F32)
    direction, residual, answer = {0: one}, {base: one}, {}
    norm, worst = gram(base, base), one
    for count in range(steps):
        applied = apply(direction)
        slope, size = form(direction, applied)
        worst = jnp.maximum(worst, size)
        rate = norm / slope
        answer = plus(answer, rate, direction)
        if not (final and count == steps - 1):
            residual = plus(residual, -rate, applied)
            follow, size = form(residual, residual)
            worst = jnp.maximum(worst, size)
            direction = plus(residual, follow / norm, direction)
            norm = follow
    return answer, direction, residual, worst


class Gram:
    def __init__(self, row, pairs, shared):
        self.row, self.place, self.shared, self.cache = row, {p: i for i, p in enumerate(pairs)}, shared, {}

    def __call__(self, i, j):
        pair = (min(i, j), max(i, j))
        if pair not in self.cache:
            at = self.place[pair]
            self.cache[pair] = jnp.broadcast_to(self.row[:, at : at + 1], (8, 128))
        return self.cache[pair]


def solve_kernel(
    nlon, nlat, vertical, band, offsets, shifts, classes, source, helm, dep, out, flag,
    inner, upper, lower, picked, gathered, circle, banded, returned,
    vs, dd, lat_in, lon_in, packs, stage, slot_lon, slot_lat, local_sems, send_sems, recv_sems,
):
    lon, lat = lax.axis_index("lon"), lax.axis_index("lat")

    def east(k):
        return lax.rem(lon + (k + nlon), nlon)

    def north(k):
        return lax.rem(lat + (k + nlat), nlat)

    own = [
        pltpu.make_async_copy(helm, dd.at[:, pl.ds(0, ROWS), pl.ds(0, COLS)], local_sems.at[0]),
        *[
            pltpu.make_async_copy(
                source.at[:, pl.ds(start, size), pl.ds(128 * b, 128)],
                into.at[:, b, pl.ds(at, size), :],
                local_sems.at[1 + 4 * n + b],
            )
            for n, (into, start, at, size) in enumerate(
                [(inner, 0, 0, ROWS), (upper, 0, DRIFT, 2 * DRIFT), (lower, ROWS - 2 * DRIFT, 0, 2 * DRIFT)]
            )
            for b in range(4)
        ],
    ]
    for copy in own:
        copy.start()
    barrier = pltpu.get_barrier_semaphore()
    greeted = 0
    for k in range(1, nlon):
        pl.semaphore_signal(barrier, inc=1, device_id=(east(k), lat), device_id_type=MESH)
        greeted += 1
    for k in range(1, nlat):
        pl.semaphore_signal(barrier, inc=1, device_id=(lon, north(k)), device_id_type=MESH)
        greeted += 1
    for a in (-1, 1):
        for b in (-1, 1):
            pl.semaphore_signal(barrier, inc=1, device_id=(east(a), north(b)), device_id_type=MESH)
            greeted += 1

    remote = Remote(send_sems, recv_sems)
    lane, sub = iota((8, 128), 1), iota((8, 128), 0)
    top_ok, bottom_ok = lat > 0, lat < nlat - 1

    zero = jnp.zeros((XR, XC), F32)
    for j in range(2 * STEPS + 1):
        vs[j, 0] = zero
        vs[j, 5] = zero
    stage[...] = jnp.zeros_like(stage)

    biggest = jnp.maximum(jnp.maximum(vertical[0], vertical[1]), jnp.maximum(vertical[2], vertical[3]))
    top = REST + 4.0 * biggest
    middle, half = 0.5 * (top + LOW), 0.5 * (top - LOW)
    double = (jnp.full((8, 128), 2.0, F32) / jnp.broadcast_to(half, (8, 128)))

    def start_exchange(tile, rows, which):
        right = left = jnp.zeros((8, 128), F32)
        for i in range(24):
            here = lane // 4 == i
            right = jnp.where(here, pltpu.roll(tile(i // 6, i % 6, 3), (4 * i + 4) % 128, 1), right)
            left = jnp.where(here, pltpu.roll(tile(i // 6, i % 6, 0), (4 * i) % 128, 1), left)
        packs[which, 0] = right
        packs[which, 1] = left
        return [
            remote.start(rows(40), lat_in.at[which, 0], lon, north(1)),
            remote.start(rows(0), lat_in.at[which, 1], lon, north(-1)),
            remote.start(packs.at[which, 0], lon_in.at[which, 0], east(1), lat),
            remote.start(packs.at[which, 0], lon_in.at[which, 1], east(1), north(1)),
            remote.start(packs.at[which, 0], lon_in.at[which, 2], east(1), north(-1)),
            remote.start(packs.at[which, 1], lon_in.at[which, 3], east(-1), lat),
            remote.start(packs.at[which, 1], lon_in.at[which, 4], east(-1), north(1)),
            remote.start(packs.at[which, 1], lon_in.at[which, 5], east(-1), north(-1)),
        ]

    def finish_exchange(copies, put, which):
        for copy in copies:
            copy.wait_recv()
        ok = jnp.where(sub < 4, bottom_ok.astype(jnp.int32), top_ok.astype(jnp.int32)) > 0
        packed = [lon_in[which, i] for i in range(6)]
        for level in range(4):
            for t in range(7):
                if t < 6:
                    i = level * 6 + t
                    west, east_ = packed[0], packed[3]
                    westward = pltpu.roll(west, (124 - 4 * i) % 128, 1)
                    eastward = pltpu.roll(east_, (-4 * i) % 128, 1)
                    put(level, t, 4, jnp.where(lane < 64, eastward, westward))
                else:
                    first, last = level * 6, level * 6 + 5
                    westward = jnp.where(
                        sub < 4,
                        pltpu.roll(packed[2], (124 - 4 * first) % 128, 1),
                        pltpu.roll(packed[1], (124 - 4 * last) % 128, 1),
                    )
                    eastward = jnp.where(
                        sub < 4,
                        pltpu.roll(packed[5], (-4 * first) % 128, 1),
                        pltpu.roll(packed[4], (-4 * last) % 128, 1),
                    )
                    put(level, t, 4, jnp.where(ok, jnp.where(lane < 64, eastward, westward), 0.0))
            for b in range(4):
                above = lat_in[which, 0, level, :, 128 * b : 128 * b + 128]
                below = lat_in[which, 1, level, :, 128 * b : 128 * b + 128]
                put(level, 6, b, jnp.where(ok, jnp.where(sub < 4, below, above), 0.0))

    def vector(j):
        def tile(level, t, b):
            return vs[j, level + 1, 8 * t : 8 * t + 8, 128 * b : 128 * b + 128]

        def put(level, t, b, value):
            vs[j, level + 1, 8 * t : 8 * t + 8, 128 * b : 128 * b + 128] = value

        def rows(at):
            return vs.at[j, pl.ds(1, 4), pl.ds(at, 8), pl.ds(0, COLS)]

        return tile, rows, put

    def diag_tile(level, t, b):
        return dd[level, 8 * t : 8 * t + 8, 128 * b : 128 * b + 128]

    def diag_put(level, t, b, value):
        dd[level, 8 * t : 8 * t + 8, 128 * b : 128 * b + 128] = value

    def diag_rows(at):
        return dd.at[:, pl.ds(at, 8), pl.ds(0, COLS)]

    def wide(x, shape):
        return jnp.broadcast_to(x[0:1, 0:1], shape)

    def chebyshev(src, before, dst):
        mask = jnp.where(iota((8, XC), 0) < 4, bottom_ok.astype(F32), top_ok.astype(F32))
        scale = wide(double, (XR, XC))

        def one(level, carry):
            mid = vs[src, level + 1]
            sides = pltpu.roll(mid, 1, 1) + pltpu.roll(mid, XC - 1, 1)
            sides = sides + (pltpu.roll(mid, 1, 0) + pltpu.roll(mid, XR - 1, 0))
            stack = vs[src, level] + vs[src, level + 2]
            value = dd[level] * mid - scale * (sides + vertical[level] * stack)
            value = 0.5 * value if before is None else value - vs[before, level + 1]
            vs[dst, level + 1, 0:ROWS, :] = value[0:ROWS]
            vs[dst, level + 1, ROWS:XR, :] = value[ROWS:XR] * mask
            return carry

        lax.fori_loop(0, 4, one, 0)

    def build(base, count):
        for k in range(1, count):
            chebyshev(base + k - 1, None if k == 1 else base + k - 2, base + k)

    def all_reduce(value, turn):
        slot_lon[turn, lon] = value
        copies = [
            remote.start(slot_lon.at[turn, lon], slot_lon.at[turn, lon], east(k), lat) for k in range(1, nlon)
        ]
        for copy in copies:
            copy.wait_recv()
        value = slot_lon[turn, 0]
        for i in range(1, nlon):
            value = value + slot_lon[turn, i]
        slot_lat[turn, lat] = value
        copies = [
            remote.start(slot_lat.at[turn, lat], slot_lat.at[turn, lat], lon, north(k)) for k in range(1, nlat)
        ]
        for copy in copies:
            copy.wait_recv()
        value = slot_lat[turn, 0]
        for i in range(1, nlat):
            value = value + slot_lat[turn, i]
        return value

    def gram(count, turn, shared):
        pairs = [(i, j) for i in range(count) for j in range(i, count)]

        def one(t, sums):
            level, r = t // 6, pl.multiple_of((t % 6) * 8, 8)
            sums = list(sums)
            for b in range(4):
                tiles = [vs[i, level + 1, pl.ds(r, 8), 128 * b : 128 * b + 128] for i in range(count)]
                for n, (i, j) in enumerate(pairs):
                    sums[n] = sums[n] + tiles[i] * tiles[j]
            return tuple(sums)

        sums = lax.fori_loop(0, 24, one, tuple(jnp.zeros((8, 128), F32) for _ in pairs))
        for n, part in enumerate(sums):
            stage[n : n + 1, :] = jnp.sum(part, axis=0, keepdims=True)
        row = lax.dot_general(
            jnp.ones((8, 128), F32), stage[...], (((1,), (1,)), ((), ())),
            precision=lax.Precision.HIGHEST, preferred_element_type=F32,
        )
        return Gram(all_reduce(row, turn), pairs, shared)

    def combine(count, outputs):
        def one(t, carry):
            level, r = t // 6, pl.multiple_of((t % 6) * 8, 8)
            for b in range(4):
                tiles = [vs[i, level + 1, pl.ds(r, 8), 128 * b : 128 * b + 128] for i in range(count)]
                values = []
                for coef, _ in outputs:
                    value = None
                    for i, x in coef.items():
                        value = x * tiles[i] if value is None else value + x * tiles[i]
                    values.append(value)
                for value, (_, write) in zip(values, outputs):
                    write(level, pl.ds(r, 8), pl.ds(128 * b, 128), value)
            return carry

        lax.fori_loop(0, 24, one, 0)

    def put_out(level, r, b, value):
        out[level, r, b] = value

    def add_out(level, r, b, value):
        out[level, r, b] = out[level, r, b] + value

    def put_vector(j):
        def write(level, r, b, value):
            vs[j, level + 1, r, b] = value

        return write

    for copy in own[1:5]:
        copy.wait()

    def pick(j, part, write):
        from_, first, rows = [(inner, 0, ROWS), (upper, -DRIFT, 3 * DRIFT), (lower, ROWS - 2 * DRIFT, 3 * DRIFT)][part]
        row = jnp.clip(j + offsets[j] - first, 0, rows - 1)
        for level in range(4):
            for b in range(4):
                write(4 * level + b, from_[level, b, pl.ds(row, 1), :])

    def pick_rows(c, k, rows, at, parts):
        for n, (j, part) in enumerate(zip(rows, parts)):

            def write(place, value, n=n):
                if k == nlon:
                    gathered[c, at + 16 * n + place : at + 16 * n + place + 1, :] = value
                else:
                    picked[k - 1, at + 16 * n + place : at + 16 * n + place + 1, :] = value

            pick(j, part, write)

    def middle_rows(c):
        return [DRIFT + 4 * c + q for q in range(4)]

    def edge_rows(c):
        return [c, ROWS - DRIFT + c]

    for k in range(1, nlon + 1):
        pick_rows(east(k % nlon), k, middle_rows(east(k % nlon)), 0, (0, 0, 0, 0))
    pl.semaphore_wait(barrier, greeted)
    beside = [
        remote.start(inner.at[:, :, pl.ds(ROWS - DRIFT, DRIFT), :], upper.at[:, :, pl.ds(0, DRIFT), :], lon, north(1)),
        remote.start(inner.at[:, :, pl.ds(0, DRIFT), :], lower.at[:, :, pl.ds(2 * DRIFT, DRIFT), :], lon, north(-1)),
    ]

    def send_picked(start, size):
        return [
            remote.start(
                picked.at[k - 1, pl.ds(start, size)], gathered.at[lon, pl.ds(start, size)], east(k), lat
            )
            for k in range(1, nlon)
        ]

    sent_middle = send_picked(0, 64)
    own[0].wait()
    diag_waiting = start_exchange(diag_tile, diag_rows, 0)
    for copy in own[5:]:
        copy.wait()
    for copy in beside:
        copy.wait_recv()
    for k in range(1, nlon + 1):
        pick_rows(east(k % nlon), k, edge_rows(east(k % nlon)), 64, (1, 2))
    sent_edge = send_picked(64, 32)

    finish_exchange(diag_waiting, diag_put, 0)
    remote.settle(diag_waiting)

    def shift_diag(level, carry):
        add = 4.0 + 2.0 * vertical[level] - middle
        dd[level] = wide(double, (XR, XC)) * (dd[level] + add)
        return carry

    lax.fori_loop(0, 4, shift_diag, 0)

    first_half = sub < 4
    lanes = iota((32, 128), 1)

    def band_rows(pp, j):
        low = pl.multiple_of(pp * 8, 8)
        for m in range(4):
            a, b = gathered[2 * m, pl.ds(low, 8), :], gathered[2 * m + 1, pl.ds(low, 8), :]
            pair = (
                jnp.where(first_half, a, pltpu.roll(b, 4, 0)),
                jnp.where(first_half, pltpu.roll(a, 4, 0), b),
            )
            for n in range(2):
                circle[2 * pp + n, 8 + 8 * m : 16 + 8 * m, :] = pair[n]
                circle[2 * pp + n, 40 + 8 * m : 48 + 8 * m, :] = pair[n]
                if m == 3:
                    circle[2 * pp + n, 0:8, :] = pair[n]
                if m == 0:
                    circle[2 * pp + n, 72:80, :] = pair[n]
        start = 8 + lax.rem(64 - shifts[j], 32)
        kind = classes[j]
        outs = []
        for n in range(2):
            now = circle[2 * pp + n, pl.ds(start, 32), :]
            before = circle[2 * pp + n, pl.ds(start - 1, 32), :]
            after = circle[2 * pp + n, pl.ds(start + 1, 32), :]
            total = band[kind, 0] * pltpu.roll(jnp.where(lanes == 127, before, now), 1, 1)
            total = total + band[kind, 1] * now
            total = total + band[kind, 2] * pltpu.roll(jnp.where(lanes == 0, after, now), 127, 1)
            total = total + band[kind, 3] * pltpu.roll(jnp.where(lanes < 2, after, now), 126, 1)
            outs.append(total)
        for m in range(4):
            a, b = outs[0][8 * m : 8 * m + 8], outs[1][8 * m : 8 * m + 8]
            banded[2 * m, pl.ds(low, 8), :] = jnp.where(first_half, a, pltpu.roll(b, 4, 0))
            banded[2 * m + 1, pl.ds(low, 8), :] = jnp.where(first_half, pltpu.roll(a, 4, 0), b)

    def middle_band(pp, carry):
        band_rows(pp, DRIFT + 4 * lon + pp // 2)
        return carry

    def edge_band(pp, carry):
        band_rows(pp, lon + (ROWS - DRIFT) * ((pp - 8) // 2))
        return carry

    def send_banded(start, size):
        here = pl.multiple_of(lon * 96 + start, 8)
        copies = [
            remote.start(banded.at[east(k), pl.ds(start, size)], returned.at[pl.ds(here, size)], east(k), lat)
            for k in range(1, nlon)
        ]
        returned[pl.ds(here, size), :] = banded[lon, pl.ds(start, size), :]
        return copies

    for copy in sent_middle:
        copy.wait_recv()
    lax.fori_loop(0, 8, middle_band, 0)
    back_middle = send_banded(0, 64)
    for copy in sent_edge:
        copy.wait_recv()
    lax.fori_loop(8, 12, edge_band, 0)
    back_edge = send_banded(64, 32)
    for copy in back_middle + back_edge:
        copy.wait_recv()
    b_tile, b_rows, b_put = vector(0)
    for level in range(4):
        for b in range(4):
            place = 4 * level + b
            for t in range(6):
                if t in (0, 5):
                    tile = returned[pl.ds(64 + 16 * (t // 5) + place, 8, stride=96), :]
                else:
                    tile = jnp.concatenate(
                        [returned[pl.ds((2 * t - 2 + n) * 96 + place, 4, stride=16), :] for n in range(2)], 0
                    )
                b_put(level, t, b, tile)
                dep[level, 8 * t : 8 * t + 8, 128 * b : 128 * b + 128] = tile
    waiting = [None, start_exchange(b_tile, b_rows, 1)]
    finish_exchange(waiting[1], b_put, 1)
    build(0, STEPS + 1)
    answer, direction, residual, worst = coefficients(gram(STEPS + 1, 0, True), STEPS, middle, half, False)
    remote.settle(waiting[1])
    combine(
        STEPS + 1,
        [(answer, put_out), (direction, put_vector(0)), (residual, put_vector(STEPS + 1))],
    )
    p_tile, p_rows, p_put = vector(0)
    r_tile, r_rows, r_put = vector(STEPS + 1)
    waiting = [start_exchange(p_tile, p_rows, 2), start_exchange(r_tile, r_rows, 3)]
    finish_exchange(waiting[0], p_put, 2)
    build(0, STEPS + 1)
    finish_exchange(waiting[1], r_put, 3)
    build(STEPS + 1, STEPS)
    answer, _, _, second = coefficients(gram(2 * STEPS + 1, 1, False), STEPS, middle, half, True)
    combine(2 * STEPS + 1, [(answer, add_out)])
    flag[...] = jnp.maximum(worst, second)
    remote.drain()


def solve(source_field, helm_diag, vertical, band, offsets, shifts, classes, nlon, nlat):
    copies = 2 + 4 * (nlon - 1) + 4 * 8 + 2 * (nlon - 1 + nlat - 1)
    vmem = pl.BlockSpec(memory_space=pltpu.VMEM)
    smem = pl.BlockSpec(memory_space=pltpu.SMEM)
    anywhere = pl.BlockSpec(memory_space=pl.ANY)
    field = jax.ShapeDtypeStruct(source_field.shape, F32)
    return pl.pallas_call(
        partial(solve_kernel, nlon, nlat),
        out_shape=(field, field, jax.ShapeDtypeStruct((8, 128), F32)),
        in_specs=[smem] * 5 + [anywhere, anywhere],
        out_specs=(vmem, vmem, vmem),
        scratch_shapes=[
            pltpu.VMEM((4, 4, ROWS, 128), F32),
            pltpu.VMEM((4, 4, 3 * DRIFT, 128), F32),
            pltpu.VMEM((4, 4, 3 * DRIFT, 128), F32),
            pltpu.VMEM((nlon - 1, 96, 128), F32),
            pltpu.VMEM((nlon, 96, 128), F32),
            pltpu.VMEM((24, 80, 128), F32),
            pltpu.VMEM((nlon, 96, 128), F32),
            pltpu.VMEM((nlon * 96, 128), F32),
            pltpu.VMEM((2 * STEPS + 1, 6, XR, XC), F32),
            pltpu.VMEM((4, XR, XC), F32),
            pltpu.VMEM((4, 2, 4, 8, COLS), F32),
            pltpu.VMEM((4, 6, 8, 128), F32),
            pltpu.VMEM((4, 2, 8, 128), F32),
            pltpu.VMEM((128, 128), F32),
            pltpu.VMEM((2, nlon, 8, 128), F32),
            pltpu.VMEM((2, nlat, 8, 128), F32),
            pltpu.SemaphoreType.DMA((13,)),
            pltpu.SemaphoreType.DMA((copies,)),
            pltpu.SemaphoreType.DMA((copies,)),
        ],
        compiler_params=pltpu.CompilerParams(
            collective_id=0, has_side_effects=True, vmem_limit_bytes=40 * 1024 * 1024
        ),
        name="solve",
    )(vertical, band, offsets, shifts, classes, source_field, helm_diag)


def iterate(departure, helm_diag, vertical):
    def one(_, carry):
        answer, residual, direction, norm = carry
        applied = operate(direction, helm_diag, vertical)
        rate = norm / lax.psum(jnp.sum(direction * applied), ("lon", "lat"))
        answer = answer + rate * direction
        residual = residual - rate * applied
        follow = squares(residual)
        return answer, residual, residual + follow / norm * direction, follow

    start = (jnp.zeros_like(departure), departure, departure, squares(departure))
    answer, _, direction, norm = lax.fori_loop(0, ITERS - 1, one, start)
    applied = operate(direction, helm_diag, vertical)
    return answer + norm / lax.psum(jnp.sum(direction * applied), ("lon", "lat")) * direction


def body(source_field, helm_diag, vertical, cubic_band, lat_offset, zonal_shift, row_class):
    departure, quick, worst = solve(
        source_field, helm_diag, vertical, cubic_band, lat_offset, zonal_shift, row_class,
        lax.axis_size("lon"), lax.axis_size("lat"),
    )
    answer = lax.cond(
        worst[0, 0] < LIMIT, lambda *_: quick, iterate, departure, helm_diag, vertical
    )
    return (departure, answer)


def solution(mesh):
    return jax.shard_map(
        body,
        mesh=mesh,
        in_specs=(
            P(None, "lat", "lon"),
            P(None, "lat", "lon"),
            P(),
            P(),
            P("lat"),
            P("lat"),
            P("lat"),
        ),
        out_specs=(P(None, "lat", "lon"), P(None, "lat", "lon")),
        check_vma=False,
    )
```

```python
from functools import partial

import jax
import jax.numpy as jnp
from jax import lax
from jax.experimental import pallas as pl
from jax.experimental.pallas import tpu as pltpu
from jax.sharding import PartitionSpec as P

DRIFT = 8
ITERS = 8


def with_halo(cells, sides, width, closed):
    for axis, dim in sides:
        count = lax.axis_size(axis)
        ends = count if closed else count - 1
        head = lax.slice_in_dim(cells, 0, width, axis=dim)
        tail = lax.slice_in_dim(cells, cells.shape[dim] - width, cells.shape[dim], axis=dim)
        cells = jnp.concatenate(
            [
                lax.ppermute(tail, axis, [(i, (i + 1) % count) for i in range(ends)]),
                cells,
                lax.ppermute(head, axis, [((i + 1) % count, i) for i in range(ends)]),
            ],
            axis=dim,
        )
    return cells


def local_terms(values, helm_diag, vertical, east_west, north_south):
    stacked = jnp.pad(values, ((1, 1), (0, 0), (0, 0)))
    up_down = stacked[2:] + stacked[:-2]
    coupling = vertical[:, None, None]
    return (
        (4.0 + 2.0 * coupling + helm_diag) * values - (east_west + north_south) - coupling * up_down
    )


def operate(values, helm_diag, vertical):
    zonal = with_halo(values, (("lon", 2),), 1, True)
    meridional = with_halo(values, (("lat", 1),), 1, False)
    east_west = zonal[:, :, 2:] + zonal[:, :, :-2]
    north_south = meridional[:, 2:, :] + meridional[:, :-2, :]
    return local_terms(values, helm_diag, vertical, east_west, north_south)


def squares(residual):
    return lax.psum(jnp.sum(residual * residual), ("lon", "lat"))


MESH = pl.DeviceIdType.MESH
F32 = jnp.float32
STEPS = 8
LIMIT = 1.5e4
ROWS, COLS = 48, 512
XR, XC = 64, 640


def iota(shape, dim):
    return lax.broadcasted_iota(jnp.int32, shape, dim)


class Remote:
    def __init__(self, send_sems, recv_sems):
        self.send_sems, self.recv_sems, self.used, self.all = send_sems, recv_sems, 0, []

    def start(self, src, dst, lon, lat):
        copy = pltpu.make_async_remote_copy(
            src_ref=src,
            dst_ref=dst,
            send_sem=self.send_sems.at[self.used],
            recv_sem=self.recv_sems.at[self.used],
            device_id=(lon, lat),
            device_id_type=MESH,
        )
        self.used += 1
        copy.start()
        self.all.append(copy)
        return copy

    def settle(self, copies):
        for copy in copies:
            copy.wait_send()
            self.all = [other for other in self.all if other is not copy]

    def drain(self):
        for copy in self.all:
            copy.wait_send()


def coefficients(gram, steps, middle, half):
    def apply(vec):
        out = {}

        def add(i, x):
            out[i] = out[i] + x if i in out else x

        for i, x in vec.items():
            add(i, x * middle)
            if i == 0:
                add(1, x * half)
            else:
                add(i + 1, x * (0.5 * half))
                add(i - 1, x * (0.5 * half))
        return out

    def form(a, b):
        total = size = None
        for i, x in a.items():
            inner = bulk = None
            for j, y in b.items():
                term = gram(i, j) * y
                inner = term if inner is None else inner + term
                bulk = jnp.abs(term) if bulk is None else bulk + jnp.abs(term)
            total = x * inner if total is None else total + x * inner
            size = jnp.abs(x) * bulk if size is None else size + jnp.abs(x) * bulk
        return total, size / jnp.abs(total)

    def plus(a, scale, b):
        return {i: a[i] + scale * b[i] if i in a and i in b else (a[i] if i in a else scale * b[i]) for i in {**a, **b}}

    one = jnp.ones((8, 128), F32)
    direction, residual, answer = {0: one}, {0: one}, {}
    norm, worst = gram(0, 0), one
    for count in range(steps):
        applied = apply(direction)
        slope, size = form(direction, applied)
        worst = jnp.maximum(worst, size)
        rate = norm / slope
        answer = plus(answer, rate, direction)
        if count < steps - 1:
            residual = plus(residual, -rate, applied)
            follow, size = form(residual, residual)
            worst = jnp.maximum(worst, size)
            direction = plus(residual, follow / norm, direction)
            norm = follow
    return answer, worst


class Gram:
    def __init__(self, row, pairs):
        self.row, self.place, self.cache = row, {p: i for i, p in enumerate(pairs)}, {}

    def __call__(self, i, j):
        pair = (min(i, j), max(i, j))
        if pair not in self.cache:
            at = self.place[pair]
            self.cache[pair] = jnp.broadcast_to(self.row[:, at : at + 1], (8, 128))
        return self.cache[pair]


def solve_kernel(
    nlon, nlat, vertical, band, offsets, shifts, classes, source, helm, dep, out, flag,
    inner, upper, lower, picked, gathered, circle, banded, returned,
    vs, dd, lon_in, packs, stage, slot_lon, slot_lat, local_sems, send_sems, recv_sems,
):
    lon, lat = lax.axis_index("lon"), lax.axis_index("lat")

    def east(k):
        return lax.rem(lon + (k + nlon), nlon)

    def north(k):
        return lax.rem(lat + (k + nlat), nlat)

    own = [
        pltpu.make_async_copy(helm, dd.at[:, pl.ds(0, ROWS), pl.ds(0, COLS)], local_sems.at[0]),
        *[
            pltpu.make_async_copy(
                source.at[:, pl.ds(start, size), pl.ds(128 * b, 128)],
                into.at[:, b, pl.ds(at, size), :],
                local_sems.at[1 + 4 * n + b],
            )
            for n, (into, start, at, size) in enumerate(
                [(inner, 0, 0, ROWS), (upper, 0, DRIFT, 2 * DRIFT), (lower, ROWS - 2 * DRIFT, 0, 2 * DRIFT)]
            )
            for b in range(4)
        ],
    ]
    for copy in own:
        copy.start()
    barrier = pltpu.get_barrier_semaphore()
    greeted = 0
    for k in range(1, nlon):
        pl.semaphore_signal(barrier, inc=1, device_id=(east(k), lat), device_id_type=MESH)
        greeted += 1
    for k in range(1, nlat):
        pl.semaphore_signal(barrier, inc=1, device_id=(lon, north(k)), device_id_type=MESH)
        greeted += 1
    for a in (-1, 1):
        for b in (-1, 1):
            pl.semaphore_signal(barrier, inc=1, device_id=(east(a), north(b)), device_id_type=MESH)
            greeted += 1

    remote = Remote(send_sems, recv_sems)
    lane, sub = iota((8, 128), 1), iota((8, 128), 0)
    top_ok, bottom_ok = lat > 0, lat < nlat - 1

    zero = jnp.zeros((XR, XC), F32)
    for j in range(STEPS + 1):
        vs[j, 0] = zero
        vs[j, 5] = zero
    stage[...] = jnp.zeros_like(stage)

    mean = 0.25 * ((vertical[0] + vertical[1]) + (vertical[2] + vertical[3]))
    top = 0.9 * (9.0 + 4.0 * mean)
    middle, half = 0.54 * top, 0.46 * top
    double = jnp.full((8, 128), 2.0, F32) / jnp.broadcast_to(half, (8, 128))

    def start_exchange(tile, place, which):
        for h in range(2):
            right = left = jnp.zeros((8, 128), F32)
            for i in range(12):
                here = lane // 8 == i
                level = 2 * h + i // 6
                right = jnp.where(here, pltpu.roll(tile(level, i % 6, 3), (8 * i + 8) % 128, 1), right)
                left = jnp.where(here, pltpu.roll(tile(level, i % 6, 0), 8 * i, 1), left)
            packs[which, 0, h] = right
            packs[which, 1, h] = left
        return [
            remote.start(place(ROWS - 8), place(ROWS + 8), lon, north(1)),
            remote.start(place(0), place(ROWS), lon, north(-1)),
            remote.start(packs.at[which, 0], lon_in.at[which, 0], east(1), lat),
            remote.start(packs.at[which, 0], lon_in.at[which, 1], east(1), north(1)),
            remote.start(packs.at[which, 0], lon_in.at[which, 2], east(1), north(-1)),
            remote.start(packs.at[which, 1], lon_in.at[which, 3], east(-1), lat),
            remote.start(packs.at[which, 1], lon_in.at[which, 4], east(-1), north(1)),
            remote.start(packs.at[which, 1], lon_in.at[which, 5], east(-1), north(-1)),
        ]

    def finish_exchange(copies, put, which):
        for copy in copies:
            copy.wait_recv()
        for level in range(4):
            packed = [lon_in[which, i, level // 2] for i in range(6)]
            for t in range(8):
                i = 6 * (level % 2) + (t if t < 6 else 0 if t == 6 else 5)
                side = 0 if t < 6 else 2 if t == 6 else 1
                westward = pltpu.roll(packed[side], (120 - 8 * i) % 128, 1)
                eastward = pltpu.roll(packed[3 + side], (-8 * i) % 128, 1)
                put(level, t, 4, jnp.where(lane < 64, eastward, westward))
        for missing, t in ((lat == nlat - 1, 6), (lat == 0, 7)):

            @pl.when(missing)
            def _(t=t):
                for level in range(4):
                    for b in range(5):
                        put(level, t, b, jnp.zeros((8, 128), F32))

    def vector(j):
        def tile(level, t, b):
            return vs[j, level + 1, 8 * t : 8 * t + 8, 128 * b : 128 * b + 128]

        def put(level, t, b, value):
            vs[j, level + 1, 8 * t : 8 * t + 8, 128 * b : 128 * b + 128] = value

        def rows(at):
            return vs.at[j, pl.ds(1, 4), pl.ds(at, 8), pl.ds(0, COLS)]

        return tile, rows, put

    def diag_tile(level, t, b):
        return dd[level, 8 * t : 8 * t + 8, 128 * b : 128 * b + 128]

    def diag_put(level, t, b, value):
        dd[level, 8 * t : 8 * t + 8, 128 * b : 128 * b + 128] = value

    def diag_rows(at):
        return dd.at[:, pl.ds(at, 8), pl.ds(0, COLS)]

    def wide(x, shape):
        return jnp.broadcast_to(x[0:1, 0:1], shape)

    def chebyshev(src, before, dst):
        mask = jnp.where(iota((16, XC), 0) < 8, bottom_ok.astype(F32), top_ok.astype(F32))
        scale = wide(double, (XR, XC))

        def one(level, carry):
            mid = vs[src, level + 1]
            sides = pltpu.roll(mid, 1, 1) + pltpu.roll(mid, XC - 1, 1)
            sides = sides + (pltpu.roll(mid, 1, 0) + pltpu.roll(mid, XR - 1, 0))
            stack = vs[src, level] + vs[src, level + 2]
            value = dd[level] * mid - scale * (sides + vertical[level] * stack)
            value = 0.5 * value if before is None else value - vs[before, level + 1]
            vs[dst, level + 1, 0:ROWS, :] = value[0:ROWS]
            vs[dst, level + 1, ROWS:XR, :] = value[ROWS:XR] * mask
            return carry

        lax.fori_loop(0, 4, one, 0)

    def build(base, count):
        for k in range(1, count):
            chebyshev(base + k - 1, None if k == 1 else base + k - 2, base + k)

    def all_reduce(value):
        slot_lon[lon] = value
        copies = [
            remote.start(slot_lon.at[lon], slot_lon.at[lon], east(k), lat) for k in range(1, nlon)
        ]
        for copy in copies:
            copy.wait_recv()
        value = slot_lon[0]
        for i in range(1, nlon):
            value = value + slot_lon[i]
        slot_lat[lat] = value
        copies = [
            remote.start(slot_lat.at[lat], slot_lat.at[lat], lon, north(k)) for k in range(1, nlat)
        ]
        for copy in copies:
            copy.wait_recv()
        value = slot_lat[0]
        for i in range(1, nlat):
            value = value + slot_lat[i]
        return value

    def gram():
        count = STEPS + 1
        pairs = [(i, j) for i in range(count) for j in range(i, count) if i < STEPS]

        def one(t, sums):
            level, r = t // 6, pl.multiple_of((t % 6) * 8, 8)
            sums = list(sums)
            for b in range(4):
                tiles = [vs[i, level + 1, pl.ds(r, 8), 128 * b : 128 * b + 128] for i in range(count)]
                for n, (i, j) in enumerate(pairs):
                    sums[n] = sums[n] + tiles[i] * tiles[j]
            return tuple(sums)

        sums = lax.fori_loop(0, 24, one, tuple(jnp.zeros((8, 128), F32) for _ in pairs))
        for n, part in enumerate(sums):
            stage[n : n + 1, :] = jnp.sum(part, axis=0, keepdims=True)
        row = lax.dot_general(
            jnp.ones((8, 128), F32), stage[...], (((1,), (1,)), ((), ())),
            precision=lax.Precision.HIGHEST, preferred_element_type=F32,
        )
        return Gram(all_reduce(row), pairs)

    def combine(coef):
        def one(t, carry):
            level, r = t // 6, pl.multiple_of((t % 6) * 8, 8)
            for b in range(4):
                value = None
                for i, x in coef.items():
                    term = x * vs[i, level + 1, pl.ds(r, 8), 128 * b : 128 * b + 128]
                    value = term if value is None else value + term
                out[level, pl.ds(r, 8), 128 * b : 128 * b + 128] = value
            return carry

        lax.fori_loop(0, 24, one, 0)

    for copy in own[1:5]:
        copy.wait()

    def pick(j, part, write):
        from_, first, rows = [(inner, 0, ROWS), (upper, -DRIFT, 3 * DRIFT), (lower, ROWS - 2 * DRIFT, 3 * DRIFT)][part]
        row = jnp.clip(j + offsets[j] - first, 0, rows - 1)
        for level in range(4):
            for b in range(4):
                write(4 * level + b, from_[level, b, pl.ds(row, 1), :])

    def pick_rows(c, k, rows, at, parts):
        for n, (j, part) in enumerate(zip(rows, parts)):

            def write(place, value, n=n):
                if k == nlon:
                    gathered[c, at + 16 * n + place : at + 16 * n + place + 1, :] = value
                else:
                    picked[k - 1, at + 16 * n + place : at + 16 * n + place + 1, :] = value

            pick(j, part, write)

    def middle_rows(c):
        return [DRIFT + 4 * c + q for q in range(4)]

    def edge_rows(c):
        return [c, ROWS - DRIFT + c]

    for k in range(1, nlon + 1):
        pick_rows(east(k % nlon), k, middle_rows(east(k % nlon)), 0, (0, 0, 0, 0))
    pl.semaphore_wait(barrier, greeted)
    beside = [
        remote.start(inner.at[:, :, pl.ds(ROWS - DRIFT, DRIFT), :], upper.at[:, :, pl.ds(0, DRIFT), :], lon, north(1)),
        remote.start(inner.at[:, :, pl.ds(0, DRIFT), :], lower.at[:, :, pl.ds(2 * DRIFT, DRIFT), :], lon, north(-1)),
    ]

    def send_picked(start, size):
        return [
            remote.start(
                picked.at[k - 1, pl.ds(start, size)], gathered.at[lon, pl.ds(start, size)], east(k), lat
            )
            for k in range(1, nlon)
        ]

    sent_middle = send_picked(0, 64)
    own[0].wait()
    diag_waiting = start_exchange(diag_tile, diag_rows, 0)
    for copy in own[5:]:
        copy.wait()
    for copy in beside:
        copy.wait_recv()
    for k in range(1, nlon + 1):
        pick_rows(east(k % nlon), k, edge_rows(east(k % nlon)), 64, (1, 2))
    sent_edge = send_picked(64, 32)

    finish_exchange(diag_waiting, diag_put, 0)
    remote.settle(diag_waiting)

    def shift_diag(level, carry):
        add = 4.0 + 2.0 * vertical[level] - middle
        dd[level] = wide(double, (XR, XC)) * (dd[level] + add)
        return carry

    lax.fori_loop(0, 4, shift_diag, 0)

    first_half = sub < 4
    lanes = iota((32, 128), 1)

    def band_rows(pp, j):
        low = pl.multiple_of(pp * 8, 8)
        for m in range(4):
            a, b = gathered[2 * m, pl.ds(low, 8), :], gathered[2 * m + 1, pl.ds(low, 8), :]
            pair = (
                jnp.where(first_half, a, pltpu.roll(b, 4, 0)),
                jnp.where(first_half, pltpu.roll(a, 4, 0), b),
            )
            for n in range(2):
                circle[2 * pp + n, 8 + 8 * m : 16 + 8 * m, :] = pair[n]
                circle[2 * pp + n, 40 + 8 * m : 48 + 8 * m, :] = pair[n]
                if m == 3:
                    circle[2 * pp + n, 0:8, :] = pair[n]
                if m == 0:
                    circle[2 * pp + n, 72:80, :] = pair[n]
        start = 8 + lax.rem(64 - shifts[j], 32)
        kind = classes[j]
        outs = []
        for n in range(2):
            now = circle[2 * pp + n, pl.ds(start, 32), :]
            before = circle[2 * pp + n, pl.ds(start - 1, 32), :]
            after = circle[2 * pp + n, pl.ds(start + 1, 32), :]
            total = band[kind, 0] * pltpu.roll(jnp.where(lanes == 127, before, now), 1, 1)
            total = total + band[kind, 1] * now
            total = total + band[kind, 2] * pltpu.roll(jnp.where(lanes == 0, after, now), 127, 1)
            total = total + band[kind, 3] * pltpu.roll(jnp.where(lanes < 2, after, now), 126, 1)
            outs.append(total)
        for m in range(4):
            a, b = outs[0][8 * m : 8 * m + 8], outs[1][8 * m : 8 * m + 8]
            banded[2 * m, pl.ds(low, 8), :] = jnp.where(first_half, a, pltpu.roll(b, 4, 0))
            banded[2 * m + 1, pl.ds(low, 8), :] = jnp.where(first_half, pltpu.roll(a, 4, 0), b)

    def middle_band(pp, carry):
        band_rows(pp, DRIFT + 4 * lon + pp // 2)
        return carry

    def edge_band(pp, carry):
        band_rows(pp, lon + (ROWS - DRIFT) * ((pp - 8) // 2))
        return carry

    def send_banded(start, size):
        here = pl.multiple_of(lon * 96 + start, 8)
        copies = [
            remote.start(banded.at[east(k), pl.ds(start, size)], returned.at[pl.ds(here, size)], east(k), lat)
            for k in range(1, nlon)
        ]
        returned[pl.ds(here, size), :] = banded[lon, pl.ds(start, size), :]
        return copies

    for copy in sent_middle:
        copy.wait_recv()
    lax.fori_loop(0, 8, middle_band, 0)
    back_middle = send_banded(0, 64)
    for copy in sent_edge:
        copy.wait_recv()
    lax.fori_loop(8, 12, edge_band, 0)
    back_edge = send_banded(64, 32)
    for copy in back_middle + back_edge:
        copy.wait_recv()
    b_tile, b_rows, b_put = vector(0)
    for level in range(4):
        for b in range(4):
            place = 4 * level + b
            for t in range(6):
                if t in (0, 5):
                    tile = returned[pl.ds(64 + 16 * (t // 5) + place, 8, stride=96), :]
                else:
                    tile = jnp.concatenate(
                        [returned[pl.ds((2 * t - 2 + n) * 96 + place, 4, stride=16), :] for n in range(2)], 0
                    )
                b_put(level, t, b, tile)
                dep[level, 8 * t : 8 * t + 8, 128 * b : 128 * b + 128] = tile
    waiting = start_exchange(b_tile, b_rows, 1)
    finish_exchange(waiting, b_put, 1)
    for k in range(1, STEPS + 1):
        chebyshev(k - 1, None if k == 1 else k - 2, k)
    answer, worst = coefficients(gram(), STEPS, middle, half)
    combine(answer)
    flag[...] = worst
    remote.drain()


def solve(source_field, helm_diag, vertical, band, offsets, shifts, classes, nlon, nlat):
    copies = 2 + 4 * (nlon - 1) + 2 * 8 + (nlon - 1 + nlat - 1)
    vmem = pl.BlockSpec(memory_space=pltpu.VMEM)
    smem = pl.BlockSpec(memory_space=pltpu.SMEM)
    anywhere = pl.BlockSpec(memory_space=pl.ANY)
    field = jax.ShapeDtypeStruct(source_field.shape, F32)
    return pl.pallas_call(
        partial(solve_kernel, nlon, nlat),
        out_shape=(field, field, jax.ShapeDtypeStruct((8, 128), F32)),
        in_specs=[smem] * 5 + [anywhere, anywhere],
        out_specs=(vmem, vmem, vmem),
        scratch_shapes=[
            pltpu.VMEM((4, 4, ROWS, 128), F32),
            pltpu.VMEM((4, 4, 3 * DRIFT, 128), F32),
            pltpu.VMEM((4, 4, 3 * DRIFT, 128), F32),
            pltpu.VMEM((nlon - 1, 96, 128), F32),
            pltpu.VMEM((nlon, 96, 128), F32),
            pltpu.VMEM((24, 80, 128), F32),
            pltpu.VMEM((nlon, 96, 128), F32),
            pltpu.VMEM((nlon * 96, 128), F32),
            pltpu.VMEM((STEPS + 1, 6, XR, XC), F32),
            pltpu.VMEM((4, XR, XC), F32),
            pltpu.VMEM((2, 6, 2, 8, 128), F32),
            pltpu.VMEM((2, 2, 2, 8, 128), F32),
            pltpu.VMEM((128, 128), F32),
            pltpu.VMEM((nlon, 8, 128), F32),
            pltpu.VMEM((nlat, 8, 128), F32),
            pltpu.SemaphoreType.DMA((13,)),
            pltpu.SemaphoreType.DMA((copies,)),
            pltpu.SemaphoreType.DMA((copies,)),
        ],
        compiler_params=pltpu.CompilerParams(
            collective_id=0, has_side_effects=True, vmem_limit_bytes=40 * 1024 * 1024
        ),
        name="solve",
    )(vertical, band, offsets, shifts, classes, source_field, helm_diag)


def iterate(departure, helm_diag, vertical):
    def one(_, carry):
        answer, residual, direction, norm = carry
        applied = operate(direction, helm_diag, vertical)
        rate = norm / lax.psum(jnp.sum(direction * applied), ("lon", "lat"))
        answer = answer + rate * direction
        residual = residual - rate * applied
        follow = squares(residual)
        return answer, residual, residual + follow / norm * direction, follow

    start = (jnp.zeros_like(departure), departure, departure, squares(departure))
    answer, _, direction, norm = lax.fori_loop(0, ITERS - 1, one, start)
    applied = operate(direction, helm_diag, vertical)
    return answer + norm / lax.psum(jnp.sum(direction * applied), ("lon", "lat")) * direction


def body(source_field, helm_diag, vertical, cubic_band, lat_offset, zonal_shift, row_class):
    departure, quick, worst = solve(
        source_field, helm_diag, vertical, cubic_band, lat_offset, zonal_shift, row_class,
        lax.axis_size("lon"), lax.axis_size("lat"),
    )
    answer = lax.cond(
        worst[0, 0] < LIMIT, lambda *_: quick, iterate, departure, helm_diag, vertical
    )
    return (departure, answer)


def solution(mesh):
    return jax.shard_map(
        body,
        mesh=mesh,
        in_specs=(
            P(None, "lat", "lon"),
            P(None, "lat", "lon"),
            P(),
            P(),
            P("lat"),
            P("lat"),
            P("lat"),
        ),
        out_specs=(P(None, "lat", "lon"), P(None, "lat", "lon")),
        check_vma=False,
    )
```

```python
import itertools
from functools import partial

import jax
import jax.numpy as jnp
from jax import lax
from jax.experimental import pallas as pl
from jax.experimental.pallas import tpu as pltpu
from jax.sharding import PartitionSpec as P

DRIFT = 8
ITERS = 8


def with_halo(cells, sides, width, closed):
    for axis, dim in sides:
        count = lax.axis_size(axis)
        ends = count if closed else count - 1
        head = lax.slice_in_dim(cells, 0, width, axis=dim)
        tail = lax.slice_in_dim(cells, cells.shape[dim] - width, cells.shape[dim], axis=dim)
        cells = jnp.concatenate(
            [
                lax.ppermute(tail, axis, [(i, (i + 1) % count) for i in range(ends)]),
                cells,
                lax.ppermute(head, axis, [((i + 1) % count, i) for i in range(ends)]),
            ],
            axis=dim,
        )
    return cells


def local_terms(values, helm_diag, vertical, east_west, north_south):
    stacked = jnp.pad(values, ((1, 1), (0, 0), (0, 0)))
    up_down = stacked[2:] + stacked[:-2]
    coupling = vertical[:, None, None]
    return (
        (4.0 + 2.0 * coupling + helm_diag) * values - (east_west + north_south) - coupling * up_down
    )


def operate(values, helm_diag, vertical):
    zonal = with_halo(values, (("lon", 2),), 1, True)
    meridional = with_halo(values, (("lat", 1),), 1, False)
    east_west = zonal[:, :, 2:] + zonal[:, :, :-2]
    north_south = meridional[:, 2:, :] + meridional[:, :-2, :]
    return local_terms(values, helm_diag, vertical, east_west, north_south)


def squares(residual):
    return lax.psum(jnp.sum(residual * residual), ("lon", "lat"))


MESH = pl.DeviceIdType.MESH
F32 = jnp.float32
STEPS = 8
SIZES = {"zl": 2, "x": 4, "zh": 2, "y": 4, "c": 2}
PLANE, REST = ("x", "y"), ("zl", "zh", "c")
LIMIT = 1.5e4
ROWS, COLS = 48, 512
XR, TOP, TILES = 80, 16, 5


def iota(shape, dim):
    return lax.broadcasted_iota(jnp.int32, shape, dim)


class Remote:
    def __init__(self, send_sems, recv_sems):
        self.send_sems, self.recv_sems, self.used, self.all = send_sems, recv_sems, 0, []

    def start(self, src, dst, lon, lat):
        copy = pltpu.make_async_remote_copy(
            src_ref=src,
            dst_ref=dst,
            send_sem=self.send_sems.at[self.used],
            recv_sem=self.recv_sems.at[self.used],
            device_id=(lon, lat),
            device_id_type=MESH,
        )
        self.used += 1
        copy.start()
        self.all.append(copy)
        return copy

    def settle(self, copies):
        for copy in copies:
            copy.wait_send()
            self.all = [other for other in self.all if other is not copy]

    def drain(self):
        for copy in self.all:
            copy.wait_send()


def coefficients(gram, steps, middle, half):
    def apply(vec):
        out = {}

        def add(i, x):
            out[i] = out[i] + x if i in out else x

        for i, x in vec.items():
            add(i, x * middle)
            if i == 0:
                add(1, x * half)
            else:
                add(i + 1, x * (0.5 * half))
                add(i - 1, x * (0.5 * half))
        return out

    def form(a, b):
        total = size = None
        for i, x in a.items():
            inner = bulk = None
            for j, y in b.items():
                term = gram(i, j) * y
                inner = term if inner is None else inner + term
                bulk = jnp.abs(term) if bulk is None else bulk + jnp.abs(term)
            total = x * inner if total is None else total + x * inner
            size = jnp.abs(x) * bulk if size is None else size + jnp.abs(x) * bulk
        return total, size / jnp.abs(total)

    def plus(a, scale, b):
        return {i: a[i] + scale * b[i] if i in a and i in b else (a[i] if i in a else scale * b[i]) for i in {**a, **b}}

    one = jnp.ones((8, 128), F32)
    direction, residual, answer = {0: one}, {0: one}, {}
    norm, worst = gram(0, 0), one
    for count in range(steps):
        applied = apply(direction)
        slope, size = form(direction, applied)
        worst = jnp.maximum(worst, size)
        rate = norm / slope
        answer = plus(answer, rate, direction)
        if count < steps - 1:
            residual = plus(residual, -rate, applied)
            follow, size = form(residual, residual)
            worst = jnp.maximum(worst, size)
            direction = plus(residual, follow / norm, direction)
            norm = follow
    return answer, worst


class Gram:
    def __init__(self, row, pairs):
        self.row, self.place, self.cache = row, {p: i for i, p in enumerate(pairs)}, {}

    def __call__(self, i, j):
        pair = (min(i, j), max(i, j))
        if pair not in self.cache:
            at = self.place[pair]
            self.cache[pair] = jnp.broadcast_to(self.row[:, at : at + 1], (8, 128))
        return self.cache[pair]


def solve_kernel(
    nlon, nlat, vertical, band, offsets, shifts, classes, source, helm, dep, out, flag,
    inner, upper, lower, picked, gathered, circle, banded, returned,
    vs, dd, lon_in, packs, stage, slot_plane, slot_rest, local_sems, send_sems, recv_sems,
):
    lon, lat = lax.axis_index("lon"), lax.axis_index("lat")

    def east(k):
        return lax.rem(lon + (k + nlon), nlon)

    def north(k):
        return lax.rem(lat + (k + nlat), nlat)

    here = {"zl": lon // 4, "x": lax.rem(lon, 4), "zh": lat // 8, "y": lax.rem(lat // 2, 4), "c": lax.rem(lat, 2)}

    def place_of(moves):
        spot = {a: lax.rem(v + moves.get(a, 0), SIZES[a]) for a, v in here.items()}
        return spot["zl"] * 4 + spot["x"], spot["zh"] * 8 + spot["y"] * 2 + spot["c"]

    def partners(axes):
        moves = [dict(zip(axes, m)) for m in itertools.product(*[range(SIZES[a]) for a in axes]) if any(m)]
        far = {"c": 0, "zl": 1, "zh": 2}
        return sorted(moves, key=lambda m: -sum(far.get(a, 1) * min(v, SIZES[a] - v) for a, v in m.items()))

    barrier = pltpu.get_barrier_semaphore()
    greet = [(east(k), lat) for k in range(1, nlon)]
    greet += [(lon, north(1)), (lon, north(-1))]
    greet += [(east(a), north(b)) for a in (-1, 1) for b in (-1, 1)]
    greet += [place_of(m) for m in partners(PLANE) if m["y"]]
    greet += [place_of(m) for m in partners(REST) if m["zh"] or m["c"]]
    for peer in greet:
        pl.semaphore_signal(barrier, inc=1, device_id=peer, device_id_type=MESH)
    greeted = len(greet)
    own = [
        pltpu.make_async_copy(
            source.at[:, pl.ds(start, size), pl.ds(128 * b, 128)],
            into.at[:, b, pl.ds(at, size), :],
            local_sems.at[4 * n + b],
        )
        for n, (into, start, at, size) in enumerate(
            [(inner, 0, 0, ROWS), (upper, 0, DRIFT, 2 * DRIFT), (lower, ROWS - 2 * DRIFT, 0, 2 * DRIFT)]
        )
        for b in range(4)
    ]
    own_diag = [
        pltpu.make_async_copy(
            helm.at[:, :, pl.ds(128 * b, 128)], dd.at[:, b, pl.ds(TOP, ROWS), :], local_sems.at[12 + b]
        )
        for b in range(4)
    ]
    for copy in own + own_diag:
        copy.start()

    remote = Remote(send_sems, recv_sems)
    lane, sub = iota((8, 128), 1), iota((8, 128), 0)
    top_ok, bottom_ok = lat > 0, lat < nlat - 1

    def clear():
        zero = jnp.zeros((8, 128), F32)

        def one(j, carry):
            for b in range(TILES):
                for t in range(XR // 8):
                    vs[j, 0, b, 8 * t : 8 * t + 8, :] = zero
                    vs[j, 5, b, 8 * t : 8 * t + 8, :] = zero
                for level in range(1, 5):
                    vs[j, level, b, 0:8, :] = zero
                    vs[j, level, b, XR - 8 : XR, :] = zero
            return carry

        lax.fori_loop(0, STEPS + 1, one, 0)
        stage[...] = jnp.zeros_like(stage)

    mean = 0.25 * ((vertical[0] + vertical[1]) + (vertical[2] + vertical[3]))
    top = 0.9 * (9.0 + 4.0 * mean)
    middle, half = 0.54 * top, 0.46 * top
    double = jnp.full((8, 128), 2.0, F32) / jnp.broadcast_to(half, (8, 128))

    def start_exchange(tile, place, which):
        for h in range(2):
            right = left = jnp.zeros((8, 128), F32)
            for i in range(12):
                here = lane // 8 == i
                level = 2 * h + i // 6
                right = jnp.where(here, pltpu.roll(tile(level, i % 6, 3), (8 * i + 8) % 128, 1), right)
                left = jnp.where(here, pltpu.roll(tile(level, i % 6, 0), 8 * i, 1), left)
            packs[which, 0, h] = right
            packs[which, 1, h] = left
        return [
            remote.start(place(TOP + ROWS - 8), place(TOP - 8), lon, north(1)),
            remote.start(place(TOP), place(TOP + ROWS), lon, north(-1)),
            remote.start(packs.at[which, 0], lon_in.at[which, 0], east(1), lat),
            remote.start(packs.at[which, 0], lon_in.at[which, 1], east(1), north(1)),
            remote.start(packs.at[which, 0], lon_in.at[which, 2], east(1), north(-1)),
            remote.start(packs.at[which, 1], lon_in.at[which, 3], east(-1), lat),
            remote.start(packs.at[which, 1], lon_in.at[which, 4], east(-1), north(1)),
            remote.start(packs.at[which, 1], lon_in.at[which, 5], east(-1), north(-1)),
        ]

    def finish_exchange(copies, put, which):
        for copy in copies:
            copy.wait_recv()
        for level in range(4):
            packed = [lon_in[which, i, level // 2] for i in range(6)]
            for t in range(-1, 7):
                i = 6 * (level % 2) + (5 if t < 0 else t if t < 6 else 0)
                side = 1 if t < 0 else 0 if t < 6 else 2
                westward = pltpu.roll(packed[side], (120 - 8 * i) % 128, 1)
                eastward = pltpu.roll(packed[3 + side], (-8 * i) % 128, 1)
                put(level, t, 4, jnp.where(lane < 64, eastward, westward))
        for missing, t in ((lat == nlat - 1, 6), (lat == 0, -1)):

            @pl.when(missing)
            def _(t=t):
                for level in range(4):
                    for b in range(5):
                        put(level, t, b, jnp.zeros((8, 128), F32))

    def b_tile(level, t, b):
        return vs[0, level + 1, b, TOP + 8 * t : TOP + 8 * t + 8, :]

    def b_put(level, t, b, value):
        vs[0, level + 1, b, TOP + 8 * t : TOP + 8 * t + 8, :] = value

    def b_rows(at):
        return vs.at[0, pl.ds(1, 4), pl.ds(0, 4), pl.ds(at, 8), :]

    def diag_tile(level, t, b):
        return dd[level, b, TOP + 8 * t : TOP + 8 * t + 8, :]

    def diag_put(level, t, b, value):
        dd[level, b, TOP + 8 * t : TOP + 8 * t + 8, :] = value

    def diag_rows(at):
        return dd.at[:, pl.ds(0, 4), pl.ds(at, 8), :]

    def shift_diag():
        def one(level, carry):
            add = 4.0 + 2.0 * vertical[level] - middle
            for b in range(TILES):
                for t in range(-1, 7):
                    value = double * (diag_tile(level, t, b) + add)
                    if t in (-1, 6):
                        value = jnp.where(top_ok if t < 0 else bottom_ok, value, 0.0)
                    diag_put(level, t, b, value)
            return carry

        lax.fori_loop(0, 4, one, 0)

    def chebyshev(src, before, dst):
        last = dst == STEPS
        first, count = (TOP, 3) if last else (TOP - 8, 4)

        def one(i, carry):
            level, pair = i // count, lax.rem(i, count)
            for u in range(2):
                r = pl.multiple_of(first + 16 * pair + 8 * u, 8)
                scale = double
                if not last and u == 0:
                    scale = jnp.where(jnp.logical_or(pair > 0, top_ok), double, 0.0)
                if not last and u == 1:
                    scale = jnp.where(jnp.logical_or(pair < count - 1, bottom_ok), double, 0.0)
                mids = [vs[src, level + 1, b, pl.ds(r, 8), :] for b in range(TILES)]
                for b in range(4 if last else TILES):
                    mid = mids[b]
                    sides = pltpu.roll(jnp.where(lane == 127, mids[b - 1], mid), 1, 1)
                    sides = sides + pltpu.roll(jnp.where(lane == 0, mids[(b + 1) % TILES], mid), 127, 1)
                    sides = sides + (
                        vs[src, level + 1, b, pl.ds(r - 1, 8), :] + vs[src, level + 1, b, pl.ds(r + 1, 8), :]
                    )
                    stack = vs[src, level, b, pl.ds(r, 8), :] + vs[src, level + 2, b, pl.ds(r, 8), :]
                    value = dd[level, b, pl.ds(r, 8), :] * mid - scale * (sides + vertical[level] * stack)
                    if before is None:
                        value = 0.5 * value
                    else:
                        value = value - vs[before, level + 1, b, pl.ds(r, 8), :]
                    vs[dst, level + 1, b, pl.ds(r, 8), :] = value
            return carry

        lax.fori_loop(0, 4 * count, one, 0)

    def all_reduce(value):
        for axes, slot in ((PLANE, slot_plane), (REST, slot_rest)):
            mine = 0
            for axis in axes:
                mine = mine * SIZES[axis] + here[axis]
            slot[mine] = value
            copies = [remote.start(slot.at[mine], slot.at[mine], *place_of(m)) for m in partners(axes)]
            for copy in copies:
                copy.wait_recv()
            value = slot[0]
            for i in range(1, slot.shape[0]):
                value = value + slot[i]
        return value

    def gram():
        count = STEPS + 1
        pairs = [(i, j) for i in range(count) for j in range(i, count) if i < STEPS]

        def one(t, sums):
            level, r = t // 6, pl.multiple_of((t % 6) * 8, 8)
            sums = list(sums)
            for b in range(4):
                tiles = [vs[i, level + 1, b, pl.ds(r + TOP, 8), :] for i in range(count)]
                for n, (i, j) in enumerate(pairs):
                    sums[n] = sums[n] + tiles[i] * tiles[j]
            return tuple(sums)

        sums = lax.fori_loop(0, 24, one, tuple(jnp.zeros((8, 128), F32) for _ in pairs))
        for n, part in enumerate(sums):
            stage[n : n + 1, :] = jnp.sum(part, axis=0, keepdims=True)
        row = lax.dot_general(
            jnp.ones((8, 128), F32), stage[...], (((1,), (1,)), ((), ())),
            precision=lax.Precision.HIGHEST, preferred_element_type=F32,
        )
        return Gram(all_reduce(row), pairs)

    def combine(coef):
        def one(t, carry):
            level, r = t // 6, pl.multiple_of((t % 6) * 8, 8)
            for b in range(4):
                value = None
                for i, x in coef.items():
                    term = x * vs[i, level + 1, b, pl.ds(r + TOP, 8), :]
                    value = term if value is None else value + term
                out[level, pl.ds(r, 8), 128 * b : 128 * b + 128] = value
            return carry

        lax.fori_loop(0, 24, one, 0)

    for copy in own[0:4]:
        copy.wait()

    def pick(j, part, write):
        from_, first, rows = [(inner, 0, ROWS), (upper, -DRIFT, 3 * DRIFT), (lower, ROWS - 2 * DRIFT, 3 * DRIFT)][part]
        row = jnp.clip(j + offsets[j] - first, 0, rows - 1)
        for level in range(4):
            for b in range(4):
                write(4 * level + b, from_[level, b, pl.ds(row, 1), :])

    def pick_rows(c, k, rows, at, parts):
        for n, (j, part) in enumerate(zip(rows, parts)):

            def write(place, value, n=n):
                if k == nlon:
                    gathered[c, at + 16 * n + place : at + 16 * n + place + 1, :] = value
                else:
                    picked[k - 1, at + 16 * n + place : at + 16 * n + place + 1, :] = value

            pick(j, part, write)

    def middle_rows(c):
        return [DRIFT + 4 * c + q for q in range(4)]

    def edge_rows(c):
        return [c, ROWS - DRIFT + c]

    for k in range(1, nlon + 1):
        pick_rows(east(k % nlon), k, middle_rows(east(k % nlon)), 0, (0, 0, 0, 0))
    pl.semaphore_wait(barrier, greeted)
    beside = [
        remote.start(inner.at[:, :, pl.ds(ROWS - DRIFT, DRIFT), :], upper.at[:, :, pl.ds(0, DRIFT), :], lon, north(1)),
        remote.start(inner.at[:, :, pl.ds(0, DRIFT), :], lower.at[:, :, pl.ds(2 * DRIFT, DRIFT), :], lon, north(-1)),
    ]

    def send_picked(start, size):
        return [
            remote.start(
                picked.at[k - 1, pl.ds(start, size)], gathered.at[lon, pl.ds(start, size)], east(k), lat
            )
            for k in range(1, nlon)
        ]

    sent_middle = send_picked(0, 64)
    for copy in own_diag:
        copy.wait()
    diag_waiting = start_exchange(diag_tile, diag_rows, 0)
    clear()
    for copy in own[4:]:
        copy.wait()
    for copy in beside:
        copy.wait_recv()
    for k in range(1, nlon + 1):
        pick_rows(east(k % nlon), k, edge_rows(east(k % nlon)), 64, (1, 2))
    sent_edge = send_picked(64, 32)

    finish_exchange(diag_waiting, diag_put, 0)
    remote.settle(diag_waiting)

    shift_diag()

    first_half = sub < 4
    lanes = iota((32, 128), 1)

    def band_rows(pp, j):
        low = pl.multiple_of(pp * 8, 8)
        for m in range(4):
            a, b = gathered[2 * m, pl.ds(low, 8), :], gathered[2 * m + 1, pl.ds(low, 8), :]
            pair = (
                jnp.where(first_half, a, pltpu.roll(b, 4, 0)),
                jnp.where(first_half, pltpu.roll(a, 4, 0), b),
            )
            for n in range(2):
                circle[2 * pp + n, 8 + 8 * m : 16 + 8 * m, :] = pair[n]
                circle[2 * pp + n, 40 + 8 * m : 48 + 8 * m, :] = pair[n]
                if m == 3:
                    circle[2 * pp + n, 0:8, :] = pair[n]
                if m == 0:
                    circle[2 * pp + n, 72:80, :] = pair[n]
        start = 8 + lax.rem(64 - shifts[j], 32)
        weight = [band[t, classes[j]] for t in range(4)]
        outs = []
        for n in range(2):
            now = circle[2 * pp + n, pl.ds(start, 32), :]
            before = circle[2 * pp + n, pl.ds(start - 1, 32), :]
            after = circle[2 * pp + n, pl.ds(start + 1, 32), :]
            total = weight[0] * pltpu.roll(jnp.where(lanes == 127, before, now), 1, 1)
            total = total + weight[1] * now
            total = total + weight[2] * pltpu.roll(jnp.where(lanes == 0, after, now), 127, 1)
            total = total + weight[3] * pltpu.roll(jnp.where(lanes < 2, after, now), 126, 1)
            outs.append(total)
        for m in range(4):
            a, b = outs[0][8 * m : 8 * m + 8], outs[1][8 * m : 8 * m + 8]
            banded[2 * m, pl.ds(low, 8), :] = jnp.where(first_half, a, pltpu.roll(b, 4, 0))
            banded[2 * m + 1, pl.ds(low, 8), :] = jnp.where(first_half, pltpu.roll(a, 4, 0), b)

    def middle_band(pp, carry):
        band_rows(pp, DRIFT + 4 * lon + pp // 2)
        return carry

    def edge_band(pp, carry):
        band_rows(pp, lon + (ROWS - DRIFT) * ((pp - 8) // 2))
        return carry

    def send_banded(start, size):
        here = pl.multiple_of(lon * 96 + start, 8)
        copies = [
            remote.start(banded.at[east(k), pl.ds(start, size)], returned.at[pl.ds(here, size)], east(k), lat)
            for k in range(1, nlon)
        ]
        returned[pl.ds(here, size), :] = banded[lon, pl.ds(start, size), :]
        return copies

    for copy in sent_middle:
        copy.wait_recv()
    lax.fori_loop(0, 8, middle_band, 0)
    back_middle = send_banded(0, 64)
    for copy in sent_edge:
        copy.wait_recv()
    lax.fori_loop(8, 12, edge_band, 0)
    back_edge = send_banded(64, 32)
    for copy in back_middle + back_edge:
        copy.wait_recv()
    for level in range(4):
        for b in range(4):
            place = 4 * level + b
            for t in range(6):
                if t in (0, 5):
                    tile = returned[pl.ds(64 + 16 * (t // 5) + place, 8, stride=96), :]
                else:
                    tile = jnp.concatenate(
                        [returned[pl.ds((2 * t - 2 + n) * 96 + place, 4, stride=16), :] for n in range(2)], 0
                    )
                b_put(level, t, b, tile)
                dep[level, 8 * t : 8 * t + 8, 128 * b : 128 * b + 128] = tile
    waiting = start_exchange(b_tile, b_rows, 1)
    finish_exchange(waiting, b_put, 1)
    for k in range(1, STEPS + 1):
        chebyshev(k - 1, None if k == 1 else k - 2, k)
    answer, worst = coefficients(gram(), STEPS, middle, half)
    combine(answer)
    flag[0, 0] = jnp.max(worst)
    remote.drain()


def solve(source_field, helm_diag, vertical, band, offsets, shifts, classes, nlon, nlat):
    copies = 2 + 4 * (nlon - 1) + 2 * 8 + 15 + 7
    vmem = pl.BlockSpec(memory_space=pltpu.VMEM)
    smem = pl.BlockSpec(memory_space=pltpu.SMEM)
    far = pl.BlockSpec(memory_space=pltpu.HBM)
    field = jax.ShapeDtypeStruct(source_field.shape, F32)
    return pl.pallas_call(
        partial(solve_kernel, nlon, nlat),
        out_shape=(field, field, jax.ShapeDtypeStruct((1, 1), F32)),
        in_specs=[smem] * 5 + [far, far],
        out_specs=(vmem, vmem, smem),
        scratch_shapes=[
            pltpu.VMEM((4, 4, ROWS, 128), F32),
            pltpu.VMEM((4, 4, 3 * DRIFT, 128), F32),
            pltpu.VMEM((4, 4, 3 * DRIFT, 128), F32),
            pltpu.VMEM((nlon - 1, 96, 128), F32),
            pltpu.VMEM((nlon, 96, 128), F32),
            pltpu.VMEM((24, 80, 128), F32),
            pltpu.VMEM((nlon, 96, 128), F32),
            pltpu.VMEM((nlon * 96, 128), F32),
            pltpu.VMEM((STEPS + 1, 6, TILES, XR, 128), F32),
            pltpu.VMEM((4, TILES, XR, 128), F32),
            pltpu.VMEM((2, 6, 2, 8, 128), F32),
            pltpu.VMEM((2, 2, 2, 8, 128), F32),
            pltpu.VMEM((128, 128), F32),
            pltpu.VMEM((16, 8, 128), F32),
            pltpu.VMEM((8, 8, 128), F32),
            pltpu.SemaphoreType.DMA((16,)),
            pltpu.SemaphoreType.DMA((copies,)),
            pltpu.SemaphoreType.DMA((copies,)),
        ],
        compiler_params=pltpu.CompilerParams(
            collective_id=0, has_side_effects=True, vmem_limit_bytes=40 * 1024 * 1024
        ),
        name="solve",
    )(vertical, band, offsets, shifts, classes, source_field, helm_diag)


def iterate(departure, helm_diag, vertical):
    def one(_, carry):
        answer, residual, direction, norm = carry
        applied = operate(direction, helm_diag, vertical)
        rate = norm / lax.psum(jnp.sum(direction * applied), ("lon", "lat"))
        answer = answer + rate * direction
        residual = residual - rate * applied
        follow = squares(residual)
        return answer, residual, residual + follow / norm * direction, follow

    start = (jnp.zeros_like(departure), departure, departure, squares(departure))
    answer, _, direction, norm = lax.fori_loop(0, ITERS - 1, one, start)
    applied = operate(direction, helm_diag, vertical)
    return answer + norm / lax.psum(jnp.sum(direction * applied), ("lon", "lat")) * direction


def body(source_field, helm_diag, vertical, cubic_band, lat_offset, zonal_shift, row_class):
    departure, quick, worst = solve(
        source_field, helm_diag, vertical, cubic_band.T, lat_offset, zonal_shift, row_class,
        lax.axis_size("lon"), lax.axis_size("lat"),
    )
    answer = lax.cond(
        worst[0, 0] < LIMIT, lambda *_: quick, iterate, departure, helm_diag, vertical
    )
    return (departure, answer)


def solution(mesh):
    return jax.shard_map(
        body,
        mesh=mesh,
        in_specs=(
            P(None, "lat", "lon"),
            P(None, "lat", "lon"),
            P(),
            P(),
            P("lat"),
            P("lat"),
            P("lat"),
        ),
        out_specs=(P(None, "lat", "lon"), P(None, "lat", "lon")),
        check_vma=False,
    )
```

```python
import itertools
from functools import partial

import jax
import jax.numpy as jnp
from jax import lax
from jax.experimental import pallas as pl
from jax.experimental.pallas import tpu as pltpu
from jax.sharding import PartitionSpec as P

DRIFT = 8
ITERS = 8


def with_halo(cells, sides, width, closed):
    for axis, dim in sides:
        count = lax.axis_size(axis)
        ends = count if closed else count - 1
        head = lax.slice_in_dim(cells, 0, width, axis=dim)
        tail = lax.slice_in_dim(cells, cells.shape[dim] - width, cells.shape[dim], axis=dim)
        cells = jnp.concatenate(
            [
                lax.ppermute(tail, axis, [(i, (i + 1) % count) for i in range(ends)]),
                cells,
                lax.ppermute(head, axis, [((i + 1) % count, i) for i in range(ends)]),
            ],
            axis=dim,
        )
    return cells


def local_terms(values, helm_diag, vertical, east_west, north_south):
    stacked = jnp.pad(values, ((1, 1), (0, 0), (0, 0)))
    up_down = stacked[2:] + stacked[:-2]
    coupling = vertical[:, None, None]
    return (
        (4.0 + 2.0 * coupling + helm_diag) * values - (east_west + north_south) - coupling * up_down
    )


def operate(values, helm_diag, vertical):
    zonal = with_halo(values, (("lon", 2),), 1, True)
    meridional = with_halo(values, (("lat", 1),), 1, False)
    east_west = zonal[:, :, 2:] + zonal[:, :, :-2]
    north_south = meridional[:, 2:, :] + meridional[:, :-2, :]
    return local_terms(values, helm_diag, vertical, east_west, north_south)


def squares(residual):
    return lax.psum(jnp.sum(residual * residual), ("lon", "lat"))


MESH = pl.DeviceIdType.MESH
F32 = jnp.float32
STEPS = 8
SIZES = {"zl": 2, "x": 4, "zh": 2, "y": 4, "c": 2}
PLANE, REST = ("x", "y"), ("zl", "zh", "c")
LIMIT = 1.5e4
ROWS, COLS = 48, 512
XR, TOP, TILES = 80, 16, 5


def iota(shape, dim):
    return lax.broadcasted_iota(jnp.int32, shape, dim)


class Remote:
    def __init__(self, send_sems, recv_sems):
        self.send_sems, self.recv_sems, self.used, self.all = send_sems, recv_sems, 0, []

    def start(self, src, dst, lon, lat):
        copy = pltpu.make_async_remote_copy(
            src_ref=src,
            dst_ref=dst,
            send_sem=self.send_sems.at[self.used],
            recv_sem=self.recv_sems.at[self.used],
            device_id=(lon, lat),
            device_id_type=MESH,
        )
        self.used += 1
        copy.start()
        self.all.append(copy)
        return copy

    def settle(self, copies):
        for copy in copies:
            copy.wait_send()
            self.all = [other for other in self.all if other is not copy]

    def drain(self):
        for copy in self.all:
            copy.wait_send()


def coefficients(gram, steps, middle, half):
    def apply(vec):
        out = {}

        def add(i, x):
            out[i] = out[i] + x if i in out else x

        for i, x in vec.items():
            add(i, x * middle)
            if i == 0:
                add(1, x * half)
            else:
                add(i + 1, x * (0.5 * half))
                add(i - 1, x * (0.5 * half))
        return out

    def form(a, b):
        total = size = None
        for i, x in a.items():
            inner = bulk = None
            for j, y in b.items():
                term = gram(i, j) * y
                inner = term if inner is None else inner + term
                bulk = jnp.abs(term) if bulk is None else bulk + jnp.abs(term)
            total = x * inner if total is None else total + x * inner
            size = jnp.abs(x) * bulk if size is None else size + jnp.abs(x) * bulk
        return total, size / jnp.abs(total)

    def plus(a, scale, b):
        return {i: a[i] + scale * b[i] if i in a and i in b else (a[i] if i in a else scale * b[i]) for i in {**a, **b}}

    one = jnp.ones((8, 128), F32)
    direction, residual, answer = {0: one}, {0: one}, {}
    norm, worst = gram(0, 0), one
    for count in range(steps):
        applied = apply(direction)
        slope, size = form(direction, applied)
        worst = jnp.maximum(worst, size)
        rate = norm / slope
        answer = plus(answer, rate, direction)
        if count < steps - 1:
            residual = plus(residual, -rate, applied)
            follow, size = form(residual, residual)
            worst = jnp.maximum(worst, size)
            direction = plus(residual, follow / norm, direction)
            norm = follow
    return answer, worst


class Gram:
    def __init__(self, row, pairs):
        self.row, self.place, self.cache = row, {p: i for i, p in enumerate(pairs)}, {}

    def __call__(self, i, j):
        pair = (min(i, j), max(i, j))
        if pair not in self.cache:
            at = self.place[pair]
            self.cache[pair] = jnp.broadcast_to(self.row[:, at : at + 1], (8, 128))
        return self.cache[pair]


def solve_kernel(
    nlon, nlat, vertical, band, offsets, shifts, classes, source, helm, dep, out, flag,
    inner, upper, lower, picked, gathered, circle, banded, returned,
    vs, dd, lon_in, packs, stage, slot_plane, slot_rest, local_sems, send_sems, recv_sems,
):
    lon, lat = lax.axis_index("lon"), lax.axis_index("lat")

    def east(k):
        return lax.rem(lon + (k + nlon), nlon)

    def north(k):
        return lax.rem(lat + (k + nlat), nlat)

    here = {"zl": lon // 4, "x": lax.rem(lon, 4), "zh": lat // 8, "y": lax.rem(lat // 2, 4), "c": lax.rem(lat, 2)}

    def place_of(moves):
        spot = {a: lax.rem(v + moves.get(a, 0), SIZES[a]) for a, v in here.items()}
        return spot["zl"] * 4 + spot["x"], spot["zh"] * 8 + spot["y"] * 2 + spot["c"]

    def partners(axes):
        moves = [dict(zip(axes, m)) for m in itertools.product(*[range(SIZES[a]) for a in axes]) if any(m)]
        far = {"c": 0, "zl": 1, "zh": 2}
        return sorted(moves, key=lambda m: -sum(far.get(a, 1) * min(v, SIZES[a] - v) for a, v in m.items()))

    barrier = pltpu.get_barrier_semaphore()
    greet = [(east(k), lat) for k in range(1, nlon)]
    greet += [(lon, north(1)), (lon, north(-1))]
    greet += [(east(a), north(b)) for a in (-1, 1) for b in (-1, 1)]
    greet += [place_of(m) for m in partners(PLANE) if m["y"]]
    greet += [place_of(m) for m in partners(REST) if m["zh"] or m["c"]]
    for peer in greet:
        pl.semaphore_signal(barrier, inc=1, device_id=peer, device_id_type=MESH)
    greeted = len(greet)
    own = [
        pltpu.make_async_copy(
            source.at[:, pl.ds(start, size), pl.ds(128 * b, 128)],
            into.at[:, b, pl.ds(at, size), :],
            local_sems.at[4 * n + b],
        )
        for n, (into, start, at, size) in enumerate(
            [(inner, 0, 0, ROWS), (upper, 0, DRIFT, 2 * DRIFT), (lower, ROWS - 2 * DRIFT, 0, 2 * DRIFT)]
        )
        for b in range(4)
    ]
    own_diag = [
        pltpu.make_async_copy(
            helm.at[:, :, pl.ds(128 * b, 128)], dd.at[:, b, pl.ds(TOP, ROWS), :], local_sems.at[12 + b]
        )
        for b in range(4)
    ]
    for copy in own + own_diag:
        copy.start()

    remote = Remote(send_sems, recv_sems)
    lane, sub = iota((8, 128), 1), iota((8, 128), 0)
    top_ok, bottom_ok = lat > 0, lat < nlat - 1

    def clear():
        zero = jnp.zeros((8, 128), F32)

        def one(j, carry):
            for b in range(TILES):
                for t in range(XR // 8):
                    vs[j, 0, b, 8 * t : 8 * t + 8, :] = zero
                    vs[j, 5, b, 8 * t : 8 * t + 8, :] = zero
                for level in range(1, 5):
                    vs[j, level, b, 0:8, :] = zero
                    vs[j, level, b, XR - 8 : XR, :] = zero
            return carry

        lax.fori_loop(0, STEPS + 1, one, 0)
        stage[...] = jnp.zeros_like(stage)

    mean = 0.25 * ((vertical[0] + vertical[1]) + (vertical[2] + vertical[3]))
    top = 0.9 * (9.0 + 4.0 * mean)
    middle, half = 0.54 * top, 0.46 * top
    double = jnp.full((8, 128), 2.0, F32) / jnp.broadcast_to(half, (8, 128))

    def start_exchange(tile, place, which):
        for h in range(2):
            right = left = jnp.zeros((8, 128), F32)
            for i in range(12):
                here = lane // 8 == i
                level = 2 * h + i // 6
                right = jnp.where(here, pltpu.roll(tile(level, i % 6, 3), (8 * i + 8) % 128, 1), right)
                left = jnp.where(here, pltpu.roll(tile(level, i % 6, 0), 8 * i, 1), left)
            packs[which, 0, h] = right
            packs[which, 1, h] = left
        return [
            remote.start(place(TOP + ROWS - 8), place(TOP - 8), lon, north(1)),
            remote.start(place(TOP), place(TOP + ROWS), lon, north(-1)),
            remote.start(packs.at[which, 0], lon_in.at[which, 0], east(1), lat),
            remote.start(packs.at[which, 0], lon_in.at[which, 1], east(1), north(1)),
            remote.start(packs.at[which, 0], lon_in.at[which, 2], east(1), north(-1)),
            remote.start(packs.at[which, 1], lon_in.at[which, 3], east(-1), lat),
            remote.start(packs.at[which, 1], lon_in.at[which, 4], east(-1), north(1)),
            remote.start(packs.at[which, 1], lon_in.at[which, 5], east(-1), north(-1)),
        ]

    def finish_exchange(copies, put, which):
        for copy in copies:
            copy.wait_recv()
        for level in range(4):
            packed = [lon_in[which, i, level // 2] for i in range(6)]
            for t in range(-1, 7):
                i = 6 * (level % 2) + (5 if t < 0 else t if t < 6 else 0)
                side = 1 if t < 0 else 0 if t < 6 else 2
                westward = pltpu.roll(packed[side], (120 - 8 * i) % 128, 1)
                eastward = pltpu.roll(packed[3 + side], (-8 * i) % 128, 1)
                put(level, t, 4, jnp.where(lane < 64, eastward, westward))
        for missing, t in ((lat == nlat - 1, 6), (lat == 0, -1)):

            @pl.when(missing)
            def _(t=t):
                for level in range(4):
                    for b in range(5):
                        put(level, t, b, jnp.zeros((8, 128), F32))

    def b_tile(level, t, b):
        return vs[0, level + 1, b, TOP + 8 * t : TOP + 8 * t + 8, :]

    def b_put(level, t, b, value):
        vs[0, level + 1, b, TOP + 8 * t : TOP + 8 * t + 8, :] = value

    def b_rows(at):
        return vs.at[0, pl.ds(1, 4), pl.ds(0, 4), pl.ds(at, 8), :]

    def diag_tile(level, t, b):
        return dd[level, b, TOP + 8 * t : TOP + 8 * t + 8, :]

    def diag_put(level, t, b, value):
        dd[level, b, TOP + 8 * t : TOP + 8 * t + 8, :] = value

    def diag_rows(at):
        return dd.at[:, pl.ds(0, 4), pl.ds(at, 8), :]

    def shift_diag():
        def one(level, carry):
            add = 4.0 + 2.0 * vertical[level] - middle
            for b in range(TILES):
                for t in range(-1, 7):
                    value = double * (diag_tile(level, t, b) + add)
                    if t in (-1, 6):
                        value = jnp.where(top_ok if t < 0 else bottom_ok, value, 0.0)
                    diag_put(level, t, b, value)
            return carry

        lax.fori_loop(0, 4, one, 0)

    def chebyshev(src, before, dst):
        last = dst == STEPS

        def one(level, carry):
            results = []
            tiles = range(0, 6) if last else range(-1, 7)
            at = lambda j, l, t, b: vs[j, l, b, TOP + 8 * t : TOP + 8 * t + 8, :]
            for t in tiles:
                scale = double
                if t == -1:
                    scale = jnp.where(top_ok, double, 0.0)
                if t == 6:
                    scale = jnp.where(bottom_ok, double, 0.0)
                mids = [at(src, level + 1, t, b) for b in range(TILES)]
                for b in range(4 if last else TILES):
                    mid = mids[b]
                    sides = pltpu.roll(jnp.where(lane == 127, mids[b - 1], mid), 1, 1)
                    sides = sides + pltpu.roll(jnp.where(lane == 0, mids[(b + 1) % TILES], mid), 127, 1)
                    above, below = at(src, level + 1, t - 1, b), at(src, level + 1, t + 1, b)
                    sides = sides + pltpu.roll(jnp.where(sub == 7, above, mid), 1, 0)
                    sides = sides + pltpu.roll(jnp.where(sub == 0, below, mid), 7, 0)
                    stack = at(src, level, t, b) + at(src, level + 2, t, b)
                    value = dd[level, b, TOP + 8 * t : TOP + 8 * t + 8, :] * mid - scale * (sides + vertical[level] * stack)
                    if before is None:
                        value = 0.5 * value
                    else:
                        value = value - at(before, level + 1, t, b)
                    results.append((b, t, value))
                    if len(results) == 20:
                        for bb, tt, v in results:
                            vs[dst, level + 1, bb, TOP + 8 * tt : TOP + 8 * tt + 8, :] = v
                        results = []
            for bb, tt, v in results:
                vs[dst, level + 1, bb, TOP + 8 * tt : TOP + 8 * tt + 8, :] = v
            return carry

        for level in range(4):
            one(level, 0)

    def all_reduce(value):
        for axes, slot in ((PLANE, slot_plane), (REST, slot_rest)):
            mine = 0
            for axis in axes:
                mine = mine * SIZES[axis] + here[axis]
            slot[mine] = value
            copies = [remote.start(slot.at[mine], slot.at[mine], *place_of(m)) for m in partners(axes)]
            for copy in copies:
                copy.wait_recv()
            value = slot[0]
            for i in range(1, slot.shape[0]):
                value = value + slot[i]
        return value

    def gram():
        count = STEPS + 1
        pairs = [(i, j) for i in range(count) for j in range(i, count) if i < STEPS]

        def one(t, sums):
            level, r = t // 6, (t % 6) * 8
            sums = list(sums)
            for b in range(4):
                tiles = [vs[i, level + 1, b, pl.ds(r + TOP, 8), :] for i in range(count)]
                for n, (i, j) in enumerate(pairs):
                    sums[n] = sums[n] + tiles[i] * tiles[j]
            return tuple(sums)

        sums = tuple(jnp.zeros((8, 128), F32) for _ in pairs)
        for t in range(24):
            sums = one(t, sums)
        for n, part in enumerate(sums):
            stage[n : n + 1, :] = jnp.sum(part, axis=0, keepdims=True)
        row = lax.dot_general(
            jnp.ones((8, 128), F32), stage[...], (((1,), (1,)), ((), ())),
            precision=lax.Precision.HIGHEST, preferred_element_type=F32,
        )
        return Gram(all_reduce(row), pairs)

    def combine(coef):
        def one(t, carry):
            level, r = t // 6, (t % 6) * 8
            for b in range(4):
                value = None
                for i, x in coef.items():
                    term = x * vs[i, level + 1, b, pl.ds(r + TOP, 8), :]
                    value = term if value is None else value + term
                out[level, pl.ds(r, 8), 128 * b : 128 * b + 128] = value
            return carry

        for t in range(24):
            one(t, 0)

    for copy in own[0:4]:
        copy.wait()

    def pick(j, part, write):
        from_, first, rows = [(inner, 0, ROWS), (upper, -DRIFT, 3 * DRIFT), (lower, ROWS - 2 * DRIFT, 3 * DRIFT)][part]
        row = jnp.clip(j + offsets[j] - first, 0, rows - 1)
        for level in range(4):
            for b in range(4):
                write(4 * level + b, from_[level, b, pl.ds(row, 1), :])

    def pick_rows(c, k, rows, at, parts):
        for n, (j, part) in enumerate(zip(rows, parts)):

            def write(place, value, n=n):
                if k == nlon:
                    gathered[c, at + 16 * n + place : at + 16 * n + place + 1, :] = value
                else:
                    picked[k - 1, at + 16 * n + place : at + 16 * n + place + 1, :] = value

            pick(j, part, write)

    def middle_rows(c):
        return [DRIFT + 4 * c + q for q in range(4)]

    def edge_rows(c):
        return [c, ROWS - DRIFT + c]

    for k in range(1, nlon + 1):
        pick_rows(east(k % nlon), k, middle_rows(east(k % nlon)), 0, (0, 0, 0, 0))
    pl.semaphore_wait(barrier, greeted)
    beside = [
        remote.start(inner.at[:, :, pl.ds(ROWS - DRIFT, DRIFT), :], upper.at[:, :, pl.ds(0, DRIFT), :], lon, north(1)),
        remote.start(inner.at[:, :, pl.ds(0, DRIFT), :], lower.at[:, :, pl.ds(2 * DRIFT, DRIFT), :], lon, north(-1)),
    ]

    def send_picked(start, size):
        return [
            remote.start(
                picked.at[k - 1, pl.ds(start, size)], gathered.at[lon, pl.ds(start, size)], east(k), lat
            )
            for k in range(1, nlon)
        ]

    sent_middle = send_picked(0, 64)
    for copy in own_diag:
        copy.wait()
    diag_waiting = start_exchange(diag_tile, diag_rows, 0)
    clear()
    for copy in own[4:]:
        copy.wait()
    for copy in beside:
        copy.wait_recv()
    for k in range(1, nlon + 1):
        pick_rows(east(k % nlon), k, edge_rows(east(k % nlon)), 64, (1, 2))
    sent_edge = send_picked(64, 32)

    finish_exchange(diag_waiting, diag_put, 0)
    remote.settle(diag_waiting)

    shift_diag()

    first_half = sub < 4
    lanes = iota((32, 128), 1)

    def band_rows(pp, j):
        low = pl.multiple_of(pp * 8, 8)
        for m in range(4):
            a, b = gathered[2 * m, pl.ds(low, 8), :], gathered[2 * m + 1, pl.ds(low, 8), :]
            pair = (
                jnp.where(first_half, a, pltpu.roll(b, 4, 0)),
                jnp.where(first_half, pltpu.roll(a, 4, 0), b),
            )
            for n in range(2):
                circle[2 * pp + n, 8 + 8 * m : 16 + 8 * m, :] = pair[n]
                circle[2 * pp + n, 40 + 8 * m : 48 + 8 * m, :] = pair[n]
                if m == 3:
                    circle[2 * pp + n, 0:8, :] = pair[n]
                if m == 0:
                    circle[2 * pp + n, 72:80, :] = pair[n]
        start = 8 + lax.rem(64 - shifts[j], 32)
        weight = [band[t, classes[j]] for t in range(4)]
        outs = []
        for n in range(2):
            now = circle[2 * pp + n, pl.ds(start, 32), :]
            before = circle[2 * pp + n, pl.ds(start - 1, 32), :]
            after = circle[2 * pp + n, pl.ds(start + 1, 32), :]
            total = weight[0] * pltpu.roll(jnp.where(lanes == 127, before, now), 1, 1)
            total = total + weight[1] * now
            total = total + weight[2] * pltpu.roll(jnp.where(lanes == 0, after, now), 127, 1)
            total = total + weight[3] * pltpu.roll(jnp.where(lanes < 2, after, now), 126, 1)
            outs.append(total)
        for m in range(4):
            a, b = outs[0][8 * m : 8 * m + 8], outs[1][8 * m : 8 * m + 8]
            banded[2 * m, pl.ds(low, 8), :] = jnp.where(first_half, a, pltpu.roll(b, 4, 0))
            banded[2 * m + 1, pl.ds(low, 8), :] = jnp.where(first_half, pltpu.roll(a, 4, 0), b)

    def middle_band(pp, carry):
        band_rows(pp, DRIFT + 4 * lon + pp // 2)
        return carry

    def edge_band(pp, carry):
        band_rows(pp, lon + (ROWS - DRIFT) * ((pp - 8) // 2))
        return carry

    def send_banded(start, size):
        here = pl.multiple_of(lon * 96 + start, 8)
        copies = [
            remote.start(banded.at[east(k), pl.ds(start, size)], returned.at[pl.ds(here, size)], east(k), lat)
            for k in range(1, nlon)
        ]
        returned[pl.ds(here, size), :] = banded[lon, pl.ds(start, size), :]
        return copies

    for copy in sent_middle:
        copy.wait_recv()
    lax.fori_loop(0, 8, middle_band, 0)
    back_middle = send_banded(0, 64)
    for copy in sent_edge:
        copy.wait_recv()
    lax.fori_loop(8, 12, edge_band, 0)
    back_edge = send_banded(64, 32)
    for copy in back_middle + back_edge:
        copy.wait_recv()
    for level in range(4):
        for b in range(4):
            place = 4 * level + b
            for t in range(6):
                if t in (0, 5):
                    tile = returned[pl.ds(64 + 16 * (t // 5) + place, 8, stride=96), :]
                else:
                    tile = jnp.concatenate(
                        [returned[pl.ds((2 * t - 2 + n) * 96 + place, 4, stride=16), :] for n in range(2)], 0
                    )
                b_put(level, t, b, tile)
                dep[level, 8 * t : 8 * t + 8, 128 * b : 128 * b + 128] = tile
    waiting = start_exchange(b_tile, b_rows, 1)
    finish_exchange(waiting, b_put, 1)
    for k in range(1, STEPS + 1):
        chebyshev(k - 1, None if k == 1 else k - 2, k)
    answer, worst = coefficients(gram(), STEPS, middle, half)
    combine(answer)
    flag[0, 0] = jnp.max(worst)
    remote.drain()


def solve(source_field, helm_diag, vertical, band, offsets, shifts, classes, nlon, nlat):
    copies = 2 + 4 * (nlon - 1) + 2 * 8 + 15 + 7
    vmem = pl.BlockSpec(memory_space=pltpu.VMEM)
    smem = pl.BlockSpec(memory_space=pltpu.SMEM)
    far = pl.BlockSpec(memory_space=pltpu.HBM)
    field = jax.ShapeDtypeStruct(source_field.shape, F32)
    return pl.pallas_call(
        partial(solve_kernel, nlon, nlat),
        out_shape=(field, field, jax.ShapeDtypeStruct((1, 1), F32)),
        in_specs=[smem] * 5 + [far, far],
        out_specs=(vmem, vmem, smem),
        scratch_shapes=[
            pltpu.VMEM((4, 4, ROWS, 128), F32),
            pltpu.VMEM((4, 4, 3 * DRIFT, 128), F32),
            pltpu.VMEM((4, 4, 3 * DRIFT, 128), F32),
            pltpu.VMEM((nlon - 1, 96, 128), F32),
            pltpu.VMEM((nlon, 96, 128), F32),
            pltpu.VMEM((24, 80, 128), F32),
            pltpu.VMEM((nlon, 96, 128), F32),
            pltpu.VMEM((nlon * 96, 128), F32),
            pltpu.VMEM((STEPS + 1, 6, TILES, XR, 128), F32),
            pltpu.VMEM((4, TILES, XR, 128), F32),
            pltpu.VMEM((2, 6, 2, 8, 128), F32),
            pltpu.VMEM((2, 2, 2, 8, 128), F32),
            pltpu.VMEM((128, 128), F32),
            pltpu.VMEM((16, 8, 128), F32),
            pltpu.VMEM((8, 8, 128), F32),
            pltpu.SemaphoreType.DMA((16,)),
            pltpu.SemaphoreType.DMA((copies,)),
            pltpu.SemaphoreType.DMA((copies,)),
        ],
        compiler_params=pltpu.CompilerParams(
            collective_id=0, has_side_effects=True, vmem_limit_bytes=62 * 1024 * 1024
        ),
        name="solve",
    )(vertical, band, offsets, shifts, classes, source_field, helm_diag)


def iterate(departure, helm_diag, vertical):
    def one(_, carry):
        answer, residual, direction, norm = carry
        applied = operate(direction, helm_diag, vertical)
        rate = norm / lax.psum(jnp.sum(direction * applied), ("lon", "lat"))
        answer = answer + rate * direction
        residual = residual - rate * applied
        follow = squares(residual)
        return answer, residual, residual + follow / norm * direction, follow

    start = (jnp.zeros_like(departure), departure, departure, squares(departure))
    answer, _, direction, norm = lax.fori_loop(0, ITERS - 1, one, start)
    applied = operate(direction, helm_diag, vertical)
    return answer + norm / lax.psum(jnp.sum(direction * applied), ("lon", "lat")) * direction


def body(source_field, helm_diag, vertical, cubic_band, lat_offset, zonal_shift, row_class):
    departure, quick, worst = solve(
        source_field, helm_diag, vertical, cubic_band.T, lat_offset, zonal_shift, row_class,
        lax.axis_size("lon"), lax.axis_size("lat"),
    )
    answer = lax.cond(
        worst[0, 0] < LIMIT, lambda *_: quick, iterate, departure, helm_diag, vertical
    )
    return (departure, answer)


def solution(mesh):
    return jax.shard_map(
        body,
        mesh=mesh,
        in_specs=(
            P(None, "lat", "lon"),
            P(None, "lat", "lon"),
            P(),
            P(),
            P("lat"),
            P("lat"),
            P("lat"),
        ),
        out_specs=(P(None, "lat", "lon"), P(None, "lat", "lon")),
        check_vma=False,
    )
```

```python
import itertools
from functools import partial

import jax
import jax.numpy as jnp
from jax import lax
from jax.experimental import pallas as pl
from jax.experimental.pallas import tpu as pltpu
from jax.sharding import PartitionSpec as P

DRIFT = 8
ITERS = 8


def with_halo(cells, sides, width, closed):
    for axis, dim in sides:
        count = lax.axis_size(axis)
        ends = count if closed else count - 1
        head = lax.slice_in_dim(cells, 0, width, axis=dim)
        tail = lax.slice_in_dim(cells, cells.shape[dim] - width, cells.shape[dim], axis=dim)
        cells = jnp.concatenate(
            [
                lax.ppermute(tail, axis, [(i, (i + 1) % count) for i in range(ends)]),
                cells,
                lax.ppermute(head, axis, [((i + 1) % count, i) for i in range(ends)]),
            ],
            axis=dim,
        )
    return cells


def local_terms(values, helm_diag, vertical, east_west, north_south):
    stacked = jnp.pad(values, ((1, 1), (0, 0), (0, 0)))
    up_down = stacked[2:] + stacked[:-2]
    coupling = vertical[:, None, None]
    return (
        (4.0 + 2.0 * coupling + helm_diag) * values - (east_west + north_south) - coupling * up_down
    )


def operate(values, helm_diag, vertical):
    zonal = with_halo(values, (("lon", 2),), 1, True)
    meridional = with_halo(values, (("lat", 1),), 1, False)
    east_west = zonal[:, :, 2:] + zonal[:, :, :-2]
    north_south = meridional[:, 2:, :] + meridional[:, :-2, :]
    return local_terms(values, helm_diag, vertical, east_west, north_south)


def squares(residual):
    return lax.psum(jnp.sum(residual * residual), ("lon", "lat"))


MESH = pl.DeviceIdType.MESH
F32 = jnp.float32
STEPS = 8
SIZES = {"zl": 2, "x": 4, "zh": 2, "y": 4, "c": 2}
PLANE, REST = ("x", "y"), ("zl", "zh", "c")
PART = 120
FAR_FIRST = [6, 2, 5, 7, 3, 1, 4]
LIMIT = 1.5e4
ROWS, COLS = 48, 512
XR, TOP, TILES = 80, 16, 5


def iota(shape, dim):
    return lax.broadcasted_iota(jnp.int32, shape, dim)


class Remote:
    def __init__(self, send_sems, recv_sems):
        self.send_sems, self.recv_sems, self.used, self.all = send_sems, recv_sems, 0, []

    def start(self, src, dst, lon, lat):
        copy = pltpu.make_async_remote_copy(
            src_ref=src,
            dst_ref=dst,
            send_sem=self.send_sems.at[self.used],
            recv_sem=self.recv_sems.at[self.used],
            device_id=(lon, lat),
            device_id_type=MESH,
        )
        self.used += 1
        copy.start()
        self.all.append(copy)
        return copy

    def settle(self, copies):
        for copy in copies:
            copy.wait_send()
            self.all = [other for other in self.all if other is not copy]

    def drain(self):
        for copy in self.all:
            copy.wait_send()


def coefficients(gram, steps, middle, half):
    def apply(vec):
        out = {}

        def add(i, x):
            out[i] = out[i] + x if i in out else x

        for i, x in vec.items():
            add(i, x * middle)
            if i == 0:
                add(1, x * half)
            else:
                add(i + 1, x * (0.5 * half))
                add(i - 1, x * (0.5 * half))
        return out

    def form(a, b):
        total = size = None
        for i, x in a.items():
            inner = bulk = None
            for j, y in b.items():
                term = gram(i, j) * y
                inner = term if inner is None else inner + term
                bulk = jnp.abs(term) if bulk is None else bulk + jnp.abs(term)
            total = x * inner if total is None else total + x * inner
            size = jnp.abs(x) * bulk if size is None else size + jnp.abs(x) * bulk
        return total, size / jnp.abs(total)

    def plus(a, scale, b):
        return {i: a[i] + scale * b[i] if i in a and i in b else (a[i] if i in a else scale * b[i]) for i in {**a, **b}}

    one = jnp.ones((8, 128), F32)
    direction, residual, answer = {0: one}, {0: one}, {}
    norm, worst = gram(0, 0), one
    for count in range(steps):
        applied = apply(direction)
        slope, size = form(direction, applied)
        worst = jnp.maximum(worst, size)
        rate = norm / slope
        answer = plus(answer, rate, direction)
        if count < steps - 1:
            residual = plus(residual, -rate, applied)
            follow, size = form(residual, residual)
            worst = jnp.maximum(worst, size)
            direction = plus(residual, follow / norm, direction)
            norm = follow
    return answer, worst


class Gram:
    def __init__(self, row, pairs):
        self.row, self.place, self.cache = row, {p: i for i, p in enumerate(pairs)}, {}

    def __call__(self, i, j):
        pair = (min(i, j), max(i, j))
        if pair not in self.cache:
            at = self.place[pair]
            self.cache[pair] = jnp.broadcast_to(self.row[:, at : at + 1], (8, 128))
        return self.cache[pair]


def solve_kernel(
    nlon, nlat, vertical, band, offsets, shifts, classes, source, helm, dep, out, flag,
    inner, upper, lower, picked, gathered, circle, looped, banded, returned, beyond,
    vs, dd, lon_in, packs, stage, slot_plane, slot_rest, local_sems, send_sems, recv_sems,
):
    lon, lat = lax.axis_index("lon"), lax.axis_index("lat")

    def east(k):
        return lax.rem(lon + (k + nlon), nlon)

    def north(k):
        return lax.rem(lat + (k + nlat), nlat)

    here = {"zl": lon // 4, "x": lax.rem(lon, 4), "zh": lat // 8, "y": lax.rem(lat // 2, 4), "c": lax.rem(lat, 2)}

    def place_of(moves):
        spot = {a: lax.rem(v + moves.get(a, 0), SIZES[a]) for a, v in here.items()}
        return spot["zl"] * 4 + spot["x"], spot["zh"] * 8 + spot["y"] * 2 + spot["c"]

    def partners(axes):
        moves = [dict(zip(axes, m)) for m in itertools.product(*[range(SIZES[a]) for a in axes]) if any(m)]
        far = {"c": 0, "zl": 1, "zh": 2}
        return sorted(moves, key=lambda m: -sum(far.get(a, 1) * min(v, SIZES[a] - v) for a, v in m.items()))

    barrier = pltpu.get_barrier_semaphore()
    greet = [(east(k), lat) for k in range(1, nlon)]
    greet += [(east(k), north(b)) for k in range(nlon) for b in (-1, 1)]
    greet += [place_of(m) for m in partners(PLANE) if m["y"]]
    greet += [place_of(m) for m in partners(REST) if m["zh"] or m["c"]]
    for peer in greet:
        pl.semaphore_signal(barrier, inc=1, device_id=peer, device_id_type=MESH)
    greeted = len(greet)
    own = [
        pltpu.make_async_copy(
            source.at[:, pl.ds(start, size), pl.ds(128 * b, 128)],
            into.at[:, b, pl.ds(at, size), :],
            local_sems.at[4 * n + b],
        )
        for n, (into, start, at, size) in enumerate(
            [(inner, 0, 0, ROWS), (upper, 0, DRIFT, 2 * DRIFT), (lower, ROWS - 2 * DRIFT, 0, 2 * DRIFT)]
        )
        for b in range(4)
    ]
    own_diag = [
        pltpu.make_async_copy(
            helm.at[:, :, pl.ds(128 * b, 128)], dd.at[:, b, pl.ds(TOP, ROWS), :], local_sems.at[12 + b]
        )
        for b in range(4)
    ]
    for copy in own + own_diag:
        copy.start()

    remote = Remote(send_sems, recv_sems)
    lane, sub = iota((8, 128), 1), iota((8, 128), 0)
    top_ok, bottom_ok = lat > 0, lat < nlat - 1

    def clear():
        zero = jnp.zeros((8, 128), F32)

        def one(j, carry):
            for b in range(TILES):
                for t in range(XR // 8):
                    vs[j, 0, b, 8 * t : 8 * t + 8, :] = zero
                    vs[j, 5, b, 8 * t : 8 * t + 8, :] = zero
                for level in range(1, 5):
                    vs[j, level, b, 0:8, :] = zero
                    vs[j, level, b, XR - 8 : XR, :] = zero
            return carry

        lax.fori_loop(0, STEPS + 1, one, 0)
        stage[...] = jnp.zeros_like(stage)

    mean = 0.25 * ((vertical[0] + vertical[1]) + (vertical[2] + vertical[3]))
    top = 0.9 * (9.0 + 4.0 * mean)
    middle, half = 0.54 * top, 0.46 * top
    double = jnp.full((8, 128), 2.0, F32) / jnp.broadcast_to(half, (8, 128))

    def start_exchange(tile, place, which):
        for h in range(2):
            right = left = jnp.zeros((8, 128), F32)
            for i in range(12):
                here = lane // 8 == i
                level = 2 * h + i // 6
                right = jnp.where(here, pltpu.roll(tile(level, i % 6, 3), (8 * i + 8) % 128, 1), right)
                left = jnp.where(here, pltpu.roll(tile(level, i % 6, 0), 8 * i, 1), left)
            packs[which, 0, h] = right
            packs[which, 1, h] = left
        return [
            remote.start(place(TOP + ROWS - 8), place(TOP - 8), lon, north(1)),
            remote.start(place(TOP), place(TOP + ROWS), lon, north(-1)),
            remote.start(packs.at[which, 0], lon_in.at[which, 0], east(1), lat),
            remote.start(packs.at[which, 0], lon_in.at[which, 1], east(1), north(1)),
            remote.start(packs.at[which, 0], lon_in.at[which, 2], east(1), north(-1)),
            remote.start(packs.at[which, 1], lon_in.at[which, 3], east(-1), lat),
            remote.start(packs.at[which, 1], lon_in.at[which, 4], east(-1), north(1)),
            remote.start(packs.at[which, 1], lon_in.at[which, 5], east(-1), north(-1)),
        ]

    def finish_exchange(copies, put, which):
        for copy in copies:
            copy.wait_recv()
        for level in range(4):
            packed = [lon_in[which, i, level // 2] for i in range(6)]
            for t in range(-1, 7):
                i = 6 * (level % 2) + (5 if t < 0 else t if t < 6 else 0)
                side = 1 if t < 0 else 0 if t < 6 else 2
                westward = pltpu.roll(packed[side], (120 - 8 * i) % 128, 1)
                eastward = pltpu.roll(packed[3 + side], (-8 * i) % 128, 1)
                put(level, t, 4, jnp.where(lane < 64, eastward, westward))
        for missing, t in ((lat == nlat - 1, 6), (lat == 0, -1)):

            @pl.when(missing)
            def _(t=t):
                for level in range(4):
                    for b in range(5):
                        put(level, t, b, jnp.zeros((8, 128), F32))

    def b_put(level, t, b, value):
        vs[0, level + 1, b, TOP + 8 * t : TOP + 8 * t + 8, :] = value

    def diag_tile(level, t, b):
        return dd[level, b, TOP + 8 * t : TOP + 8 * t + 8, :]

    def diag_put(level, t, b, value):
        dd[level, b, TOP + 8 * t : TOP + 8 * t + 8, :] = value

    def diag_rows(at):
        return dd.at[:, pl.ds(0, 4), pl.ds(at, 8), :]

    def shift_diag():
        def one(level, carry):
            add = 4.0 + 2.0 * vertical[level] - middle
            for b in range(TILES):
                for t in range(-1, 7):
                    value = double * (diag_tile(level, t, b) + add)
                    if t in (-1, 6):
                        value = jnp.where(top_ok if t < 0 else bottom_ok, value, 0.0)
                    diag_put(level, t, b, value)
            return carry

        lax.fori_loop(0, 4, one, 0)

    def chebyshev(src, before, dst):
        last = dst == STEPS

        def one(level, carry):
            results = []
            tiles = range(0, 6) if last else range(-1, 7)
            at = lambda j, l, t, b: vs[j, l, b, TOP + 8 * t : TOP + 8 * t + 8, :]
            for t in tiles:
                scale = double
                if t == -1:
                    scale = jnp.where(top_ok, double, 0.0)
                if t == 6:
                    scale = jnp.where(bottom_ok, double, 0.0)
                mids = [at(src, level + 1, t, b) for b in range(TILES)]
                for b in range(4 if last else TILES):
                    mid = mids[b]
                    sides = pltpu.roll(jnp.where(lane == 127, mids[b - 1], mid), 1, 1)
                    sides = sides + pltpu.roll(jnp.where(lane == 0, mids[(b + 1) % TILES], mid), 127, 1)
                    above, below = at(src, level + 1, t - 1, b), at(src, level + 1, t + 1, b)
                    sides = sides + pltpu.roll(jnp.where(sub == 7, above, mid), 1, 0)
                    sides = sides + pltpu.roll(jnp.where(sub == 0, below, mid), 7, 0)
                    stack = at(src, level, t, b) + at(src, level + 2, t, b)
                    value = dd[level, b, TOP + 8 * t : TOP + 8 * t + 8, :] * mid - scale * (sides + vertical[level] * stack)
                    if before is None:
                        value = 0.5 * value
                    else:
                        value = value - at(before, level + 1, t, b)
                    results.append((b, t, value))
                    if len(results) == 20:
                        for bb, tt, v in results:
                            vs[dst, level + 1, bb, TOP + 8 * tt : TOP + 8 * tt + 8, :] = v
                        results = []
            for bb, tt, v in results:
                vs[dst, level + 1, bb, TOP + 8 * tt : TOP + 8 * tt + 8, :] = v
            return carry

        for level in range(4):
            one(level, 0)

    def all_reduce(value):
        for axes, slot in ((PLANE, slot_plane), (REST, slot_rest)):
            mine = 0
            for axis in axes:
                mine = mine * SIZES[axis] + here[axis]
            slot[mine] = value
            copies = [remote.start(slot.at[mine], slot.at[mine], *place_of(m)) for m in partners(axes)]
            for copy in copies:
                copy.wait_recv()
            value = slot[0]
            for i in range(1, slot.shape[0]):
                value = value + slot[i]
        return value

    def gram():
        count = STEPS + 1
        pairs = [(i, j) for i in range(count) for j in range(i, count) if i < STEPS]

        def one(t, sums):
            level, r = t // 6, (t % 6) * 8
            sums = list(sums)
            for b in range(4):
                tiles = [vs[i, level + 1, b, pl.ds(r + TOP, 8), :] for i in range(count)]
                for n, (i, j) in enumerate(pairs):
                    sums[n] = sums[n] + tiles[i] * tiles[j]
            return tuple(sums)

        sums = tuple(jnp.zeros((8, 128), F32) for _ in pairs)
        for t in range(24):
            sums = one(t, sums)
        for n, part in enumerate(sums):
            stage[n : n + 1, :] = jnp.sum(part, axis=0, keepdims=True)
        row = lax.dot_general(
            jnp.ones((8, 128), F32), stage[...], (((1,), (1,)), ((), ())),
            precision=lax.Precision.HIGHEST, preferred_element_type=F32,
        )
        return Gram(all_reduce(row), pairs)

    def combine(coef):
        def one(t, carry):
            level, r = t // 6, (t % 6) * 8
            for b in range(4):
                value = None
                for i, x in coef.items():
                    term = x * vs[i, level + 1, b, pl.ds(r + TOP, 8), :]
                    value = term if value is None else value + term
                out[level, pl.ds(r, 8), 128 * b : 128 * b + 128] = value
            return carry

        for t in range(24):
            one(t, 0)

    for copy in own[0:4]:
        copy.wait()

    def pick(j, part, write):
        from_, first, rows = [(inner, 0, ROWS), (upper, -DRIFT, 3 * DRIFT), (lower, ROWS - 2 * DRIFT, 3 * DRIFT)][part]
        row = jnp.clip(j + offsets[j] - first, 0, rows - 1)
        for level in range(4):
            for b in range(4):
                write(4 * level + b, from_[level, b, pl.ds(row, 1), :])

    def pick_rows(c, k, rows, at, parts):
        for n, (j, part) in enumerate(zip(rows, parts)):

            def write(place, value, n=n):
                if k == nlon:
                    gathered[c, at + 16 * n + place : at + 16 * n + place + 1, :] = value
                else:
                    picked[k - 1, at + 16 * n + place : at + 16 * n + place + 1, :] = value

            pick(j, part, write)

    def middle_rows(c):
        return [DRIFT + 4 * c + q for q in range(4)]

    def edge_rows(c):
        return [c, ROWS - DRIFT + c]

    for k in range(1, nlon + 1):
        pick_rows(east(k % nlon), k, middle_rows(east(k % nlon)), 0, (0, 0, 0, 0))
    pl.semaphore_wait(barrier, greeted)
    beside = [
        remote.start(inner.at[:, :, pl.ds(ROWS - DRIFT, DRIFT), :], upper.at[:, :, pl.ds(0, DRIFT), :], lon, north(1)),
        remote.start(inner.at[:, :, pl.ds(0, DRIFT), :], lower.at[:, :, pl.ds(2 * DRIFT, DRIFT), :], lon, north(-1)),
    ]

    def send_picked(start, size):
        return [
            remote.start(
                picked.at[k - 1, pl.ds(start, size)], gathered.at[lon, pl.ds(start, size)], east(k), lat
            )
            for k in range(1, nlon)
        ]

    sent_middle = send_picked(0, 64)
    for copy in own_diag:
        copy.wait()
    diag_waiting = start_exchange(diag_tile, diag_rows, 0)
    clear()
    for copy in own[4:]:
        copy.wait()
    for copy in beside:
        copy.wait_recv()
    for k in range(1, nlon + 1):
        pick_rows(east(k % nlon), k, edge_rows(east(k % nlon)), 64, (1, 2))
    sent_edge = send_picked(64, 32)

    finish_exchange(diag_waiting, diag_put, 0)
    remote.settle(diag_waiting)

    shift_diag()

    first_half = sub < 4
    lanes = iota((32, 128), 1)

    def fill_circle(pp):
        for m in range(4):
            a, b = gathered[2 * m, 8 * pp : 8 * pp + 8, :], gathered[2 * m + 1, 8 * pp : 8 * pp + 8, :]
            pair = (
                jnp.where(first_half, a, pltpu.roll(b, 4, 0)),
                jnp.where(first_half, pltpu.roll(a, 4, 0), b),
            )
            for n in range(2):
                circle[2 * pp + n, 8 + 8 * m : 16 + 8 * m, :] = pair[n]
                circle[2 * pp + n, 40 + 8 * m : 48 + 8 * m, :] = pair[n]
                if m == 3:
                    circle[2 * pp + n, 0:8, :] = pair[n]
                if m == 0:
                    circle[2 * pp + n, 72:80, :] = pair[n]

    def band_row(row, j, at, edge_at):
        start = 8 + lax.rem(64 - shifts[j], 32)
        weight = [band[t, classes[j]] for t in range(4)]
        outs = []
        for level in range(4):
            now = circle[4 * row + level, pl.ds(start, 32), :]
            before = circle[4 * row + level, pl.ds(start - 1, 32), :]
            after = circle[4 * row + level, pl.ds(start + 1, 32), :]
            total = weight[0] * pltpu.roll(jnp.where(lanes == 127, before, now), 1, 1)
            total = total + weight[1] * now
            total = total + weight[2] * pltpu.roll(jnp.where(lanes == 0, after, now), 127, 1)
            total = total + weight[3] * pltpu.roll(jnp.where(lanes < 2, after, now), 126, 1)
            outs.append(total)
        for half in range(2):
            for m in range(4):
                a, b = outs[2 * half][8 * m : 8 * m + 8], outs[2 * half + 1][8 * m : 8 * m + 8]
                here = slice(at + 8 * half, at + 8 * half + 8)
                banded[2 * m, here, :] = jnp.where(first_half, a, pltpu.roll(b, 4, 0))
                banded[2 * m + 1, here, :] = jnp.where(first_half, pltpu.roll(a, 4, 0), b)
        edges = jnp.zeros((8, 128), F32)
        for level in range(4):
            looped[4 * row + level, 0:8, :] = outs[level][24:32]
            looped[4 * row + level, 8:40, :] = outs[level]
            looped[4 * row + level, 40:48, :] = outs[level][0:8]
        for level in range(4):
            west = looped[4 * row + level, pl.ds(7, 8, stride=4), :]
            east_ = looped[4 * row + level, pl.ds(12, 8, stride=4), :]
            both = pltpu.roll(jnp.where(lane < 64, east_, west), 16 * level + 8, 1)
            edges = jnp.where(lane // 16 == level, both, edges)
        for d in range(nlon):
            banded[d, edge_at : edge_at + 1, :] = edges[d : d + 1]

    def send_banded(start, size):
        here = pl.multiple_of(lon * PART + start, 8)
        copies = [
            remote.start(banded.at[east(k), pl.ds(start, size)], returned.at[pl.ds(here, size)], east(k), lat)
            for k in FAR_FIRST
        ]
        returned[pl.ds(here, size), :] = banded[lon, pl.ds(start, size), :]
        return copies

    def send_beyond():
        here = pl.multiple_of(lon * 24, 8)
        copies = []
        for k in FAR_FIRST + [0]:
            for start, side, step in ((96, 0, 1), (72, 1, -1)):
                copies.append(
                    remote.start(
                        banded.at[east(k), pl.ds(start, 24)], beyond.at[side, pl.ds(here, 24)], east(k), north(step)
                    )
                )
        return copies

    for copy in sent_middle:
        copy.wait_recv()
    for pp in range(8):
        fill_circle(pp)
    for q in range(4):
        band_row(q, DRIFT + 4 * lon + q, 16 * q, 64 + q)
    arriving = send_banded(0, 72)
    for copy in sent_edge:
        copy.wait_recv()
    for pp in range(8, 12):
        fill_circle(pp)
    band_row(4, lon, 72, 88)
    band_row(5, lon + ROWS - DRIFT, 96, 112)
    arriving += send_beyond() + send_banded(72, 48)
    for copy in arriving:
        copy.wait_recv()

    def row_tile(t, place, beside):
        if t in (-1, 6):
            place = 16 if beside else place
            return beyond[t // 6 if t > 0 else 0, pl.ds(place, 8, stride=24), :]
        if t in (0, 5):
            place = 16 if beside else place
            return returned[pl.ds(72 + 24 * (t // 5) + place, 8, stride=PART), :]
        both = []
        for c in (2 * t - 2, 2 * t - 1):
            if beside:
                both.append(returned[c * PART + 64 : c * PART + 68, :])
            else:
                both.append(returned[pl.ds(c * PART + place, 4, stride=16), :])
        return jnp.concatenate(both, 0)

    for t in range(-1, 7):
        outside = {-1: top_ok, 6: bottom_ok}.get(t)
        beside = row_tile(t, 0, True)
        for level in range(4):
            tiles = [row_tile(t, 4 * level + b, False) for b in range(4)]
            tiles.append(pltpu.roll(beside, (120 - 16 * level) % 128, 1))
            for b, tile in enumerate(tiles):
                if outside is not None:
                    tile = jnp.where(outside, tile, 0.0)
                elif b < 4:
                    dep[level, 8 * t : 8 * t + 8, 128 * b : 128 * b + 128] = tile
                b_put(level, t, b, tile)
    for k in range(1, STEPS + 1):
        chebyshev(k - 1, None if k == 1 else k - 2, k)
    answer, worst = coefficients(gram(), STEPS, middle, half)
    combine(answer)
    flag[0, 0] = jnp.max(worst)
    remote.drain()


def solve(source_field, helm_diag, vertical, band, offsets, shifts, classes, nlon, nlat):
    copies = 2 + 4 * (nlon - 1) + 8 + 2 * nlon + 15 + 7
    vmem = pl.BlockSpec(memory_space=pltpu.VMEM)
    smem = pl.BlockSpec(memory_space=pltpu.SMEM)
    far = pl.BlockSpec(memory_space=pltpu.HBM)
    field = jax.ShapeDtypeStruct(source_field.shape, F32)
    return pl.pallas_call(
        partial(solve_kernel, nlon, nlat),
        out_shape=(field, field, jax.ShapeDtypeStruct((1, 1), F32)),
        in_specs=[smem] * 5 + [far, far],
        out_specs=(vmem, vmem, smem),
        scratch_shapes=[
            pltpu.VMEM((4, 4, ROWS, 128), F32),
            pltpu.VMEM((4, 4, 3 * DRIFT, 128), F32),
            pltpu.VMEM((4, 4, 3 * DRIFT, 128), F32),
            pltpu.VMEM((nlon - 1, 96, 128), F32),
            pltpu.VMEM((nlon, 96, 128), F32),
            pltpu.VMEM((24, 80, 128), F32),
            pltpu.VMEM((24, 48, 128), F32),
            pltpu.VMEM((nlon, PART, 128), F32),
            pltpu.VMEM((nlon * PART, 128), F32),
            pltpu.VMEM((2, nlon * 24, 128), F32),
            pltpu.VMEM((STEPS + 1, 6, TILES, XR, 128), F32),
            pltpu.VMEM((4, TILES, XR, 128), F32),
            pltpu.VMEM((1, 6, 2, 8, 128), F32),
            pltpu.VMEM((1, 2, 2, 8, 128), F32),
            pltpu.VMEM((128, 128), F32),
            pltpu.VMEM((16, 8, 128), F32),
            pltpu.VMEM((8, 8, 128), F32),
            pltpu.SemaphoreType.DMA((16,)),
            pltpu.SemaphoreType.DMA((copies,)),
            pltpu.SemaphoreType.DMA((copies,)),
        ],
        compiler_params=pltpu.CompilerParams(
            collective_id=0, has_side_effects=True, vmem_limit_bytes=62 * 1024 * 1024
        ),
        name="solve",
    )(vertical, band, offsets, shifts, classes, source_field, helm_diag)


def iterate(departure, helm_diag, vertical):
    def one(_, carry):
        answer, residual, direction, norm = carry
        applied = operate(direction, helm_diag, vertical)
        rate = norm / lax.psum(jnp.sum(direction * applied), ("lon", "lat"))
        answer = answer + rate * direction
        residual = residual - rate * applied
        follow = squares(residual)
        return answer, residual, residual + follow / norm * direction, follow

    start = (jnp.zeros_like(departure), departure, departure, squares(departure))
    answer, _, direction, norm = lax.fori_loop(0, ITERS - 1, one, start)
    applied = operate(direction, helm_diag, vertical)
    return answer + norm / lax.psum(jnp.sum(direction * applied), ("lon", "lat")) * direction


def body(source_field, helm_diag, vertical, cubic_band, lat_offset, zonal_shift, row_class):
    departure, quick, worst = solve(
        source_field, helm_diag, vertical, cubic_band.T, lat_offset, zonal_shift, row_class,
        lax.axis_size("lon"), lax.axis_size("lat"),
    )
    answer = lax.cond(
        worst[0, 0] < LIMIT, lambda *_: quick, iterate, departure, helm_diag, vertical
    )
    return (departure, answer)


def solution(mesh):
    return jax.shard_map(
        body,
        mesh=mesh,
        in_specs=(
            P(None, "lat", "lon"),
            P(None, "lat", "lon"),
            P(),
            P(),
            P("lat"),
            P("lat"),
            P("lat"),
        ),
        out_specs=(P(None, "lat", "lon"), P(None, "lat", "lon")),
        check_vma=False,
    )
```

```python
import itertools
from functools import partial

import jax
import jax.numpy as jnp
from jax import lax
from jax.experimental import pallas as pl
from jax.experimental.pallas import tpu as pltpu
from jax.sharding import PartitionSpec as P

DRIFT = 8
ITERS = 8


def with_halo(cells, sides, width, closed):
    for axis, dim in sides:
        count = lax.axis_size(axis)
        ends = count if closed else count - 1
        head = lax.slice_in_dim(cells, 0, width, axis=dim)
        tail = lax.slice_in_dim(cells, cells.shape[dim] - width, cells.shape[dim], axis=dim)
        cells = jnp.concatenate(
            [
                lax.ppermute(tail, axis, [(i, (i + 1) % count) for i in range(ends)]),
                cells,
                lax.ppermute(head, axis, [((i + 1) % count, i) for i in range(ends)]),
            ],
            axis=dim,
        )
    return cells


def local_terms(values, helm_diag, vertical, east_west, north_south):
    stacked = jnp.pad(values, ((1, 1), (0, 0), (0, 0)))
    up_down = stacked[2:] + stacked[:-2]
    coupling = vertical[:, None, None]
    return (
        (4.0 + 2.0 * coupling + helm_diag) * values - (east_west + north_south) - coupling * up_down
    )


def operate(values, helm_diag, vertical):
    zonal = with_halo(values, (("lon", 2),), 1, True)
    meridional = with_halo(values, (("lat", 1),), 1, False)
    east_west = zonal[:, :, 2:] + zonal[:, :, :-2]
    north_south = meridional[:, 2:, :] + meridional[:, :-2, :]
    return local_terms(values, helm_diag, vertical, east_west, north_south)


def squares(residual):
    return lax.psum(jnp.sum(residual * residual), ("lon", "lat"))


MESH = pl.DeviceIdType.MESH
F32 = jnp.float32
STEPS = 8
SIZES = {"zl": 2, "x": 4, "zh": 2, "y": 4, "c": 2}
PLANE, REST = ("x", "y"), ("zl", "zh", "c")
PART = 112
FAR_FIRST = [6, 2, 5, 7, 3, 1, 4]
LIMIT = 1.5e4
ROWS, COLS = 48, 512
XR, TOP, TILES = 80, 16, 5


def iota(shape, dim):
    return lax.broadcasted_iota(jnp.int32, shape, dim)


class Remote:
    def __init__(self, send_sems, recv_sems):
        self.send_sems, self.recv_sems, self.used, self.all = send_sems, recv_sems, 0, []

    def start(self, src, dst, lon, lat):
        copy = pltpu.make_async_remote_copy(
            src_ref=src,
            dst_ref=dst,
            send_sem=self.send_sems.at[self.used],
            recv_sem=self.recv_sems.at[self.used],
            device_id=(lon, lat),
            device_id_type=MESH,
        )
        self.used += 1
        copy.start()
        self.all.append(copy)
        return copy

    def settle(self, copies):
        for copy in copies:
            copy.wait_send()
            self.all = [other for other in self.all if other is not copy]

    def drain(self):
        for copy in self.all:
            copy.wait_send()


def coefficients(gram, steps, middle, half):
    def apply(vec):
        out = {}

        def add(i, x):
            out[i] = out[i] + x if i in out else x

        for i, x in vec.items():
            add(i, x * middle)
            if i == 0:
                add(1, x * half)
            else:
                add(i + 1, x * (0.5 * half))
                add(i - 1, x * (0.5 * half))
        return out

    def form(a, b):
        total = size = None
        for i, x in a.items():
            inner = bulk = None
            for j, y in b.items():
                term = gram(i, j) * y
                inner = term if inner is None else inner + term
                bulk = jnp.abs(term) if bulk is None else bulk + jnp.abs(term)
            total = x * inner if total is None else total + x * inner
            size = jnp.abs(x) * bulk if size is None else size + jnp.abs(x) * bulk
        return total, size / jnp.abs(total)

    def plus(a, scale, b):
        return {i: a[i] + scale * b[i] if i in a and i in b else (a[i] if i in a else scale * b[i]) for i in {**a, **b}}

    one = jnp.ones((8, 128), F32)
    direction, residual, answer = {0: one}, {0: one}, {}
    norm, worst = gram(0, 0), one
    for count in range(steps):
        applied = apply(direction)
        slope, size = form(direction, applied)
        worst = jnp.maximum(worst, size)
        rate = norm / slope
        answer = plus(answer, rate, direction)
        if count < steps - 1:
            residual = plus(residual, -rate, applied)
            follow, size = form(residual, residual)
            worst = jnp.maximum(worst, size)
            direction = plus(residual, follow / norm, direction)
            norm = follow
    return answer, worst


class Gram:
    def __init__(self, row, pairs):
        self.row, self.place, self.cache = row, {p: i for i, p in enumerate(pairs)}, {}

    def __call__(self, i, j):
        pair = (min(i, j), max(i, j))
        if pair not in self.cache:
            at = self.place[pair]
            self.cache[pair] = jnp.broadcast_to(self.row[:, at : at + 1], (8, 128))
        return self.cache[pair]


def solve_kernel(
    nlon, nlat, vertical_far, band_far, offsets_far, shifts_far, classes_far, source, helm, dep, out, flag,
    vertical, band, offsets, shifts, classes,
    inner, upper, lower, picked, gathered, circle, looped, banded, returned, beyond,
    vs, dd, lon_in, packs, stage, slot_plane, slot_rest, local_sems, send_sems, recv_sems,
):
    lon, lat = lax.axis_index("lon"), lax.axis_index("lat")

    def east(k):
        return lax.rem(lon + (k + nlon), nlon)

    def north(k):
        return lax.rem(lat + (k + nlat), nlat)

    small = [
        pltpu.make_async_copy(a, b, local_sems.at[16 + n])
        for n, (a, b) in enumerate(
            [
                (vertical_far, vertical), (band_far, band), (offsets_far, offsets),
                (shifts_far, shifts), (classes_far, classes),
            ]
        )
    ]
    for copy in small:
        copy.start()
    here = {"zl": lon // 4, "x": lax.rem(lon, 4), "zh": lat // 8, "y": lax.rem(lat // 2, 4), "c": lax.rem(lat, 2)}

    def place_of(moves):
        spot = {a: lax.rem(v + moves.get(a, 0), SIZES[a]) for a, v in here.items()}
        return spot["zl"] * 4 + spot["x"], spot["zh"] * 8 + spot["y"] * 2 + spot["c"]

    def partners(axes):
        moves = [dict(zip(axes, m)) for m in itertools.product(*[range(SIZES[a]) for a in axes]) if any(m)]
        far = {"c": 0, "zl": 1, "zh": 2}
        return sorted(moves, key=lambda m: -sum(far.get(a, 1) * min(v, SIZES[a] - v) for a, v in m.items()))

    barrier = pltpu.get_barrier_semaphore()
    greet = [(east(k), lat) for k in range(1, nlon)]
    greet += [(east(k), north(b)) for k in range(nlon) for b in (-1, 1)]
    greet += [place_of(m) for m in partners(PLANE) if m["y"]]
    greet += [place_of(m) for m in partners(REST) if m["zh"] or m["c"]]
    for peer in greet:
        pl.semaphore_signal(barrier, inc=1, device_id=peer, device_id_type=MESH)
    greeted = len(greet)
    own = [
        pltpu.make_async_copy(
            source.at[:, pl.ds(start, size), pl.ds(128 * b, 128)],
            into.at[:, b, pl.ds(at, size), :],
            local_sems.at[4 * n + b],
        )
        for n, (into, start, at, size) in enumerate(
            [(inner, 0, 0, ROWS), (upper, 0, DRIFT, 2 * DRIFT), (lower, ROWS - 2 * DRIFT, 0, 2 * DRIFT)]
        )
        for b in range(4)
    ]
    own_diag = [
        pltpu.make_async_copy(
            helm.at[:, :, pl.ds(128 * b, 128)], dd.at[:, b, pl.ds(TOP, ROWS), :], local_sems.at[12 + b]
        )
        for b in range(4)
    ]
    for copy in own + own_diag:
        copy.start()

    remote = Remote(send_sems, recv_sems)
    lane, sub = iota((8, 128), 1), iota((8, 128), 0)
    top_ok, bottom_ok = lat > 0, lat < nlat - 1

    def clear():
        zero = jnp.zeros((8, 128), F32)

        def one(j, carry):
            for b in range(TILES):
                for t in range(XR // 8):
                    vs[j, 0, b, 8 * t : 8 * t + 8, :] = zero
                    vs[j, 5, b, 8 * t : 8 * t + 8, :] = zero
                for level in range(1, 5):
                    vs[j, level, b, 0:8, :] = zero
                    vs[j, level, b, XR - 8 : XR, :] = zero
            return carry

        lax.fori_loop(0, STEPS + 1, one, 0)
        stage[...] = jnp.zeros_like(stage)

    for copy in small:
        copy.wait()
    mean = 0.25 * ((vertical[0] + vertical[1]) + (vertical[2] + vertical[3]))
    top = 0.9 * (9.0 + 4.0 * mean)
    middle, half = 0.54 * top, 0.46 * top
    double = jnp.full((8, 128), 2.0, F32) / jnp.broadcast_to(half, (8, 128))

    def start_exchange(tile, place, which):
        for h in range(2):
            right = left = jnp.zeros((8, 128), F32)
            for i in range(12):
                here = lane // 8 == i
                level = 2 * h + i // 6
                right = jnp.where(here, pltpu.roll(tile(level, i % 6, 3), (8 * i + 8) % 128, 1), right)
                left = jnp.where(here, pltpu.roll(tile(level, i % 6, 0), 8 * i, 1), left)
            packs[which, 0, h] = right
            packs[which, 1, h] = left
        return [
            remote.start(place(TOP + ROWS - 8), place(TOP - 8), lon, north(1)),
            remote.start(place(TOP), place(TOP + ROWS), lon, north(-1)),
            remote.start(packs.at[which, 0], lon_in.at[which, 0], east(1), lat),
            remote.start(packs.at[which, 0], lon_in.at[which, 1], east(1), north(1)),
            remote.start(packs.at[which, 0], lon_in.at[which, 2], east(1), north(-1)),
            remote.start(packs.at[which, 1], lon_in.at[which, 3], east(-1), lat),
            remote.start(packs.at[which, 1], lon_in.at[which, 4], east(-1), north(1)),
            remote.start(packs.at[which, 1], lon_in.at[which, 5], east(-1), north(-1)),
        ]

    def finish_exchange(copies, put, which):
        for copy in copies:
            copy.wait_recv()
        for level in range(4):
            packed = [lon_in[which, i, level // 2] for i in range(6)]
            for t in range(-1, 7):
                i = 6 * (level % 2) + (5 if t < 0 else t if t < 6 else 0)
                side = 1 if t < 0 else 0 if t < 6 else 2
                westward = pltpu.roll(packed[side], (120 - 8 * i) % 128, 1)
                eastward = pltpu.roll(packed[3 + side], (-8 * i) % 128, 1)
                put(level, t, 4, jnp.where(lane < 64, eastward, westward))
        for missing, t in ((lat == nlat - 1, 6), (lat == 0, -1)):

            @pl.when(missing)
            def _(t=t):
                for level in range(4):
                    for b in range(5):
                        put(level, t, b, jnp.zeros((8, 128), F32))

    def b_put(level, t, b, value):
        vs[0, level + 1, b, TOP + 8 * t : TOP + 8 * t + 8, :] = value

    def diag_tile(level, t, b):
        return dd[level, b, TOP + 8 * t : TOP + 8 * t + 8, :]

    def diag_put(level, t, b, value):
        dd[level, b, TOP + 8 * t : TOP + 8 * t + 8, :] = value

    def diag_rows(at):
        return dd.at[:, pl.ds(0, 4), pl.ds(at, 8), :]

    def shift_diag():
        def one(level, carry):
            add = 4.0 + 2.0 * vertical[level] - middle
            for b in range(TILES):
                for t in range(-1, 7):
                    value = double * (diag_tile(level, t, b) + add)
                    if t in (-1, 6):
                        value = jnp.where(top_ok if t < 0 else bottom_ok, value, 0.0)
                    diag_put(level, t, b, value)
            return carry

        lax.fori_loop(0, 4, one, 0)

    def chebyshev(src, before, dst):
        last = dst == STEPS

        def one(level, carry):
            results = []
            tiles = range(0, 6) if last else range(-1, 7)
            at = lambda j, l, t, b: vs[j, l, b, TOP + 8 * t : TOP + 8 * t + 8, :]
            for t in tiles:
                scale = double
                if t == -1:
                    scale = jnp.where(top_ok, double, 0.0)
                if t == 6:
                    scale = jnp.where(bottom_ok, double, 0.0)
                mids = [at(src, level + 1, t, b) for b in range(TILES)]
                for b in range(4 if last else TILES):
                    mid = mids[b]
                    sides = pltpu.roll(jnp.where(lane == 127, mids[b - 1], mid), 1, 1)
                    sides = sides + pltpu.roll(jnp.where(lane == 0, mids[(b + 1) % TILES], mid), 127, 1)
                    above, below = at(src, level + 1, t - 1, b), at(src, level + 1, t + 1, b)
                    sides = sides + pltpu.roll(jnp.where(sub == 7, above, mid), 1, 0)
                    sides = sides + pltpu.roll(jnp.where(sub == 0, below, mid), 7, 0)
                    stack = at(src, level, t, b) + at(src, level + 2, t, b)
                    value = dd[level, b, TOP + 8 * t : TOP + 8 * t + 8, :] * mid - scale * (sides + vertical[level] * stack)
                    if before is None:
                        value = 0.5 * value
                    else:
                        value = value - at(before, level + 1, t, b)
                    results.append((b, t, value))
                    if len(results) == 20:
                        for bb, tt, v in results:
                            vs[dst, level + 1, bb, TOP + 8 * tt : TOP + 8 * tt + 8, :] = v
                        results = []
            for bb, tt, v in results:
                vs[dst, level + 1, bb, TOP + 8 * tt : TOP + 8 * tt + 8, :] = v
            return carry

        for level in range(4):
            one(level, 0)

    def all_reduce(value):
        for axes, slot in ((PLANE, slot_plane), (REST, slot_rest)):
            mine = 0
            for axis in axes:
                mine = mine * SIZES[axis] + here[axis]
            slot[mine] = value[0:1]
            copies = [remote.start(slot.at[mine], slot.at[mine], *place_of(m)) for m in partners(axes)]
            for copy in copies:
                copy.wait_recv()
            value = slot[0]
            for i in range(1, slot.shape[0]):
                value = value + slot[i]
        return value

    def gram():
        count = STEPS + 1
        pairs = [(i, j) for i in range(count) for j in range(i, count) if i < STEPS]

        def one(t, sums):
            level, r = t // 6, (t % 6) * 8
            sums = list(sums)
            for b in range(4):
                tiles = [vs[i, level + 1, b, pl.ds(r + TOP, 8), :] for i in range(count)]
                for n, (i, j) in enumerate(pairs):
                    sums[n] = sums[n] + tiles[i] * tiles[j]
            return tuple(sums)

        sums = tuple(jnp.zeros((8, 128), F32) for _ in pairs)
        for t in range(24):
            sums = one(t, sums)
        for n, part in enumerate(sums):
            stage[n : n + 1, :] = jnp.sum(part, axis=0, keepdims=True)
        row = lax.dot_general(
            jnp.ones((8, 128), F32), stage[...], (((1,), (1,)), ((), ())),
            precision=lax.Precision.HIGHEST, preferred_element_type=F32,
        )
        return Gram(all_reduce(row), pairs)

    def combine(coef):
        def one(t, carry):
            level, r = t // 6, (t % 6) * 8
            for b in range(4):
                value = None
                for i, x in coef.items():
                    term = x * vs[i, level + 1, b, pl.ds(r + TOP, 8), :]
                    value = term if value is None else value + term
                out[level, pl.ds(r, 8), 128 * b : 128 * b + 128] = value
            return carry

        for t in range(24):
            one(t, 0)

    for copy in own[0:4]:
        copy.wait()

    def pick(j, part, write):
        from_, first, rows = [(inner, 0, ROWS), (upper, -DRIFT, 3 * DRIFT), (lower, ROWS - 2 * DRIFT, 3 * DRIFT)][part]
        row = jnp.clip(j + offsets[j] - first, 0, rows - 1)
        for level in range(4):
            for b in range(4):
                write(4 * level + b, from_[level, b, pl.ds(row, 1), :])

    def pick_rows(c, k, rows, at, parts):
        for n, (j, part) in enumerate(zip(rows, parts)):

            def write(place, value, n=n):
                if k == nlon:
                    gathered[c, at + 16 * n + place : at + 16 * n + place + 1, :] = value
                else:
                    picked[k - 1, at + 16 * n + place : at + 16 * n + place + 1, :] = value

            pick(j, part, write)

    def middle_rows(c):
        return [DRIFT + 4 * c + q for q in range(4)]

    def edge_rows(c):
        return [c, ROWS - DRIFT + c]

    for k in range(1, nlon + 1):
        pick_rows(east(k % nlon), k, middle_rows(east(k % nlon)), 0, (0, 0, 0, 0))
    pl.semaphore_wait(barrier, greeted)
    beside = [
        remote.start(inner.at[:, :, pl.ds(ROWS - DRIFT, DRIFT), :], upper.at[:, :, pl.ds(0, DRIFT), :], lon, north(1)),
        remote.start(inner.at[:, :, pl.ds(0, DRIFT), :], lower.at[:, :, pl.ds(2 * DRIFT, DRIFT), :], lon, north(-1)),
    ]

    def send_picked(start, size):
        return [
            remote.start(
                picked.at[k - 1, pl.ds(start, size)], gathered.at[lon, pl.ds(start, size)], east(k), lat
            )
            for k in range(1, nlon)
        ]

    sent_middle = send_picked(0, 64)
    for copy in own_diag:
        copy.wait()
    diag_waiting = start_exchange(diag_tile, diag_rows, 0)
    clear()
    for copy in own[4:]:
        copy.wait()
    for copy in beside:
        copy.wait_recv()
    for k in range(1, nlon + 1):
        pick_rows(east(k % nlon), k, edge_rows(east(k % nlon)), 64, (1, 2))
    sent_edge = send_picked(64, 32)

    finish_exchange(diag_waiting, diag_put, 0)
    remote.settle(diag_waiting)

    shift_diag()

    first_half = sub < 4
    lanes = iota((32, 128), 1)

    def fill_circle(pp):
        for m in range(4):
            a, b = gathered[2 * m, 8 * pp : 8 * pp + 8, :], gathered[2 * m + 1, 8 * pp : 8 * pp + 8, :]
            pair = (
                jnp.where(first_half, a, pltpu.roll(b, 4, 0)),
                jnp.where(first_half, pltpu.roll(a, 4, 0), b),
            )
            for n in range(2):
                circle[2 * pp + n, 8 + 8 * m : 16 + 8 * m, :] = pair[n]
                circle[2 * pp + n, 40 + 8 * m : 48 + 8 * m, :] = pair[n]
                if m == 3:
                    circle[2 * pp + n, 0:8, :] = pair[n]
                if m == 0:
                    circle[2 * pp + n, 72:80, :] = pair[n]

    def band_row(row, j, at, edge_at):
        start = 8 + lax.rem(64 - shifts[j], 32)
        weight = [band[t, classes[j]] for t in range(4)]
        outs = []
        for level in range(4):
            now = circle[4 * row + level, pl.ds(start, 32), :]
            before = circle[4 * row + level, pl.ds(start - 1, 32), :]
            after = circle[4 * row + level, pl.ds(start + 1, 32), :]
            total = weight[0] * pltpu.roll(jnp.where(lanes == 127, before, now), 1, 1)
            total = total + weight[1] * now
            total = total + weight[2] * pltpu.roll(jnp.where(lanes == 0, after, now), 127, 1)
            total = total + weight[3] * pltpu.roll(jnp.where(lanes < 2, after, now), 126, 1)
            outs.append(total)
        for half in range(2):
            for m in range(4):
                a, b = outs[2 * half][8 * m : 8 * m + 8], outs[2 * half + 1][8 * m : 8 * m + 8]
                here = slice(at + 8 * half, at + 8 * half + 8)
                banded[2 * m, here, :] = jnp.where(first_half, a, pltpu.roll(b, 4, 0))
                banded[2 * m + 1, here, :] = jnp.where(first_half, pltpu.roll(a, 4, 0), b)
        edges = jnp.zeros((8, 128), F32)
        for level in range(4):
            looped[4 * row + level, 0:8, :] = outs[level][24:32]
            looped[4 * row + level, 8:40, :] = outs[level]
            looped[4 * row + level, 40:48, :] = outs[level][0:8]
        for level in range(4):
            west = looped[4 * row + level, pl.ds(7, 8, stride=4), :]
            east_ = looped[4 * row + level, pl.ds(12, 8, stride=4), :]
            both = pltpu.roll(jnp.where(lane < 64, east_, west), 16 * level + 8, 1)
            edges = jnp.where(lane // 16 == level, both, edges)
        for d in range(nlon):
            banded[d, edge_at : edge_at + 1, :] = edges[d : d + 1]

    def send_banded(start, size):
        here = pl.multiple_of(lon * PART + start, 8)
        copies = [
            remote.start(banded.at[east(k), pl.ds(start, size)], returned.at[pl.ds(here, size)], east(k), lat)
            for k in FAR_FIRST
        ]
        returned[pl.ds(here, size), :] = banded[lon, pl.ds(start, size), :]
        return copies

    def send_beyond():
        here = pl.multiple_of(lon * 24, 8)
        copies = []
        for k in FAR_FIRST + [0]:
            for start, side, step in ((89, 0, 1), (72, 1, -1)):
                copies.append(
                    remote.start(
                        banded.at[east(k), pl.ds(start, 17)], beyond.at[side, pl.ds(here, 17)], east(k), north(step)
                    )
                )
        return copies

    for copy in sent_middle:
        copy.wait_recv()
    for pp in range(8):
        fill_circle(pp)
    for q in range(4):
        band_row(q, DRIFT + 4 * lon + q, 16 * q, 64 + q)
    arriving = send_banded(0, 68)
    for copy in sent_edge:
        copy.wait_recv()
    for pp in range(8, 12):
        fill_circle(pp)
    band_row(4, lon, 72, 88)
    band_row(5, lon + ROWS - DRIFT, 90, 89)
    arriving += send_beyond() + send_banded(72, 34)
    for copy in arriving:
        copy.wait_recv()

    def row_tile(t, place, beside):
        if t in (-1, 6):
            place = (16 if t > 0 else 0) if beside else place + (t < 0)
            return beyond[t // 6 if t > 0 else 0, pl.ds(place, 8, stride=24), :]
        if t in (0, 5):
            place = 88 + t // 5 if beside else 72 + 18 * (t // 5) + place
            return returned[pl.ds(place, 8, stride=PART), :]
        both = []
        for c in (2 * t - 2, 2 * t - 1):
            if beside:
                both.append(returned[c * PART + 64 : c * PART + 68, :])
            else:
                both.append(returned[pl.ds(c * PART + place, 4, stride=16), :])
        return jnp.concatenate(both, 0)

    for t in range(-1, 7):
        outside = {-1: top_ok, 6: bottom_ok}.get(t)
        beside = row_tile(t, 0, True)
        for level in range(4):
            tiles = [row_tile(t, 4 * level + b, False) for b in range(4)]
            tiles.append(pltpu.roll(beside, (120 - 16 * level) % 128, 1))
            for b, tile in enumerate(tiles):
                if outside is not None:
                    tile = jnp.where(outside, tile, 0.0)
                elif b < 4:
                    dep[level, 8 * t : 8 * t + 8, 128 * b : 128 * b + 128] = tile
                b_put(level, t, b, tile)
    for k in range(1, STEPS + 1):
        chebyshev(k - 1, None if k == 1 else k - 2, k)
    answer, worst = coefficients(gram(), STEPS, middle, half)
    combine(answer)
    flag[0, 0] = jnp.max(worst)
    remote.drain()


def solve(source_field, helm_diag, vertical, band, offsets, shifts, classes, nlon, nlat):
    copies = 2 + 4 * (nlon - 1) + 8 + 2 * nlon + 15 + 7
    vmem = pl.BlockSpec(memory_space=pltpu.VMEM)
    smem = pl.BlockSpec(memory_space=pltpu.SMEM)
    far = pl.BlockSpec(memory_space=pltpu.HBM)
    field = jax.ShapeDtypeStruct(source_field.shape, F32)
    return pl.pallas_call(
        partial(solve_kernel, nlon, nlat),
        out_shape=(field, field, jax.ShapeDtypeStruct((1, 1), F32)),
        in_specs=[far] * 7,
        out_specs=(vmem, vmem, smem),
        scratch_shapes=[
            pltpu.SMEM((4,), F32),
            pltpu.SMEM(band.shape, F32),
            pltpu.SMEM(offsets.shape, jnp.int32),
            pltpu.SMEM(shifts.shape, jnp.int32),
            pltpu.SMEM(classes.shape, jnp.int32),
            pltpu.VMEM((4, 4, ROWS, 128), F32),
            pltpu.VMEM((4, 4, 3 * DRIFT, 128), F32),
            pltpu.VMEM((4, 4, 3 * DRIFT, 128), F32),
            pltpu.VMEM((nlon - 1, 96, 128), F32),
            pltpu.VMEM((nlon, 96, 128), F32),
            pltpu.VMEM((24, 80, 128), F32),
            pltpu.VMEM((24, 48, 128), F32),
            pltpu.VMEM((nlon, PART, 128), F32),
            pltpu.VMEM((nlon * PART, 128), F32),
            pltpu.VMEM((2, nlon * 24, 128), F32),
            pltpu.VMEM((STEPS + 1, 6, TILES, XR, 128), F32),
            pltpu.VMEM((4, TILES, XR, 128), F32),
            pltpu.VMEM((1, 6, 2, 8, 128), F32),
            pltpu.VMEM((1, 2, 2, 8, 128), F32),
            pltpu.VMEM((128, 128), F32),
            pltpu.VMEM((16, 1, 128), F32),
            pltpu.VMEM((8, 1, 128), F32),
            pltpu.SemaphoreType.DMA((21,)),
            pltpu.SemaphoreType.DMA((copies,)),
            pltpu.SemaphoreType.DMA((copies,)),
        ],
        compiler_params=pltpu.CompilerParams(
            collective_id=0, has_side_effects=True, vmem_limit_bytes=62 * 1024 * 1024
        ),
        name="solve",
    )(vertical, band, offsets, shifts, classes, source_field, helm_diag)


def finish_kernel(departure, answer, departure_out, answer_out, sems):
    copies = [
        pltpu.make_async_copy(a.at[k], b.at[k], sems.at[n, k])
        for n, (a, b) in enumerate([(departure, departure_out), (answer, answer_out)])
        for k in range(4)
    ]
    for copy in copies:
        copy.start()
    for copy in copies:
        copy.wait()


def finish(departure, answer):
    anywhere = pl.BlockSpec(memory_space=pl.ANY)
    field = jax.ShapeDtypeStruct(departure.shape, F32)
    return pl.pallas_call(
        finish_kernel,
        out_shape=(field, field),
        in_specs=[anywhere] * 2,
        out_specs=(anywhere, anywhere),
        scratch_shapes=[pltpu.SemaphoreType.DMA((2, 4))],
        name="finish",
    )(departure, answer)


def iterate(departure, helm_diag, vertical):
    def one(_, carry):
        answer, residual, direction, norm = carry
        applied = operate(direction, helm_diag, vertical)
        rate = norm / lax.psum(jnp.sum(direction * applied), ("lon", "lat"))
        answer = answer + rate * direction
        residual = residual - rate * applied
        follow = squares(residual)
        return answer, residual, residual + follow / norm * direction, follow

    start = (jnp.zeros_like(departure), departure, departure, squares(departure))
    answer, _, direction, norm = lax.fori_loop(0, ITERS - 1, one, start)
    applied = operate(direction, helm_diag, vertical)
    return answer + norm / lax.psum(jnp.sum(direction * applied), ("lon", "lat")) * direction


def body(source_field, helm_diag, vertical, cubic_band, lat_offset, zonal_shift, row_class):
    departure, quick, worst = solve(
        source_field, helm_diag, vertical, cubic_band.T, lat_offset, zonal_shift, row_class,
        lax.axis_size("lon"), lax.axis_size("lat"),
    )
    answer = lax.cond(
        worst[0, 0] < LIMIT, lambda *_: quick, iterate, departure, helm_diag, vertical
    )
    return finish(departure, answer)


def solution(mesh):
    return jax.shard_map(
        body,
        mesh=mesh,
        in_specs=(
            P(None, "lat", "lon"),
            P(None, "lat", "lon"),
            P(),
            P(),
            P("lat"),
            P("lat"),
            P("lat"),
        ),
        out_specs=(P(None, "lat", "lon"), P(None, "lat", "lon")),
        check_vma=False,
    )
```

```python
import itertools
from functools import partial

import jax
import jax.numpy as jnp
from jax import lax
from jax.experimental import pallas as pl
from jax.experimental.pallas import tpu as pltpu
from jax.sharding import PartitionSpec as P

DRIFT = 8
ITERS = 8


def with_halo(cells, sides, width, closed):
    for axis, dim in sides:
        count = lax.axis_size(axis)
        ends = count if closed else count - 1
        head = lax.slice_in_dim(cells, 0, width, axis=dim)
        tail = lax.slice_in_dim(cells, cells.shape[dim] - width, cells.shape[dim], axis=dim)
        cells = jnp.concatenate(
            [
                lax.ppermute(tail, axis, [(i, (i + 1) % count) for i in range(ends)]),
                cells,
                lax.ppermute(head, axis, [((i + 1) % count, i) for i in range(ends)]),
            ],
            axis=dim,
        )
    return cells


def local_terms(values, helm_diag, vertical, east_west, north_south):
    stacked = jnp.pad(values, ((1, 1), (0, 0), (0, 0)))
    up_down = stacked[2:] + stacked[:-2]
    coupling = vertical[:, None, None]
    return (
        (4.0 + 2.0 * coupling + helm_diag) * values - (east_west + north_south) - coupling * up_down
    )


def operate(values, helm_diag, vertical):
    zonal = with_halo(values, (("lon", 2),), 1, True)
    meridional = with_halo(values, (("lat", 1),), 1, False)
    east_west = zonal[:, :, 2:] + zonal[:, :, :-2]
    north_south = meridional[:, 2:, :] + meridional[:, :-2, :]
    return local_terms(values, helm_diag, vertical, east_west, north_south)


def squares(residual):
    return lax.psum(jnp.sum(residual * residual), ("lon", "lat"))


MESH = pl.DeviceIdType.MESH
F32 = jnp.float32
STEPS = 8
SIZES = {"zl": 2, "x": 4, "zh": 2, "y": 4, "c": 2}
PLANE, REST = ("x", "y"), ("zl", "zh", "c")
PART = 112
FAR_FIRST = [6, 2, 5, 7, 3, 1, 4]
LIMIT = 1.5e4
ROWS, COLS = 48, 512
XR, TOP, TILES = 80, 16, 5


def iota(shape, dim):
    return lax.broadcasted_iota(jnp.int32, shape, dim)


class Remote:
    def __init__(self, send_sems, recv_sems):
        self.send_sems, self.recv_sems, self.used, self.all = send_sems, recv_sems, 0, []

    def start(self, src, dst, lon, lat):
        copy = pltpu.make_async_remote_copy(
            src_ref=src,
            dst_ref=dst,
            send_sem=self.send_sems.at[self.used],
            recv_sem=self.recv_sems.at[self.used],
            device_id=(lon, lat),
            device_id_type=MESH,
        )
        self.used += 1
        copy.start()
        self.all.append(copy)
        return copy

    def settle(self, copies):
        for copy in copies:
            copy.wait_send()
            self.all = [other for other in self.all if other is not copy]

    def drain(self):
        for copy in self.all:
            copy.wait_send()


def coefficients(gram, steps, middle, half):
    def apply(vec):
        out = {}

        def add(i, x):
            out[i] = out[i] + x if i in out else x

        for i, x in vec.items():
            add(i, x * middle)
            if i == 0:
                add(1, x * half)
            else:
                add(i + 1, x * (0.5 * half))
                add(i - 1, x * (0.5 * half))
        return out

    def form(a, b):
        total = size = None
        for i, x in a.items():
            inner = bulk = None
            for j, y in b.items():
                term = gram(i, j) * y
                inner = term if inner is None else inner + term
                bulk = jnp.abs(term) if bulk is None else bulk + jnp.abs(term)
            total = x * inner if total is None else total + x * inner
            size = jnp.abs(x) * bulk if size is None else size + jnp.abs(x) * bulk
        return total, size / jnp.abs(total)

    def plus(a, scale, b):
        return {i: a[i] + scale * b[i] if i in a and i in b else (a[i] if i in a else scale * b[i]) for i in {**a, **b}}

    one = jnp.ones((8, 128), F32)
    direction, residual, answer = {0: one}, {0: one}, {}
    norm, worst = gram(0, 0), one
    for count in range(steps):
        applied = apply(direction)
        slope, size = form(direction, applied)
        worst = jnp.maximum(worst, size)
        rate = norm / slope
        answer = plus(answer, rate, direction)
        if count < steps - 1:
            residual = plus(residual, -rate, applied)
            follow, size = form(residual, residual)
            worst = jnp.maximum(worst, size)
            direction = plus(residual, follow / norm, direction)
            norm = follow
    return answer, worst


class Gram:
    def __init__(self, row, pairs):
        self.row, self.place, self.cache = row, {p: i for i, p in enumerate(pairs)}, {}

    def __call__(self, i, j):
        pair = (min(i, j), max(i, j))
        if pair not in self.cache:
            at = self.place[pair]
            self.cache[pair] = jnp.broadcast_to(self.row[:, at : at + 1], (8, 128))
        return self.cache[pair]


def solve_kernel(
    nlon, nlat, vertical_far, band_far, offsets_far, shifts_far, classes_far, source, helm, dep, out, flag, coupling,
    vertical, band, offsets, shifts, classes,
    inner, upper, lower, picked, gathered, circle, looped, banded, returned, beyond,
    vs, dd, lon_in, packs, stage, slot_plane, slot_rest, local_sems, send_sems, recv_sems,
):
    lon, lat = lax.axis_index("lon"), lax.axis_index("lat")

    def east(k):
        return lax.rem(lon + (k + nlon), nlon)

    def north(k):
        return lax.rem(lat + (k + nlat), nlat)

    small = [
        pltpu.make_async_copy(a, b, local_sems.at[16 + n])
        for n, (a, b) in enumerate(
            [
                (vertical_far, vertical), (band_far, band), (offsets_far, offsets),
                (shifts_far, shifts), (classes_far, classes),
            ]
        )
    ]
    for copy in small:
        copy.start()
    here = {"zl": lon // 4, "x": lax.rem(lon, 4), "zh": lat // 8, "y": lax.rem(lat // 2, 4), "c": lax.rem(lat, 2)}

    def place_of(moves):
        spot = {a: lax.rem(v + moves.get(a, 0), SIZES[a]) for a, v in here.items()}
        return spot["zl"] * 4 + spot["x"], spot["zh"] * 8 + spot["y"] * 2 + spot["c"]

    def partners(axes):
        moves = [dict(zip(axes, m)) for m in itertools.product(*[range(SIZES[a]) for a in axes]) if any(m)]
        far = {"c": 0, "zl": 1, "zh": 2}
        return sorted(moves, key=lambda m: -sum(far.get(a, 1) * min(v, SIZES[a] - v) for a, v in m.items()))

    barrier = pltpu.get_barrier_semaphore()
    greet = [(east(k), lat) for k in range(1, nlon)]
    greet += [(east(k), north(b)) for k in range(nlon) for b in (-1, 1)]
    greet += [place_of(m) for m in partners(PLANE) if m["y"]]
    greet += [place_of(m) for m in partners(REST) if m["zh"] or m["c"]]
    for peer in greet:
        pl.semaphore_signal(barrier, inc=1, device_id=peer, device_id_type=MESH)
    greeted = len(greet)
    own = [
        pltpu.make_async_copy(
            source.at[:, pl.ds(start, size), pl.ds(128 * b, 128)],
            into.at[:, b, pl.ds(at, size), :],
            local_sems.at[4 * n + b],
        )
        for n, (into, start, at, size) in enumerate(
            [(inner, 0, 0, ROWS), (upper, 0, DRIFT, 2 * DRIFT), (lower, ROWS - 2 * DRIFT, 0, 2 * DRIFT)]
        )
        for b in range(4)
    ]
    own_diag = [
        pltpu.make_async_copy(
            helm.at[:, :, pl.ds(128 * b, 128)], dd.at[:, b, pl.ds(TOP, ROWS), :], local_sems.at[12 + b]
        )
        for b in range(4)
    ]
    for copy in own + own_diag:
        copy.start()

    remote = Remote(send_sems, recv_sems)
    lane, sub = iota((8, 128), 1), iota((8, 128), 0)
    top_ok, bottom_ok = lat > 0, lat < nlat - 1

    def clear():
        zero = jnp.zeros((8, 128), F32)

        def one(j, carry):
            for b in range(TILES):
                for t in range(XR // 8):
                    vs[j, 0, b, 8 * t : 8 * t + 8, :] = zero
                    vs[j, 5, b, 8 * t : 8 * t + 8, :] = zero
                for level in range(1, 5):
                    vs[j, level, b, 0:8, :] = zero
                    vs[j, level, b, XR - 8 : XR, :] = zero
            return carry

        lax.fori_loop(0, STEPS + 1, one, 0)
        stage[...] = jnp.zeros_like(stage)

    for copy in small:
        copy.wait()
    mean = 0.25 * ((vertical[0] + vertical[1]) + (vertical[2] + vertical[3]))
    top = 0.9 * (9.0 + 4.0 * mean)
    middle, half = 0.54 * top, 0.46 * top
    double = jnp.full((8, 128), 2.0, F32) / jnp.broadcast_to(half, (8, 128))

    def start_exchange(tile, place, which):
        for h in range(2):
            right = left = jnp.zeros((8, 128), F32)
            for i in range(12):
                here = lane // 8 == i
                level = 2 * h + i // 6
                right = jnp.where(here, pltpu.roll(tile(level, i % 6, 3), (8 * i + 8) % 128, 1), right)
                left = jnp.where(here, pltpu.roll(tile(level, i % 6, 0), 8 * i, 1), left)
            packs[which, 0, h] = right
            packs[which, 1, h] = left
        return [
            remote.start(place(TOP + ROWS - 8), place(TOP - 8), lon, north(1)),
            remote.start(place(TOP), place(TOP + ROWS), lon, north(-1)),
            remote.start(packs.at[which, 0], lon_in.at[which, 0], east(1), lat),
            remote.start(packs.at[which, 0], lon_in.at[which, 1], east(1), north(1)),
            remote.start(packs.at[which, 0], lon_in.at[which, 2], east(1), north(-1)),
            remote.start(packs.at[which, 1], lon_in.at[which, 3], east(-1), lat),
            remote.start(packs.at[which, 1], lon_in.at[which, 4], east(-1), north(1)),
            remote.start(packs.at[which, 1], lon_in.at[which, 5], east(-1), north(-1)),
        ]

    def finish_exchange(copies, put, which):
        for copy in copies:
            copy.wait_recv()
        for level in range(4):
            packed = [lon_in[which, i, level // 2] for i in range(6)]
            for t in range(-1, 7):
                i = 6 * (level % 2) + (5 if t < 0 else t if t < 6 else 0)
                side = 1 if t < 0 else 0 if t < 6 else 2
                westward = pltpu.roll(packed[side], (120 - 8 * i) % 128, 1)
                eastward = pltpu.roll(packed[3 + side], (-8 * i) % 128, 1)
                put(level, t, 4, jnp.where(lane < 64, eastward, westward))
        for missing, t in ((lat == nlat - 1, 6), (lat == 0, -1)):

            @pl.when(missing)
            def _(t=t):
                for level in range(4):
                    for b in range(5):
                        put(level, t, b, jnp.zeros((8, 128), F32))

    def b_put(level, t, b, value):
        vs[0, level + 1, b, TOP + 8 * t : TOP + 8 * t + 8, :] = value

    def diag_tile(level, t, b):
        return dd[level, b, TOP + 8 * t : TOP + 8 * t + 8, :]

    def diag_put(level, t, b, value):
        dd[level, b, TOP + 8 * t : TOP + 8 * t + 8, :] = value

    def diag_rows(at):
        return dd.at[:, pl.ds(0, 4), pl.ds(at, 8), :]

    def shift_diag():
        def one(level, carry):
            add = 4.0 + 2.0 * vertical[level] - middle
            for b in range(TILES):
                for t in range(-1, 7):
                    value = double * (diag_tile(level, t, b) + add)
                    if t in (-1, 6):
                        value = jnp.where(top_ok if t < 0 else bottom_ok, value, 0.0)
                    diag_put(level, t, b, value)
            return carry

        lax.fori_loop(0, 4, one, 0)

    def chebyshev(src, before, dst):
        last = dst == STEPS

        def one(level, carry):
            results = []
            tiles = range(0, 6) if last else range(-1, 7)
            at = lambda j, l, t, b: vs[j, l, b, TOP + 8 * t : TOP + 8 * t + 8, :]
            for t in tiles:
                scale = double
                if t == -1:
                    scale = jnp.where(top_ok, double, 0.0)
                if t == 6:
                    scale = jnp.where(bottom_ok, double, 0.0)
                mids = [at(src, level + 1, t, b) for b in range(TILES)]
                for b in range(4 if last else TILES):
                    mid = mids[b]
                    sides = pltpu.roll(jnp.where(lane == 127, mids[b - 1], mid), 1, 1)
                    sides = sides + pltpu.roll(jnp.where(lane == 0, mids[(b + 1) % TILES], mid), 127, 1)
                    above, below = at(src, level + 1, t - 1, b), at(src, level + 1, t + 1, b)
                    sides = sides + pltpu.roll(jnp.where(sub == 7, above, mid), 1, 0)
                    sides = sides + pltpu.roll(jnp.where(sub == 0, below, mid), 7, 0)
                    stack = at(src, level, t, b) + at(src, level + 2, t, b)
                    value = dd[level, b, TOP + 8 * t : TOP + 8 * t + 8, :] * mid - scale * (sides + vertical[level] * stack)
                    if before is None:
                        value = 0.5 * value
                    else:
                        value = value - at(before, level + 1, t, b)
                    results.append((b, t, value))
                    if len(results) == 20:
                        for bb, tt, v in results:
                            vs[dst, level + 1, bb, TOP + 8 * tt : TOP + 8 * tt + 8, :] = v
                        results = []
            for bb, tt, v in results:
                vs[dst, level + 1, bb, TOP + 8 * tt : TOP + 8 * tt + 8, :] = v
            return carry

        for level in range(4):
            one(level, 0)

    def all_reduce(value):
        for axes, slot in ((PLANE, slot_plane), (REST, slot_rest)):
            mine = 0
            for axis in axes:
                mine = mine * SIZES[axis] + here[axis]
            slot[mine] = value[0:1]
            copies = [remote.start(slot.at[mine], slot.at[mine], *place_of(m)) for m in partners(axes)]
            for copy in copies:
                copy.wait_recv()
            value = slot[0]
            for i in range(1, slot.shape[0]):
                value = value + slot[i]
        return value

    def gram():
        count = STEPS + 1
        pairs = [(i, j) for i in range(count) for j in range(i, count) if i < STEPS]

        def one(t, sums):
            level, r = t // 6, (t % 6) * 8
            sums = list(sums)
            for b in range(4):
                tiles = [vs[i, level + 1, b, pl.ds(r + TOP, 8), :] for i in range(count)]
                for n, (i, j) in enumerate(pairs):
                    sums[n] = sums[n] + tiles[i] * tiles[j]
            return tuple(sums)

        sums = tuple(jnp.zeros((8, 128), F32) for _ in pairs)
        for t in range(24):
            sums = one(t, sums)
        for n, part in enumerate(sums):
            stage[n : n + 1, :] = jnp.sum(part, axis=0, keepdims=True)
        row = lax.dot_general(
            jnp.ones((8, 128), F32), stage[...], (((1,), (1,)), ((), ())),
            precision=lax.Precision.HIGHEST, preferred_element_type=F32,
        )
        return Gram(all_reduce(row), pairs)

    def combine(coef):
        def one(t, carry):
            level, r = t // 6, (t % 6) * 8
            for b in range(4):
                value = None
                for i, x in coef.items():
                    term = x * vs[i, level + 1, b, pl.ds(r + TOP, 8), :]
                    value = term if value is None else value + term
                out[level, pl.ds(r, 8), 128 * b : 128 * b + 128] = value
            return carry

        for t in range(24):
            one(t, 0)

    for copy in own[0:4]:
        copy.wait()

    def pick(j, part, write):
        from_, first, rows = [(inner, 0, ROWS), (upper, -DRIFT, 3 * DRIFT), (lower, ROWS - 2 * DRIFT, 3 * DRIFT)][part]
        row = jnp.clip(j + offsets[j] - first, 0, rows - 1)
        for level in range(4):
            for b in range(4):
                write(4 * level + b, from_[level, b, pl.ds(row, 1), :])

    def pick_rows(c, k, rows, at, parts):
        for n, (j, part) in enumerate(zip(rows, parts)):

            def write(place, value, n=n):
                if k == nlon:
                    gathered[c, at + 16 * n + place : at + 16 * n + place + 1, :] = value
                else:
                    picked[k - 1, at + 16 * n + place : at + 16 * n + place + 1, :] = value

            pick(j, part, write)

    def middle_rows(c):
        return [DRIFT + 4 * c + q for q in range(4)]

    def edge_rows(c):
        return [c, ROWS - DRIFT + c]

    for k in range(1, nlon + 1):
        pick_rows(east(k % nlon), k, middle_rows(east(k % nlon)), 0, (0, 0, 0, 0))
    pl.semaphore_wait(barrier, greeted)
    beside = [
        remote.start(inner.at[:, :, pl.ds(ROWS - DRIFT, DRIFT), :], upper.at[:, :, pl.ds(0, DRIFT), :], lon, north(1)),
        remote.start(inner.at[:, :, pl.ds(0, DRIFT), :], lower.at[:, :, pl.ds(2 * DRIFT, DRIFT), :], lon, north(-1)),
    ]

    def send_picked(start, size):
        return [
            remote.start(
                picked.at[k - 1, pl.ds(start, size)], gathered.at[lon, pl.ds(start, size)], east(k), lat
            )
            for k in range(1, nlon)
        ]

    sent_middle = send_picked(0, 64)
    for copy in own_diag:
        copy.wait()
    diag_waiting = start_exchange(diag_tile, diag_rows, 0)
    clear()
    for copy in own[4:]:
        copy.wait()
    for copy in beside:
        copy.wait_recv()
    for k in range(1, nlon + 1):
        pick_rows(east(k % nlon), k, edge_rows(east(k % nlon)), 64, (1, 2))
    sent_edge = send_picked(64, 32)

    finish_exchange(diag_waiting, diag_put, 0)
    remote.settle(diag_waiting)

    shift_diag()

    first_half = sub < 4
    lanes = iota((32, 128), 1)

    def fill_circle(pp):
        for m in range(4):
            a, b = gathered[2 * m, 8 * pp : 8 * pp + 8, :], gathered[2 * m + 1, 8 * pp : 8 * pp + 8, :]
            pair = (
                jnp.where(first_half, a, pltpu.roll(b, 4, 0)),
                jnp.where(first_half, pltpu.roll(a, 4, 0), b),
            )
            for n in range(2):
                circle[2 * pp + n, 8 + 8 * m : 16 + 8 * m, :] = pair[n]
                circle[2 * pp + n, 40 + 8 * m : 48 + 8 * m, :] = pair[n]
                if m == 3:
                    circle[2 * pp + n, 0:8, :] = pair[n]
                if m == 0:
                    circle[2 * pp + n, 72:80, :] = pair[n]

    def band_row(row, j, at, edge_at):
        start = 8 + lax.rem(64 - shifts[j], 32)
        weight = [band[t, classes[j]] for t in range(4)]
        outs = []
        for level in range(4):
            now = circle[4 * row + level, pl.ds(start, 32), :]
            before = circle[4 * row + level, pl.ds(start - 1, 32), :]
            after = circle[4 * row + level, pl.ds(start + 1, 32), :]
            total = weight[0] * pltpu.roll(jnp.where(lanes == 127, before, now), 1, 1)
            total = total + weight[1] * now
            total = total + weight[2] * pltpu.roll(jnp.where(lanes == 0, after, now), 127, 1)
            total = total + weight[3] * pltpu.roll(jnp.where(lanes < 2, after, now), 126, 1)
            outs.append(total)
        for half in range(2):
            for m in range(4):
                a, b = outs[2 * half][8 * m : 8 * m + 8], outs[2 * half + 1][8 * m : 8 * m + 8]
                here = slice(at + 8 * half, at + 8 * half + 8)
                banded[2 * m, here, :] = jnp.where(first_half, a, pltpu.roll(b, 4, 0))
                banded[2 * m + 1, here, :] = jnp.where(first_half, pltpu.roll(a, 4, 0), b)
        edges = jnp.zeros((8, 128), F32)
        for level in range(4):
            looped[4 * row + level, 0:8, :] = outs[level][24:32]
            looped[4 * row + level, 8:40, :] = outs[level]
            looped[4 * row + level, 40:48, :] = outs[level][0:8]
        for level in range(4):
            west = looped[4 * row + level, pl.ds(7, 8, stride=4), :]
            east_ = looped[4 * row + level, pl.ds(12, 8, stride=4), :]
            both = pltpu.roll(jnp.where(lane < 64, east_, west), 16 * level + 8, 1)
            edges = jnp.where(lane // 16 == level, both, edges)
        for d in range(nlon):
            banded[d, edge_at : edge_at + 1, :] = edges[d : d + 1]

    def send_banded(start, size):
        here = pl.multiple_of(lon * PART + start, 8)
        copies = [
            remote.start(banded.at[east(k), pl.ds(start, size)], returned.at[pl.ds(here, size)], east(k), lat)
            for k in FAR_FIRST
        ]
        returned[pl.ds(here, size), :] = banded[lon, pl.ds(start, size), :]
        return copies

    def send_beyond():
        here = pl.multiple_of(lon * 24, 8)
        copies = []
        for k in FAR_FIRST + [0]:
            for start, side, step in ((89, 0, 1), (72, 1, -1)):
                copies.append(
                    remote.start(
                        banded.at[east(k), pl.ds(start, 17)], beyond.at[side, pl.ds(here, 17)], east(k), north(step)
                    )
                )
        return copies

    for copy in sent_middle:
        copy.wait_recv()
    for pp in range(8):
        fill_circle(pp)
    for q in range(4):
        band_row(q, DRIFT + 4 * lon + q, 16 * q, 64 + q)
    arriving = send_banded(0, 68)
    for copy in sent_edge:
        copy.wait_recv()
    for pp in range(8, 12):
        fill_circle(pp)
    band_row(4, lon, 72, 88)
    band_row(5, lon + ROWS - DRIFT, 90, 89)
    arriving += send_beyond() + send_banded(72, 34)
    for copy in arriving:
        copy.wait_recv()

    def row_tile(t, place, beside):
        if t in (-1, 6):
            place = (16 if t > 0 else 0) if beside else place + (t < 0)
            return beyond[t // 6 if t > 0 else 0, pl.ds(place, 8, stride=24), :]
        if t in (0, 5):
            place = 88 + t // 5 if beside else 72 + 18 * (t // 5) + place
            return returned[pl.ds(place, 8, stride=PART), :]
        both = []
        for c in (2 * t - 2, 2 * t - 1):
            if beside:
                both.append(returned[c * PART + 64 : c * PART + 68, :])
            else:
                both.append(returned[pl.ds(c * PART + place, 4, stride=16), :])
        return jnp.concatenate(both, 0)

    for t in range(-1, 7):
        outside = {-1: top_ok, 6: bottom_ok}.get(t)
        beside = row_tile(t, 0, True)
        for level in range(4):
            tiles = [row_tile(t, 4 * level + b, False) for b in range(4)]
            tiles.append(pltpu.roll(beside, (120 - 16 * level) % 128, 1))
            for b, tile in enumerate(tiles):
                if outside is not None:
                    tile = jnp.where(outside, tile, 0.0)
                elif b < 4:
                    dep[level, 8 * t : 8 * t + 8, 128 * b : 128 * b + 128] = tile
                b_put(level, t, b, tile)
    for k in range(1, STEPS + 1):
        chebyshev(k - 1, None if k == 1 else k - 2, k)
    answer, worst = coefficients(gram(), STEPS, middle, half)
    combine(answer)
    flag[0, 0] = jnp.max(worst)
    for k in range(4):
        coupling[k : k + 1, :] = jnp.full((1, 128), vertical[k], F32)
    remote.drain()


def solve(source_field, helm_diag, vertical, band, offsets, shifts, classes, nlon, nlat):
    copies = 2 + 4 * (nlon - 1) + 8 + 2 * nlon + 15 + 7
    vmem = pl.BlockSpec(memory_space=pltpu.VMEM)
    smem = pl.BlockSpec(memory_space=pltpu.SMEM)
    far = pl.BlockSpec(memory_space=pltpu.HBM)
    field = jax.ShapeDtypeStruct(source_field.shape, F32)
    return pl.pallas_call(
        partial(solve_kernel, nlon, nlat),
        out_shape=(pltpu.VMEM(field.shape, F32), pltpu.VMEM(field.shape, F32), pltpu.SMEM((1, 1), F32), pltpu.VMEM((4, 128), F32)),
        in_specs=[far] * 7,
        out_specs=(vmem, vmem, smem, vmem),
        scratch_shapes=[
            pltpu.SMEM((4,), F32),
            pltpu.SMEM(band.shape, F32),
            pltpu.SMEM(offsets.shape, jnp.int32),
            pltpu.SMEM(shifts.shape, jnp.int32),
            pltpu.SMEM(classes.shape, jnp.int32),
            pltpu.VMEM((4, 4, ROWS, 128), F32),
            pltpu.VMEM((4, 4, 3 * DRIFT, 128), F32),
            pltpu.VMEM((4, 4, 3 * DRIFT, 128), F32),
            pltpu.VMEM((nlon - 1, 96, 128), F32),
            pltpu.VMEM((nlon, 96, 128), F32),
            pltpu.VMEM((24, 80, 128), F32),
            pltpu.VMEM((24, 48, 128), F32),
            pltpu.VMEM((nlon, PART, 128), F32),
            pltpu.VMEM((nlon * PART, 128), F32),
            pltpu.VMEM((2, nlon * 24, 128), F32),
            pltpu.VMEM((STEPS + 1, 6, TILES, XR, 128), F32),
            pltpu.VMEM((4, TILES, XR, 128), F32),
            pltpu.VMEM((1, 6, 2, 8, 128), F32),
            pltpu.VMEM((1, 2, 2, 8, 128), F32),
            pltpu.VMEM((128, 128), F32),
            pltpu.VMEM((16, 1, 128), F32),
            pltpu.VMEM((8, 1, 128), F32),
            pltpu.SemaphoreType.DMA((21,)),
            pltpu.SemaphoreType.DMA((copies,)),
            pltpu.SemaphoreType.DMA((copies,)),
        ],
        compiler_params=pltpu.CompilerParams(
            collective_id=0, has_side_effects=True, vmem_limit_bytes=62 * 1024 * 1024
        ),
        name="solve",
    )(vertical, band, offsets, shifts, classes, source_field, helm_diag)


def finish_kernel(departure, answer, departure_out, answer_out, sems):
    copies = [
        pltpu.make_async_copy(a.at[k], b.at[k], sems.at[n, k])
        for n, (a, b) in enumerate([(departure, departure_out), (answer, answer_out)])
        for k in range(4)
    ]
    for copy in copies:
        copy.start()
    for copy in copies:
        copy.wait()


def finish(departure, answer):
    anywhere = pl.BlockSpec(memory_space=pl.ANY)
    field = jax.ShapeDtypeStruct(departure.shape, F32)
    return pl.pallas_call(
        finish_kernel,
        out_shape=(field, field),
        in_specs=[anywhere] * 2,
        out_specs=(anywhere, anywhere),
        scratch_shapes=[pltpu.SemaphoreType.DMA((2, 4))],
        name="finish",
    )(departure, answer)


def iterate(departure, helm_diag, coupling):
    vertical = coupling[:, 0]

    def one(_, carry):
        answer, residual, direction, norm = carry
        applied = operate(direction, helm_diag, vertical)
        rate = norm / lax.psum(jnp.sum(direction * applied), ("lon", "lat"))
        answer = answer + rate * direction
        residual = residual - rate * applied
        follow = squares(residual)
        return answer, residual, residual + follow / norm * direction, follow

    start = (jnp.zeros_like(departure), departure, departure, squares(departure))
    answer, _, direction, norm = lax.fori_loop(0, ITERS - 1, one, start)
    applied = operate(direction, helm_diag, vertical)
    return answer + norm / lax.psum(jnp.sum(direction * applied), ("lon", "lat")) * direction


def body(source_field, helm_diag, vertical, cubic_band, lat_offset, zonal_shift, row_class):
    departure, quick, worst, coupling = solve(
        source_field, helm_diag, vertical, cubic_band.T, lat_offset, zonal_shift, row_class,
        lax.axis_size("lon"), lax.axis_size("lat"),
    )
    answer = lax.cond(
        worst[0, 0] < LIMIT, lambda *_: quick, iterate, departure, helm_diag, coupling
    )
    return finish(departure, answer)


def solution(mesh):
    return jax.shard_map(
        body,
        mesh=mesh,
        in_specs=(
            P(None, "lat", "lon"),
            P(None, "lat", "lon"),
            P(),
            P(),
            P("lat"),
            P("lat"),
            P("lat"),
        ),
        out_specs=(P(None, "lat", "lon"), P(None, "lat", "lon")),
        check_vma=False,
    )
```

```python
import itertools
from functools import partial

import jax
import jax.numpy as jnp
from jax import lax
from jax.experimental import pallas as pl
from jax.experimental.pallas import tpu as pltpu
from jax.sharding import PartitionSpec as P

DRIFT = 8
ITERS = 8


def with_halo(cells, sides, width, closed):
    for axis, dim in sides:
        count = lax.axis_size(axis)
        ends = count if closed else count - 1
        head = lax.slice_in_dim(cells, 0, width, axis=dim)
        tail = lax.slice_in_dim(cells, cells.shape[dim] - width, cells.shape[dim], axis=dim)
        cells = jnp.concatenate(
            [
                lax.ppermute(tail, axis, [(i, (i + 1) % count) for i in range(ends)]),
                cells,
                lax.ppermute(head, axis, [((i + 1) % count, i) for i in range(ends)]),
            ],
            axis=dim,
        )
    return cells


def local_terms(values, helm_diag, vertical, east_west, north_south):
    stacked = jnp.pad(values, ((1, 1), (0, 0), (0, 0)))
    up_down = stacked[2:] + stacked[:-2]
    coupling = vertical[:, None, None]
    return (
        (4.0 + 2.0 * coupling + helm_diag) * values - (east_west + north_south) - coupling * up_down
    )


def operate(values, helm_diag, vertical):
    zonal = with_halo(values, (("lon", 2),), 1, True)
    meridional = with_halo(values, (("lat", 1),), 1, False)
    east_west = zonal[:, :, 2:] + zonal[:, :, :-2]
    north_south = meridional[:, 2:, :] + meridional[:, :-2, :]
    return local_terms(values, helm_diag, vertical, east_west, north_south)


def squares(residual):
    return lax.psum(jnp.sum(residual * residual), ("lon", "lat"))


MESH = pl.DeviceIdType.MESH
F32 = jnp.float32
STEPS = 8
SIZES = {"zl": 2, "x": 4, "zh": 2, "y": 4, "c": 2}
PLANE, REST = ("x", "y"), ("zl", "zh", "c")
PART = 112
FAR_FIRST = [6, 2, 5, 7, 3, 1, 4]
LIMIT = 1.5e4
ROWS, COLS = 48, 512
XR, TOP, TILES = 80, 16, 5


def iota(shape, dim):
    return lax.broadcasted_iota(jnp.int32, shape, dim)


class Remote:
    def __init__(self, send_sems, recv_sems):
        self.send_sems, self.recv_sems, self.used, self.all = send_sems, recv_sems, 0, []

    def start(self, src, dst, lon, lat):
        copy = pltpu.make_async_remote_copy(
            src_ref=src,
            dst_ref=dst,
            send_sem=self.send_sems.at[self.used],
            recv_sem=self.recv_sems.at[self.used],
            device_id=(lon, lat),
            device_id_type=MESH,
        )
        self.used += 1
        copy.start()
        self.all.append(copy)
        return copy

    def settle(self, copies):
        for copy in copies:
            copy.wait_send()
            self.all = [other for other in self.all if other is not copy]

    def drain(self):
        for copy in self.all:
            copy.wait_send()


def coefficients(gram, steps, middle, half):
    def apply(vec):
        out = {}

        def add(i, x):
            out[i] = out[i] + x if i in out else x

        for i, x in vec.items():
            add(i, x * middle)
            if i == 0:
                add(1, x * half)
            else:
                add(i + 1, x * (0.5 * half))
                add(i - 1, x * (0.5 * half))
        return out

    def form(a, b):
        total = size = None
        for i, x in a.items():
            inner = bulk = None
            for j, y in b.items():
                term = gram(i, j) * y
                inner = term if inner is None else inner + term
                bulk = jnp.abs(term) if bulk is None else bulk + jnp.abs(term)
            total = x * inner if total is None else total + x * inner
            size = jnp.abs(x) * bulk if size is None else size + jnp.abs(x) * bulk
        return total, size / jnp.abs(total)

    def plus(a, scale, b):
        return {i: a[i] + scale * b[i] if i in a and i in b else (a[i] if i in a else scale * b[i]) for i in {**a, **b}}

    one = jnp.ones((8, 128), F32)
    direction, residual, answer = {0: one}, {0: one}, {}
    norm, worst = gram(0, 0), one
    for count in range(steps):
        applied = apply(direction)
        slope, size = form(direction, applied)
        worst = jnp.maximum(worst, size)
        rate = norm / slope
        answer = plus(answer, rate, direction)
        if count < steps - 1:
            residual = plus(residual, -rate, applied)
            follow, size = form(residual, residual)
            worst = jnp.maximum(worst, size)
            direction = plus(residual, follow / norm, direction)
            norm = follow
    return answer, worst


class Gram:
    def __init__(self, row, pairs):
        self.row, self.place, self.cache = row, {p: i for i, p in enumerate(pairs)}, {}

    def __call__(self, i, j):
        pair = (min(i, j), max(i, j))
        if pair not in self.cache:
            at = self.place[pair]
            self.cache[pair] = jnp.broadcast_to(self.row[:, at : at + 1], (8, 128))
        return self.cache[pair]


def solve_kernel(
    nlon, nlat, vertical_far, band_far, offsets_far, shifts_far, classes_far, source, helm, dep, out, flag, coupling,
    vertical, band, offsets, shifts, classes,
    inner, upper, lower, picked, gathered, circle, looped, banded, returned, beyond,
    vs, dd, lon_in, packs, stage, slot_plane, slot_rest, local_sems, send_sems, recv_sems,
):
    lon, lat = lax.axis_index("lon"), lax.axis_index("lat")

    def east(k):
        return lax.rem(lon + (k + nlon), nlon)

    def north(k):
        return lax.rem(lat + (k + nlat), nlat)

    small = [
        pltpu.make_async_copy(a, b, local_sems.at[16 + n])
        for n, (a, b) in enumerate(
            [
                (vertical_far, vertical), (band_far, band), (offsets_far, offsets),
                (shifts_far, shifts), (classes_far, classes),
            ]
        )
    ]
    for copy in small:
        copy.start()
    here = {"zl": lon // 4, "x": lax.rem(lon, 4), "zh": lat // 8, "y": lax.rem(lat // 2, 4), "c": lax.rem(lat, 2)}

    def place_of(moves):
        spot = {a: lax.rem(v + moves.get(a, 0), SIZES[a]) for a, v in here.items()}
        return spot["zl"] * 4 + spot["x"], spot["zh"] * 8 + spot["y"] * 2 + spot["c"]

    def partners(axes):
        moves = [dict(zip(axes, m)) for m in itertools.product(*[range(SIZES[a]) for a in axes]) if any(m)]
        far = {"c": 0, "zl": 1, "zh": 2}
        return sorted(moves, key=lambda m: -sum(far.get(a, 1) * min(v, SIZES[a] - v) for a, v in m.items()))

    barrier = pltpu.get_barrier_semaphore()
    greet = [(east(k), lat) for k in range(1, nlon)]
    greet += [(east(k), north(b)) for k in (-1, 0, 1) for b in (-1, 1)]
    greet += [place_of(m) for m in partners(PLANE) if m["y"]]
    greet += [place_of(m) for m in partners(REST) if m["zh"] or m["c"]]
    for peer in greet:
        pl.semaphore_signal(barrier, inc=1, device_id=peer, device_id_type=MESH)
    greeted = len(greet)
    own = [
        pltpu.make_async_copy(
            source.at[:, pl.ds(start, size), pl.ds(128 * b, 128)],
            into.at[:, b, pl.ds(at, size), :],
            local_sems.at[4 * n + b],
        )
        for n, (into, start, at, size) in enumerate(
            [(inner, 0, 0, ROWS), (upper, 0, DRIFT, 2 * DRIFT), (lower, ROWS - 2 * DRIFT, 0, 2 * DRIFT)]
        )
        for b in range(4)
    ]
    own_diag = [
        pltpu.make_async_copy(
            helm.at[:, :, pl.ds(128 * b, 128)], dd.at[:, b, pl.ds(TOP, ROWS), :], local_sems.at[12 + b]
        )
        for b in range(4)
    ]
    for copy in own + own_diag:
        copy.start()

    remote = Remote(send_sems, recv_sems)
    lane, sub = iota((8, 128), 1), iota((8, 128), 0)
    top_ok, bottom_ok = lat > 0, lat < nlat - 1

    def clear():
        zero = jnp.zeros((8, 128), F32)

        def one(j, carry):
            for b in range(TILES):
                for t in range(XR // 8):
                    vs[j, 0, b, 8 * t : 8 * t + 8, :] = zero
                    vs[j, 5, b, 8 * t : 8 * t + 8, :] = zero
                for level in range(1, 5):
                    vs[j, level, b, 0:8, :] = zero
                    vs[j, level, b, XR - 8 : XR, :] = zero
            return carry

        lax.fori_loop(0, STEPS + 1, one, 0)
        stage[...] = jnp.zeros_like(stage)

    for copy in small:
        copy.wait()
    mean = 0.25 * ((vertical[0] + vertical[1]) + (vertical[2] + vertical[3]))
    top = 0.9 * (9.0 + 4.0 * mean)
    middle, half = 0.54 * top, 0.46 * top
    double = jnp.full((8, 128), 2.0, F32) / jnp.broadcast_to(half, (8, 128))

    def start_exchange(tile, place, which):
        for h in range(2):
            right = left = jnp.zeros((8, 128), F32)
            for i in range(12):
                here = lane // 8 == i
                level = 2 * h + i // 6
                right = jnp.where(here, pltpu.roll(tile(level, i % 6, 3), (8 * i + 8) % 128, 1), right)
                left = jnp.where(here, pltpu.roll(tile(level, i % 6, 0), 8 * i, 1), left)
            packs[which, 0, h] = right
            packs[which, 1, h] = left
        return [
            remote.start(place(TOP + ROWS - 8), place(TOP - 8), lon, north(1)),
            remote.start(place(TOP), place(TOP + ROWS), lon, north(-1)),
            remote.start(packs.at[which, 0], lon_in.at[which, 0], east(1), lat),
            remote.start(packs.at[which, 0], lon_in.at[which, 1], east(1), north(1)),
            remote.start(packs.at[which, 0], lon_in.at[which, 2], east(1), north(-1)),
            remote.start(packs.at[which, 1], lon_in.at[which, 3], east(-1), lat),
            remote.start(packs.at[which, 1], lon_in.at[which, 4], east(-1), north(1)),
            remote.start(packs.at[which, 1], lon_in.at[which, 5], east(-1), north(-1)),
        ]

    def finish_exchange(copies, put, which):
        for copy in copies:
            copy.wait_recv()
        for level in range(4):
            packed = [lon_in[which, i, level // 2] for i in range(6)]
            for t in range(-1, 7):
                i = 6 * (level % 2) + (5 if t < 0 else t if t < 6 else 0)
                side = 1 if t < 0 else 0 if t < 6 else 2
                westward = pltpu.roll(packed[side], (120 - 8 * i) % 128, 1)
                eastward = pltpu.roll(packed[3 + side], (-8 * i) % 128, 1)
                put(level, t, 4, jnp.where(lane < 64, eastward, westward))
        for missing, t in ((lat == nlat - 1, 6), (lat == 0, -1)):

            @pl.when(missing)
            def _(t=t):
                for level in range(4):
                    for b in range(5):
                        put(level, t, b, jnp.zeros((8, 128), F32))

    def b_put(level, t, b, value):
        vs[0, level + 1, b, TOP + 8 * t : TOP + 8 * t + 8, :] = value

    def diag_tile(level, t, b):
        return dd[level, b, TOP + 8 * t : TOP + 8 * t + 8, :]

    def diag_put(level, t, b, value):
        dd[level, b, TOP + 8 * t : TOP + 8 * t + 8, :] = value

    def diag_rows(at):
        return dd.at[:, pl.ds(0, 4), pl.ds(at, 8), :]

    def shift_diag():
        def one(level, carry):
            add = 4.0 + 2.0 * vertical[level] - middle
            for b in range(TILES):
                for t in range(-1, 7):
                    value = double * (diag_tile(level, t, b) + add)
                    if t in (-1, 6):
                        value = jnp.where(top_ok if t < 0 else bottom_ok, value, 0.0)
                    diag_put(level, t, b, value)
            return carry

        lax.fori_loop(0, 4, one, 0)

    def chebyshev(src, before, dst):
        last = dst == STEPS

        def one(level, carry):
            results = []
            tiles = range(0, 6) if last else range(-1, 7)
            at = lambda j, l, t, b: vs[j, l, b, TOP + 8 * t : TOP + 8 * t + 8, :]
            for t in tiles:
                scale = double
                if t == -1:
                    scale = jnp.where(top_ok, double, 0.0)
                if t == 6:
                    scale = jnp.where(bottom_ok, double, 0.0)
                mids = [at(src, level + 1, t, b) for b in range(TILES)]
                for b in range(4 if last else TILES):
                    mid = mids[b]
                    sides = pltpu.roll(jnp.where(lane == 127, mids[b - 1], mid), 1, 1)
                    sides = sides + pltpu.roll(jnp.where(lane == 0, mids[(b + 1) % TILES], mid), 127, 1)
                    above, below = at(src, level + 1, t - 1, b), at(src, level + 1, t + 1, b)
                    sides = sides + pltpu.roll(jnp.where(sub == 7, above, mid), 1, 0)
                    sides = sides + pltpu.roll(jnp.where(sub == 0, below, mid), 7, 0)
                    stack = at(src, level, t, b) + at(src, level + 2, t, b)
                    value = dd[level, b, TOP + 8 * t : TOP + 8 * t + 8, :] * mid - scale * (sides + vertical[level] * stack)
                    if before is None:
                        value = 0.5 * value
                    else:
                        value = value - at(before, level + 1, t, b)
                    results.append((b, t, value))
                    if len(results) == 20:
                        for bb, tt, v in results:
                            vs[dst, level + 1, bb, TOP + 8 * tt : TOP + 8 * tt + 8, :] = v
                        results = []
            for bb, tt, v in results:
                vs[dst, level + 1, bb, TOP + 8 * tt : TOP + 8 * tt + 8, :] = v
            return carry

        for level in range(4):
            one(level, 0)

    def all_reduce(value):
        for axes, slot in ((PLANE, slot_plane), (REST, slot_rest)):
            mine = 0
            for axis in axes:
                mine = mine * SIZES[axis] + here[axis]
            slot[mine] = value[0:1]
            copies = [remote.start(slot.at[mine], slot.at[mine], *place_of(m)) for m in partners(axes)]
            for copy in copies:
                copy.wait_recv()
            value = slot[0]
            for i in range(1, slot.shape[0]):
                value = value + slot[i]
        return value

    def gram():
        count = STEPS + 1
        pairs = [(i, j) for i in range(count) for j in range(i, count) if i < STEPS]

        def one(t, sums):
            level, r = t // 6, (t % 6) * 8
            sums = list(sums)
            for b in range(4):
                tiles = [vs[i, level + 1, b, pl.ds(r + TOP, 8), :] for i in range(count)]
                for n, (i, j) in enumerate(pairs):
                    sums[n] = sums[n] + tiles[i] * tiles[j]
            return tuple(sums)

        sums = tuple(jnp.zeros((8, 128), F32) for _ in pairs)
        for t in range(24):
            sums = one(t, sums)
        for n, part in enumerate(sums):
            stage[n : n + 1, :] = jnp.sum(part, axis=0, keepdims=True)
        row = lax.dot_general(
            jnp.ones((8, 128), F32), stage[...], (((1,), (1,)), ((), ())),
            precision=lax.Precision.HIGHEST, preferred_element_type=F32,
        )
        return Gram(all_reduce(row), pairs)

    def combine(coef):
        def one(t, carry):
            level, r = t // 6, (t % 6) * 8
            for b in range(4):
                value = None
                for i, x in coef.items():
                    term = x * vs[i, level + 1, b, pl.ds(r + TOP, 8), :]
                    value = term if value is None else value + term
                out[level, pl.ds(r, 8), 128 * b : 128 * b + 128] = value
            return carry

        for t in range(24):
            one(t, 0)

    for copy in own[0:4]:
        copy.wait()

    def pick(j, part, write):
        from_, first, rows = [(inner, 0, ROWS), (upper, -DRIFT, 3 * DRIFT), (lower, ROWS - 2 * DRIFT, 3 * DRIFT)][part]
        row = jnp.clip(j + offsets[j] - first, 0, rows - 1)
        for level in range(4):
            for b in range(4):
                write(4 * level + b, from_[level, b, pl.ds(row, 1), :])

    def pick_rows(c, k, rows, at, parts):
        for n, (j, part) in enumerate(zip(rows, parts)):

            def write(place, value, n=n):
                if k == nlon:
                    gathered[c, at + 16 * n + place : at + 16 * n + place + 1, :] = value
                else:
                    picked[k - 1, at + 16 * n + place : at + 16 * n + place + 1, :] = value

            pick(j, part, write)

    def middle_rows(c):
        return [DRIFT + 4 * c + q for q in range(4)]

    def edge_rows(c):
        return [c, ROWS - DRIFT + c]

    for k in range(1, nlon + 1):
        pick_rows(east(k % nlon), k, middle_rows(east(k % nlon)), 0, (0, 0, 0, 0))
    pl.semaphore_wait(barrier, greeted)
    beside = [
        remote.start(inner.at[:, :, pl.ds(ROWS - DRIFT, DRIFT), :], upper.at[:, :, pl.ds(0, DRIFT), :], lon, north(1)),
        remote.start(inner.at[:, :, pl.ds(0, DRIFT), :], lower.at[:, :, pl.ds(2 * DRIFT, DRIFT), :], lon, north(-1)),
    ]

    def send_picked(start, size):
        return [
            remote.start(
                picked.at[k - 1, pl.ds(start, size)], gathered.at[lon, pl.ds(start, size)], east(k), lat
            )
            for k in range(1, nlon)
        ]

    sent_middle = send_picked(0, 64)
    for copy in own_diag:
        copy.wait()
    diag_waiting = start_exchange(diag_tile, diag_rows, 0)
    clear()
    for copy in own[4:]:
        copy.wait()
    for copy in beside:
        copy.wait_recv()
    for k in range(1, nlon + 1):
        pick_rows(east(k % nlon), k, edge_rows(east(k % nlon)), 64, (1, 2))
    sent_edge = send_picked(64, 32)

    finish_exchange(diag_waiting, diag_put, 0)
    remote.settle(diag_waiting)

    shift_diag()

    first_half = sub < 4
    lanes = iota((32, 128), 1)

    def fill_circle(pp):
        for m in range(4):
            a, b = gathered[2 * m, 8 * pp : 8 * pp + 8, :], gathered[2 * m + 1, 8 * pp : 8 * pp + 8, :]
            pair = (
                jnp.where(first_half, a, pltpu.roll(b, 4, 0)),
                jnp.where(first_half, pltpu.roll(a, 4, 0), b),
            )
            for n in range(2):
                circle[2 * pp + n, 8 + 8 * m : 16 + 8 * m, :] = pair[n]
                circle[2 * pp + n, 40 + 8 * m : 48 + 8 * m, :] = pair[n]
                if m == 3:
                    circle[2 * pp + n, 0:8, :] = pair[n]
                if m == 0:
                    circle[2 * pp + n, 72:80, :] = pair[n]

    def band_row(row, j, at, edge_at):
        start = 8 + lax.rem(64 - shifts[j], 32)
        weight = [band[t, classes[j]] for t in range(4)]
        outs = []
        for level in range(4):
            now = circle[4 * row + level, pl.ds(start, 32), :]
            before = circle[4 * row + level, pl.ds(start - 1, 32), :]
            after = circle[4 * row + level, pl.ds(start + 1, 32), :]
            total = weight[0] * pltpu.roll(jnp.where(lanes == 127, before, now), 1, 1)
            total = total + weight[1] * now
            total = total + weight[2] * pltpu.roll(jnp.where(lanes == 0, after, now), 127, 1)
            total = total + weight[3] * pltpu.roll(jnp.where(lanes < 2, after, now), 126, 1)
            outs.append(total)
        for half in range(2):
            for m in range(4):
                a, b = outs[2 * half][8 * m : 8 * m + 8], outs[2 * half + 1][8 * m : 8 * m + 8]
                here = slice(at + 8 * half, at + 8 * half + 8)
                banded[2 * m, here, :] = jnp.where(first_half, a, pltpu.roll(b, 4, 0))
                banded[2 * m + 1, here, :] = jnp.where(first_half, pltpu.roll(a, 4, 0), b)
        edges = jnp.zeros((8, 128), F32)
        for level in range(4):
            looped[4 * row + level, 0:8, :] = outs[level][24:32]
            looped[4 * row + level, 8:40, :] = outs[level]
            looped[4 * row + level, 40:48, :] = outs[level][0:8]
        for level in range(4):
            west = looped[4 * row + level, pl.ds(7, 8, stride=4), :]
            east_ = looped[4 * row + level, pl.ds(12, 8, stride=4), :]
            both = pltpu.roll(jnp.where(lane < 64, east_, west), 16 * level + 8, 1)
            edges = jnp.where(lane // 16 == level, both, edges)
        for d in range(nlon):
            banded[d, edge_at : edge_at + 1, :] = edges[d : d + 1]

    def send_banded(start, size):
        here = pl.multiple_of(lon * PART + start, 8)
        copies = [
            remote.start(banded.at[east(k), pl.ds(start, size)], returned.at[pl.ds(here, size)], east(k), lat)
            for k in FAR_FIRST
        ]
        returned[pl.ds(here, size), :] = banded[lon, pl.ds(start, size), :]
        return copies

    def send_beyond():
        here = pl.multiple_of(lon * 24, 8)
        copies = []
        for k in FAR_FIRST + [0]:
            for start, side, step in ((89, 0, 1), (72, 1, -1)):
                copies.append(
                    remote.start(
                        banded.at[east(k), pl.ds(start, 17)], beyond.at[side, pl.ds(here, 17)], east(k), north(step)
                    )
                )
        return copies

    for copy in sent_middle:
        copy.wait_recv()
    for pp in range(8):
        fill_circle(pp)
    for q in range(4):
        band_row(q, DRIFT + 4 * lon + q, 16 * q, 64 + q)
    arriving = send_banded(0, 68)
    for copy in sent_edge:
        copy.wait_recv()
    for pp in range(8, 12):
        fill_circle(pp)
    band_row(4, lon, 72, 88)
    band_row(5, lon + ROWS - DRIFT, 90, 89)
    arriving += send_beyond() + send_banded(72, 34)
    for copy in arriving:
        copy.wait_recv()

    def row_tile(t, place, beside):
        if t in (-1, 6):
            place = (16 if t > 0 else 0) if beside else place + (t < 0)
            return beyond[t // 6 if t > 0 else 0, pl.ds(place, 8, stride=24), :]
        if t in (0, 5):
            place = 88 + t // 5 if beside else 72 + 18 * (t // 5) + place
            return returned[pl.ds(place, 8, stride=PART), :]
        both = []
        for c in (2 * t - 2, 2 * t - 1):
            if beside:
                both.append(returned[c * PART + 64 : c * PART + 68, :])
            else:
                both.append(returned[pl.ds(c * PART + place, 4, stride=16), :])
        return jnp.concatenate(both, 0)

    for t in range(-1, 7):
        outside = {-1: top_ok, 6: bottom_ok}.get(t)
        beside = row_tile(t, 0, True)
        for level in range(4):
            tiles = [row_tile(t, 4 * level + b, False) for b in range(4)]
            tiles.append(pltpu.roll(beside, (120 - 16 * level) % 128, 1))
            for b, tile in enumerate(tiles):
                if outside is not None:
                    tile = jnp.where(outside, tile, 0.0)
                elif b < 4:
                    dep[level, 8 * t : 8 * t + 8, 128 * b : 128 * b + 128] = tile
                b_put(level, t, b, tile)
    for k in range(1, STEPS + 1):
        chebyshev(k - 1, None if k == 1 else k - 2, k)
    answer, worst = coefficients(gram(), STEPS, middle, half)
    combine(answer)
    flag[0, 0] = jnp.max(worst)
    for k in range(4):
        coupling[k : k + 1, :] = jnp.full((1, 128), vertical[k], F32)
    remote.drain()


def solve(source_field, helm_diag, vertical, band, offsets, shifts, classes, nlon, nlat):
    copies = 2 + 4 * (nlon - 1) + 8 + 2 * nlon + 15 + 7
    vmem = pl.BlockSpec(memory_space=pltpu.VMEM)
    smem = pl.BlockSpec(memory_space=pltpu.SMEM)
    far = pl.BlockSpec(memory_space=pltpu.HBM)
    field = jax.ShapeDtypeStruct(source_field.shape, F32)
    return pl.pallas_call(
        partial(solve_kernel, nlon, nlat),
        out_shape=(pltpu.VMEM(field.shape, F32), pltpu.VMEM(field.shape, F32), pltpu.SMEM((1, 1), F32), pltpu.VMEM((4, 128), F32)),
        in_specs=[far] * 7,
        out_specs=(vmem, vmem, smem, vmem),
        scratch_shapes=[
            pltpu.SMEM((4,), F32),
            pltpu.SMEM(band.shape, F32),
            pltpu.SMEM(offsets.shape, jnp.int32),
            pltpu.SMEM(shifts.shape, jnp.int32),
            pltpu.SMEM(classes.shape, jnp.int32),
            pltpu.VMEM((4, 4, ROWS, 128), F32),
            pltpu.VMEM((4, 4, 3 * DRIFT, 128), F32),
            pltpu.VMEM((4, 4, 3 * DRIFT, 128), F32),
            pltpu.VMEM((nlon - 1, 96, 128), F32),
            pltpu.VMEM((nlon, 96, 128), F32),
            pltpu.VMEM((24, 80, 128), F32),
            pltpu.VMEM((24, 48, 128), F32),
            pltpu.VMEM((nlon, PART, 128), F32),
            pltpu.VMEM((nlon * PART, 128), F32),
            pltpu.VMEM((2, nlon * 24, 128), F32),
            pltpu.VMEM((STEPS + 1, 6, TILES, XR, 128), F32),
            pltpu.VMEM((4, TILES, XR, 128), F32),
            pltpu.VMEM((1, 6, 2, 8, 128), F32),
            pltpu.VMEM((1, 2, 2, 8, 128), F32),
            pltpu.VMEM((128, 128), F32),
            pltpu.VMEM((16, 1, 128), F32),
            pltpu.VMEM((8, 1, 128), F32),
            pltpu.SemaphoreType.DMA((21,)),
            pltpu.SemaphoreType.DMA((copies,)),
            pltpu.SemaphoreType.DMA((copies,)),
        ],
        compiler_params=pltpu.CompilerParams(
            collective_id=0, has_side_effects=True, vmem_limit_bytes=62 * 1024 * 1024
        ),
        name="solve",
    )(vertical, band, offsets, shifts, classes, source_field, helm_diag)


def finish_kernel(departure, answer, departure_out, answer_out, sems):
    copies = [
        pltpu.make_async_copy(a.at[k], b.at[k], sems.at[n, k])
        for n, (a, b) in enumerate([(departure, departure_out), (answer, answer_out)])
        for k in range(4)
    ]
    for copy in copies:
        copy.start()
    for copy in copies:
        copy.wait()


def finish(departure, answer):
    anywhere = pl.BlockSpec(memory_space=pl.ANY)
    field = jax.ShapeDtypeStruct(departure.shape, F32)
    return pl.pallas_call(
        finish_kernel,
        out_shape=(field, field),
        in_specs=[anywhere] * 2,
        out_specs=(anywhere, anywhere),
        scratch_shapes=[pltpu.SemaphoreType.DMA((2, 4))],
        name="finish",
    )(departure, answer)


def iterate(departure, helm_diag, coupling):
    vertical = coupling[:, 0]

    def one(_, carry):
        answer, residual, direction, norm = carry
        applied = operate(direction, helm_diag, vertical)
        rate = norm / lax.psum(jnp.sum(direction * applied), ("lon", "lat"))
        answer = answer + rate * direction
        residual = residual - rate * applied
        follow = squares(residual)
        return answer, residual, residual + follow / norm * direction, follow

    start = (jnp.zeros_like(departure), departure, departure, squares(departure))
    answer, _, direction, norm = lax.fori_loop(0, ITERS - 1, one, start)
    applied = operate(direction, helm_diag, vertical)
    return answer + norm / lax.psum(jnp.sum(direction * applied), ("lon", "lat")) * direction


def body(source_field, helm_diag, vertical, cubic_band, lat_offset, zonal_shift, row_class):
    departure, quick, worst, coupling = solve(
        source_field, helm_diag, vertical, cubic_band.T, lat_offset, zonal_shift, row_class,
        lax.axis_size("lon"), lax.axis_size("lat"),
    )
    answer = lax.cond(
        worst[0, 0] < LIMIT, lambda *_: quick, iterate, departure, helm_diag, coupling
    )
    return finish(departure, answer)


def solution(mesh):
    return jax.shard_map(
        body,
        mesh=mesh,
        in_specs=(
            P(None, "lat", "lon"),
            P(None, "lat", "lon"),
            P(),
            P(),
            P("lat"),
            P("lat"),
            P("lat"),
        ),
        out_specs=(P(None, "lat", "lon"), P(None, "lat", "lon")),
        check_vma=False,
    )
```
